256 devices in a mesh: band: 8 (over x, y_lo), fft: 32 (over z, y_hi, core).
Axes of the slice: x: 4, y: 4 (y_hi: 2, y_lo: 2; y = y_hi * 2 + y_lo), z: 8, core: 2. Of those that a mesh axis runs over, the one named last changes fastest.
Arguments:
- orbitals: float32 [32, 5184, 216], P('band', 'fft'), may hold values from -6 to 6
- picked: int32 [8], P('band'), may hold values from 0 to 3, as said below
- shells: int32 [64], replicated, may hold values 0 or 1
Outputs:
- potentials: float32 [8, 5184, 216], P('band', 'fft')
- intersection: float32 [32, 1], P('band')
The draws below stay inside these ranges and needn't reach their ends.
Inputs may be any that keep to these rules, and one draw needn't show every extreme that they name: `picked`: within each group's 1 entries the bands named are distinct; every value from 0 to 3 is named by some group.
All inputs are finite; a program needn't handle non-finite values.
Results may differ from the reference program's by a relative error of at most 0.0003.
Values sent between devices are 32-bit elements; how exact they have to be, the bound alone decides.
A program may use at most 128 MiB of HBM per device.

```python
import math
import jax
import jax.numpy as jnp
from jax import lax

NX = 72
NY = 72
NZ = 216
BLK = 4
SEL = 1
NSHELL = 64
NBANDS = 32
NSEL = 8
N_BAND = 8


def draw_picked(key, part):
    key = jax.random.fold_in(key, 7)
    group_total = NSEL // SEL
    order = jax.random.permutation(key, group_total)
    chosen_rows = (order % BLK)[:, None] + jnp.zeros((1, SEL), jnp.int32)
    return chosen_rows.reshape(NSEL).astype(jnp.int32)


def touch_ends(result, key, low, high):
    longest = result.shape.index(max(result.shape))
    spots = []
    for shift in (0, 1):
        where = [jax.random.randint(jax.random.fold_in(key, axis), (), 0, length) for axis, length in enumerate(result.shape)]
        where[longest] = (where[longest] + shift) % result.shape[longest]
        spots.append(tuple(where))
    return result.at[spots[0]].set(low).at[spots[1]].set(high)


def block_levels(key, dims, shards, smallest, top_value):
    loudness, own = 1.0, jax.random.fold_in(key, 6)
    for dim, shards_of in shards:
        draws = jnp.exp(jax.random.uniform(jax.random.fold_in(own, dim), (shards_of,), jnp.float32, smallest / len(shards), top_value / len(shards)))
        loudness = loudness * jnp.repeat(draws, dims[dim] // shards_of).reshape([-1 if axis == dim else 1 for axis in range(len(dims))])
    return loudness


def bell_draw(own_key, extent, deviation, bound, shards=(), held_as=jnp.bfloat16):
    gain = block_levels(own_key, extent, shards, -0.22, 0.18) if shards else 1.0
    result = jax.random.normal(own_key, extent, jnp.float32) * deviation * gain
    return jnp.minimum(jnp.maximum(result, -bound), bound).astype(held_as)


def setup_inputs(seed: int = 0) -> dict:
    key_list = jax.random.split(jax.random.key(seed), 4)
    return {
        "orbitals": bell_draw(key_list[0], (NBANDS, NX * NY, NZ), 1.0, 6.0, ((0, 8), (1, 32)), jnp.float32),
        "picked": draw_picked(jax.random.fold_in(key_list[3], 71), 0),
        "shells": touch_ends((jax.random.randint(key_list[2], (NSHELL,), 0, 4) < 3).astype(jnp.int32), jax.random.fold_in(key_list[2], 1), 0, 1),
    }


SPACING = 0.2
SCREENING = 0.106
FRACTION = 0.25


def signed(index, length):
    return jnp.where(index > length // 2, index - length, index)


def kernel_grid(shells):
    span_cells = math.lcm(NX, NY, NZ)
    shell_top = (span_cells // NX) ** 2 * (NX // 2) ** 2 + (span_cells // NY) ** 2 * (NY // 2) ** 2 + (span_cells // NZ) ** 2 * (NZ // 2) ** 2
    signed_x = signed(jnp.arange(NX, dtype=jnp.int32), NX)
    signed_y = signed(jnp.arange(NY, dtype=jnp.int32), NY)
    signed_z = signed(jnp.arange(NZ, dtype=jnp.int32), NZ)
    squared = ((span_cells // NX) ** 2 * signed_x * signed_x)[:, None, None]
    squared = squared + ((span_cells // NY) ** 2 * signed_y * signed_y)[None, :, None]
    squared = squared + ((span_cells // NZ) ** 2 * signed_z * signed_z)[None, None, :]
    shell_index = jnp.minimum(squared * NSHELL // (shell_top + 1), NSHELL - 1)
    shell_gain = shells[shell_index].astype(jnp.float32)
    g_squared = (2.0 * math.pi / (SPACING * span_cells)) ** 2 * squared.astype(jnp.float32)
    safe = jnp.where(squared == 0, 1.0, g_squared)
    kernel_value = jnp.where(squared == 0, math.pi / SCREENING ** 2, 4.0 * math.pi / safe * (-jnp.expm1(-safe / (4.0 * SCREENING ** 2))))
    return kernel_value * shell_gain


def reference(orbitals, picked, shells):
    kernel = kernel_grid(shells)
    grid_cells = orbitals.reshape(NBANDS, NX, NY, NZ)
    potential_list = []
    intersection_list = []
    for group in range(N_BAND):
        lower = (group - 1) % N_BAND
        upper = (group + 1) % N_BAND
        own_block = grid_cells[group * BLK:(group + 1) * BLK]
        previous = grid_cells[lower * BLK:(lower + 1) * BLK]
        following = grid_cells[upper * BLK:(upper + 1) * BLK]
        visitors = jnp.concatenate([previous, following], axis=0)
        chosen = own_block[picked[group * SEL:(group + 1) * SEL]]

        def one_band(orbital):
            def one_pair(visitor):
                spectrum = jnp.fft.fftn(orbital * visitor)
                field_values = jnp.fft.ifftn(kernel * spectrum).real
                return visitor * field_values
            return -FRACTION * jnp.sum(lax.map(one_pair, visitors), axis=0)

        built_terms = lax.map(one_band, chosen)
        flat_terms = built_terms.reshape(SEL, NX * NY * NZ)
        intersection_list.append(SPACING ** 3 * jnp.dot(own_block.reshape(BLK, NX * NY * NZ), flat_terms.T, precision=lax.Precision.HIGHEST))
        potential_list.append(built_terms.reshape(SEL, NX * NY, NZ))
    return jnp.concatenate(potential_list, axis=0), jnp.concatenate(intersection_list, axis=0)
```

```python
import math

import jax
import jax.numpy as jnp
import numpy as np
from jax import lax
from jax.experimental import pallas as pl
from jax.experimental.pallas import tpu as pltpu
from jax.sharding import PartitionSpec as P

NX = 72
NY = 72
NZ = 216
BLK = 4
NSHELL = 64
FIELDS = 7
FFT = 32
ROWS = 162
MAIN = 128
TAIL = ROWS - MAIN
SLABS = 9
PLANES = 13

SPACING = 0.2
SCREENING = 0.106
FRACTION = 0.25
SPAN = math.lcm(NX, NY, NZ)
QTOP = (SPAN // NX) ** 2 * (NX // 2) ** 2 + (SPAN // NY) ** 2 * (NY // 2) ** 2 + (SPAN // NZ) ** 2 * (NZ // 2) ** 2
MESH = pl.DeviceIdType.MESH
F32 = jnp.float32
BF16 = jnp.bfloat16
VMEM_LIMIT = 60 * 1024 * 1024


def halves(table):
    table = np.asarray(table, np.float32)
    high = table.astype(jnp.bfloat16)
    low = (table - high.astype(np.float32)).astype(jnp.bfloat16)
    return high, low


def z_tables():
    freq, is_sin = np.zeros(NZ, np.int64), np.zeros(NZ, bool)
    for t in range(NZ // 8):
        for i in range(4):
            freq[8 * t + i] = 4 * t + i
            freq[8 * t + 4 + i] = 4 * t + i
            is_sin[8 * t + 4 + i] = True
    freq[4], is_sin[4] = NZ // 2, False
    angle = 2 * np.pi * (freq[:, None] * np.arange(NZ)[None, :] % NZ) / NZ
    forward = np.where(is_sin[:, None], -np.sin(angle), np.cos(angle))
    weight = np.where((freq == 0) | (freq == NZ // 2), 1.0, 2.0) / (NX * NY * NZ)
    inverse = (-FRACTION * weight[:, None] * forward).T
    return forward, inverse


def z_stacks():
    forward, inverse = z_tables()
    pad = np.zeros((8, NZ), jnp.bfloat16)

    def stack(table):
        high, low = halves(table)
        return np.concatenate([high, pad, low, pad], axis=0)

    return stack(forward), stack(inverse)


def xy_angle():
    index = np.arange(NX)
    return 2 * np.pi * (index[:, None] * index[None, :] % NX) / NX


def x_table():
    table = np.concatenate([np.cos(xy_angle()), np.sin(xy_angle())], axis=0)
    high, low = halves(table)
    pad = np.zeros((2 * NX, 8), high.dtype)
    return np.concatenate([high, pad, low, pad, high, pad], axis=1)


def y_tables():
    cosine, sine = np.cos(xy_angle()), np.sin(xy_angle())
    forward = np.zeros((256, 256))
    forward[:NY, :NY] = cosine
    forward[128:128 + NY, 128:128 + NY] = cosine
    forward[:NY, 128:128 + NY] = -sine
    forward[128:128 + NY, :NY] = sine
    fh, fl = halves(forward)
    return np.stack([fh, fl, fh.T, fl.T])


def xy_square():
    index = np.arange(NX)
    signed = np.where(index > NX // 2, index - NX, index)
    square = np.zeros((NX, 128), np.float32)
    square[:, :NY] = 9 * (signed[:, None] ** 2 + signed[None, :] ** 2)
    return square


def split(value):
    high = value.astype(BF16)
    return high, (value - high.astype(F32)).astype(BF16)


def mm(left, right):
    return lax.dot_general(left, right, (((1,), (0,)), ((), ())), preferred_element_type=F32)


def lanes(shape):
    return lax.broadcasted_iota(jnp.int32, shape, len(shape) - 1)


def turn(value, shift):
    shift = shift % 128
    return value if shift == 0 else pltpu.roll(value, shift, 1)


def pack_tail(parts):
    lane = lanes(parts[0].shape)
    upper = jnp.where(lane < 2 * TAIL, turn(parts[1], TAIL), turn(parts[2], 2 * TAIL))
    return jnp.where(lane < TAIL, parts[0], upper)


def pack_thirds(tail):
    third = NZ // 3
    return pack_tail([tail[third * g:third * (g + 1)] for g in range(3)])


def pack_field(wide):
    return jnp.concatenate([wide[:, :MAIN], pack_thirds(wide[:, MAIN:])], axis=0)


def unpack_field(packed):
    tail = packed[NZ:]
    tails = jnp.concatenate([turn(tail, -TAIL * g) for g in range(3)], axis=0)
    return jnp.concatenate([packed[:NZ], tails], axis=1)


def z_transform(table_ref, wide):
    high, low = split(wide)
    both = mm(table_ref[...], high)
    return both[:NZ] + both[NZ + 8:2 * NZ + 8] + mm(table_ref[:NZ + 8], low)[:NZ]


def order_bands(picked, orbitals_ref, own_ref, order_ref, pad_ref):
    pad_ref[...] = jnp.zeros_like(pad_ref)
    for b in range(BLK):
        pad_ref[:ROWS, :NZ] = orbitals_ref[:, b, :]
        own_ref[b] = pack_field(jnp.transpose(pad_ref[...])[:NZ])
    chosen = own_ref[0]
    for b in range(1, BLK):
        chosen = jnp.where(picked == b, own_ref[b], chosen)
    order_ref[0] = chosen


def order_others(picked, own_ref, order_ref):
    for j in range(1, BLK):
        order_ref[j] = jnp.where(picked >= j, own_ref[j - 1], own_ref[j])


def visitor_of(f):
    return (True, f + 1) if f < 3 else (False, f - 3)


def cuts_of(f):
    result = []
    for chunk in range(2):
        low, high = max(NZ * f, 768 * chunk), min(NZ * (f + 1), 768 * (chunk + 1))
        if low < high:
            result.append((low, high - low, low + 256 * chunk))
    return result


def runs(row, rows):
    tile, count = row // 8, rows // 8
    done = 0
    while done < count:
        place, peer = divmod(tile + done, FFT)
        take = min(count - done, FFT - peer)
        yield place // 4, place % 4, peer, take, done
        done += take


def put_rows(buffer, row, value):
    tiles = value.reshape(value.shape[0] // 8, 8, 128)
    for chunk, part, peer, take, done in runs(row, value.shape[0]):
        buffer[chunk, peer:peer + take, part] = tiles[done:done + take]


def get_rows(buffer, row, rows):
    parts = [buffer[chunk, peer:peer + take, part].reshape(8 * take, 128) for chunk, part, peer, take, _ in runs(row, rows)]
    return parts[0] if len(parts) == 1 else jnp.concatenate(parts, axis=0)


def spectrum_of(f, order_ref, upper_ref, lower_ref, table_ref, buffer, tail_ref):
    low_side, j = visitor_of(f)
    density = (lower_ref if low_side else upper_ref)[...] * order_ref[j]
    spectrum = z_transform(table_ref, unpack_field(density))
    for low, count, place in cuts_of(f):
        first = low - NZ * f
        put_rows(buffer, place, spectrum[first:first + count, :MAIN])
        tail_ref[pl.ds(low, count), :] = spectrum[first:first + count, MAIN:]


def close_tails(chunk, buffer, tail_ref):
    parts = [tail_ref[pl.ds(768 * chunk + 256 * p, 256), :] for p in range(3)]
    put_rows(buffer, 1024 * chunk + 768, pack_tail(parts))


def open_tails(chunk, buffer, tail_ref):
    tails = get_rows(buffer, 1024 * chunk + 768, 256)
    for p in range(3):
        tail_ref[pl.ds(768 * chunk + 256 * p, 256), :] = turn(tails, -TAIL * p)


def main_of(f, buffer):
    mains = [get_rows(buffer, place, count) for _, count, place in cuts_of(f)]
    return mains[0] if len(mains) == 1 else jnp.concatenate(mains, axis=0)


def tail_of(f, tail_ref):
    return tail_ref[pl.ds(NZ * f, NZ), :]


def pieces():
    result = []
    row = 0
    while row < 4 * ROWS:
        source, j = divmod(row, ROWS)
        slab, y = divmod(row, NY)
        stop = min((source + 1) * ROWS, (slab + 1) * NY)
        if j < MAIN:
            stop = min(stop, source * ROWS + MAIN)
        result.append((source, j >= MAIN, j if j < MAIN else j - MAIN, slab, y, stop - row))
        row = stop
    return result


def tile_of(owner, chunk, p):
    return lax.rem(96 * chunk + 32 * p + owner, NZ // 8)


def gain_of(owner, plane, shells_ref, xy_ref, gain):
    chunk, place = plane // PLANES, lax.rem(plane, PLANES)
    depth = jnp.where(place == PLANES - 1, NZ // 2, 4 * tile_of(owner, chunk, place // 4) + lax.rem(place, 4))
    square = xy_ref[...] + (depth * depth).astype(F32)
    total = jnp.full(square.shape, shells_ref[0].astype(F32), F32)
    for s in range(1, NSHELL):
        step = (shells_ref[s] - shells_ref[s - 1]).astype(F32)
        total = total + jnp.where(square >= float(-(-s * (QTOP + 1) // NSHELL)), step, 0.0)
    g_squared = (2.0 * math.pi / (SPACING * SPAN)) ** 2 * square
    safe = jnp.where(square == 0, 1.0, g_squared)
    value = 4.0 * math.pi / safe * (1.0 - jnp.exp(-safe / (4.0 * SCREENING**2)))
    gain[pl.ds(pl.multiple_of(plane * NX, 8), NX), :] = total * jnp.where(square == 0, math.pi / SCREENING**2, value)


def open_rows(got_ref, chunk, box):
    cuts = pieces()
    lane = lanes((8, 128))

    def one(chip, carry):
        for slab in range(SLABS):
            mine = [c for c in cuts if c[3] == slab]
            for p in range(3):
                value = None
                for source, tail, first, _, y, _ in mine:
                    part = got_ref[chunk, 4 * chip + source, 3 if tail else p]
                    part = turn(part, y - first - (TAIL * p if tail else 0))
                    value = part if value is None else jnp.where(lane >= y, part, value)
                box[pl.ds(8 * p * NX + SLABS * chip + slab, 8, stride=NX), :] = value
        return carry

    lax.fori_loop(0, 8, one, 0)


def close_rows(box, chunk, send_ref):
    cuts = pieces()
    lane = lanes((8, 128))

    def one(chip, carry):
        fields = [[box[pl.ds(8 * p * NX + SLABS * chip + slab, 8, stride=NX), :] for slab in range(SLABS)] for p in range(3)]
        for source in range(4):
            tail_value = None
            for p in range(3):
                value = None
                for s, tail, first, slab, y, _ in cuts:
                    if s != source:
                        continue
                    if tail:
                        place = first + TAIL * p
                        part = turn(fields[p][slab], place - y)
                        tail_value = part if tail_value is None else jnp.where(lane >= place, part, tail_value)
                    else:
                        part = turn(fields[p][slab], first - y)
                        value = part if value is None else jnp.where(lane >= first, part, value)
                send_ref[chunk, 4 * chip + source, p] = value
            send_ref[chunk, 4 * chip + source, 3] = tail_value
        return carry

    lax.fori_loop(0, 8, one, 0)


def screen_planes(owner, chunk, x_ref, y_ref, box, work, gain):
    flags = [jnp.where(tile_of(owner, chunk, p) == 0, 1.0, 0.0).astype(F32) for p in range(3)]

    def along_x(real, imag):
        wide = jnp.concatenate([real, imag], axis=1)
        wide = jnp.concatenate([wide, jnp.zeros((8, 256), F32)], axis=0)
        high, low = split(wide)
        both = mm(x_ref[...], jnp.concatenate([high, high, low], axis=0))
        return both[:NX, :128], both[:NX, 128:], both[NX:, :128], both[NX:, 128:]

    def along_y(value, k):
        high, low = split(value)
        return mm(high, y_ref[k]) + mm(low, y_ref[k]) + mm(high, y_ref[k + 1])

    for plane in range(PLANES):
        if plane == 12:
            real = sum(flags[p] * box[pl.ds((8 * p + 4) * NX, NX), :] for p in range(3))
            imag = jnp.zeros_like(real)
        else:
            p, i = divmod(plane, 4)
            real = box[pl.ds((8 * p + i) * NX, NX), :]
            imag = box[pl.ds((8 * p + 4 + i) * NX, NX), :]
            if i == 0:
                imag = imag * (1.0 - flags[p])
        cr, ci, sr, si = along_x(real, imag)
        work[pl.ds(plane * NX, NX), :] = jnp.concatenate([cr + si, ci - sr], axis=1)
    weight = gain[pl.ds(chunk * PLANES * NX, PLANES * NX), :]
    value = along_y(work[...], 0) * jnp.concatenate([weight, weight], axis=1)
    work[...] = along_y(value, 2)
    extra = None
    for plane in reversed(range(PLANES)):
        rows = work[pl.ds(plane * NX, NX), :]
        cr, ci, sr, si = along_x(rows[:, :128], rows[:, 128:])
        real, imag = cr - si, ci + sr
        if plane == 12:
            extra = real
        else:
            p, i = divmod(plane, 4)
            if i == 0:
                imag = imag * (1.0 - flags[p]) + extra * flags[p]
            box[pl.ds((8 * p + i) * NX, NX), :] = real
            box[pl.ds((8 * p + 4 + i) * NX, NX), :] = imag


def intersect(total, bands_ref, partial_ref):
    lines = []
    for b in range(BLK):
        product = (bands_ref[b] * total).reshape(36, 8, 128)
        line = jnp.sum(jnp.sum(product, axis=0), axis=0, keepdims=True)
        line = line + turn(line, 64)
        lines.append(line + turn(line, 32))
    quarter = lanes((1, 128)) // 32
    row = lines[0]
    for b in range(1, BLK):
        row = jnp.where(quarter == b, lines[b], row)
    partial_ref[...] = row * SPACING**3


STEPS = [(far, turned) for turned in range(4) for far in (4, 1, -1, 2, -2, 3, -3)] + [(0, turned) for turned in range(1, 4)]


class Ring:
    def __init__(self, me, source, target, send_sem, recv_sem):
        self.source, self.target = source, target
        self.send_sem, self.recv_sem = send_sem, recv_sem
        self.me = me
        self.places = [lax.rem(me // 4 + k, 8) for k in range(8)]
        self.parts = [lax.rem(lax.rem(me, 4) + k, 4) for k in range(4)]

    def device(self, far, turned):
        return 4 * self.places[far % 8] + self.parts[turned % 4]

    def copy(self, source, target, peer, k):
        return pltpu.make_async_remote_copy(
            src_ref=source, dst_ref=target, send_sem=self.send_sem.at[k], recv_sem=self.recv_sem.at[k],
            device_id={"fft": peer}, device_id_type=MESH,
        )

    def start(self, chunk, first, count, k):
        rows = pl.ds(first, count)
        for far, turned in STEPS:
            peer = self.device(far, turned)
            self.copy(self.source.at[chunk, peer, rows], self.target.at[chunk, self.me, rows], peer, k).start()
        self.target[chunk, self.me, first:first + count] = self.source[chunk, self.me, first:first + count]

    def wait_recv(self, chunk, first, count, k):
        whole = self.target.at[chunk, pl.ds(0, FFT - 1), pl.ds(first, count)]
        self.copy(whole, whole, self.device(1, 0), k).wait_recv()

    def wait_send(self, chunk, first, count, k):
        whole = self.source.at[chunk, pl.ds(0, FFT - 1), pl.ds(first, count)]
        self.copy(whole, whole, self.device(1, 0), k).wait_send()


def whole_kernel(
    picked_ref, shells_ref, orbitals_far, forward_far, inverse_far, xy_far, x_far, y_far,
    total_ref, result_ref,
    orbitals_ref, forward_ref, inverse_ref, xy_ref, x_ref, y_ref, fetch_sem,
    own, order, upper, lower, up, down, above, below, mine, sent, got, back, returned, tails, box, work, gain, pad,
    partial, ring_slots, near, near_slots,
    there_send, there_recv, home_send, home_recv, band_send, band_recv, ring_send, ring_recv, near_send, near_recv,
):
    me = lax.axis_index("fft")
    group = lax.axis_index("band")
    count = lax.axis_size("band")
    above_me, below_me = lax.rem(group + 1, count), lax.rem(group + count - 1, count)

    barrier = pltpu.get_barrier_semaphore()
    for peer in (above_me, below_me):
        pl.semaphore_signal(barrier, inc=1, device_id={"band": peer}, device_id_type=MESH)
    there = Ring(me, sent, got, there_send, there_recv)
    home = Ring(me, back, returned, home_send, home_recv)
    for far, turned in STEPS:
        peer = there.device(far, turned)
        pl.semaphore_signal(barrier, inc=1, device_id={"fft": peer}, device_id_type=MESH)

    def to_band(source, target, peer, k):
        return pltpu.make_async_remote_copy(
            src_ref=source, dst_ref=target, send_sem=band_send.at[k], recv_sem=band_recv.at[k],
            device_id={"band": peer}, device_id_type=MESH,
        )

    chosen_up = to_band(order.at[0], lower, above_me, 0)
    chosen_down = to_band(order.at[0], upper, below_me, 1)
    sum_down = to_band(down, above, below_me, 2)
    main, tail = pl.ds(0, NZ), pl.ds(NZ, NZ // 3)
    sum_up_main = to_band(up.at[main], below.at[main], above_me, 3)
    sum_up_tail = to_band(up.at[tail], below.at[tail], above_me, 4)

    fetches = [
        pltpu.make_async_copy(far, ref, fetch_sem.at[k])
        for k, (far, ref) in enumerate(
            [
                (orbitals_far, orbitals_ref), (xy_far, xy_ref), (forward_far, forward_ref),
                (x_far, x_ref), (y_far, y_ref), (inverse_far, inverse_ref),
            ]
        )
    ]
    for one in fetches:
        one.start()
    picked = picked_ref[0]
    fetches[0].wait()
    order_bands(picked, orbitals_ref, own, order, pad)
    pl.semaphore_wait(barrier, FFT + 1)
    chosen_up.start()
    order_others(picked, own, order)

    def gain_step(plane, carry):
        gain_of(me, plane, shells_ref, xy_ref, gain)
        return carry

    for one in fetches[1:]:
        one.wait()
    lax.fori_loop(0, 6, gain_step, 0)
    chosen_down.start()
    lax.fori_loop(6, 10, gain_step, 0)
    tails[pl.ds(NZ * FIELDS, 24), :] = jnp.zeros((24, 128), F32)
    put_rows(sent, NZ * FIELDS + 256, jnp.zeros((24, 128), F32))

    chosen_up.wait_recv()
    for f in range(3):
        spectrum_of(f, order, upper, lower, forward_ref, sent, tails)
    there.start(0, 0, 2, 0)
    chosen_down.wait_recv()
    spectrum_of(3, order, upper, lower, forward_ref, sent, tails)
    close_tails(0, sent, tails)
    there.start(0, 2, 2, 0)
    for f in range(4, FIELDS):
        spectrum_of(f, order, upper, lower, forward_ref, sent, tails)
    close_tails(1, sent, tails)
    there.start(1, 0, 4, 1)
    lax.fori_loop(10, 2 * PLANES, gain_step, 0)

    for chunk in range(2):
        there.wait_recv(chunk, 0, 4, chunk)
        open_rows(got, chunk, box)
        screen_planes(me, chunk, x_ref, y_ref, box, work, gain)
        close_rows(box, chunk, back)
        if chunk == 0:
            home.start(0, 0, 4, 0)
        else:
            home.start(1, 0, 3, 1)
            home.start(1, 3, 1, 2)

    home.wait_recv(0, 0, 4, 0)
    open_tails(0, returned, tails)
    total = None
    for f in range(3):
        field = pack_field(z_transform(inverse_ref, jnp.concatenate([main_of(f, returned), tail_of(f, tails)], axis=1)))
        term = field * order[visitor_of(f)[1]]
        total = term if total is None else total + term
    down[...] = total
    sum_down.start()

    def up_part(rows, fields):
        total = None
        for f, field in fields:
            if f == 3:
                mine[rows, :] = field * upper[rows, :]
            term = field * order[visitor_of(f)[1], rows, :]
            total = term if total is None else total + term
        up[rows, :] = total

    home.wait_recv(1, 0, 3, 1)
    up_part(main, [(f, z_transform(inverse_ref, main_of(f, returned))) for f in range(3, FIELDS)])
    sum_up_main.start()
    home.wait_recv(1, 3, 1, 2)
    open_tails(1, returned, tails)
    up_part(tail, [(f, pack_thirds(z_transform(inverse_ref, tail_of(f, tails)))) for f in range(3, FIELDS)])
    sum_up_tail.start()
    sum_down.wait_recv()
    mine[...] += above[...]
    sum_up_main.wait_recv()
    sum_up_tail.wait_recv()
    total = mine[...] + below[...]
    total_ref[...] = total
    intersect(total, own, partial)

    place, part = me // 4, lax.rem(me, 4)

    def row_to(source, target, peer, send_sem, recv_sem):
        return pltpu.make_async_remote_copy(
            src_ref=source, dst_ref=target, send_sem=send_sem, recv_sem=recv_sem,
            device_id={"fft": peer}, device_id_type=MESH,
        )

    ring = [
        row_to(partial, ring_slots.at[k], 4 * lax.rem(place + k, 8) + part, ring_send.at[k], ring_recv.at[k])
        for k in range(1, 8)
    ]
    for one in ring:
        one.start()
    row = partial[...]
    for k, one in enumerate(ring):
        one.wait()
        row = row + ring_slots[k + 1]
    near[...] = row
    beside = [
        row_to(near, near_slots.at[k], 4 * place + lax.rem(part + k, 4), near_send.at[k], near_recv.at[k])
        for k in range(1, 4)
    ]
    for one in beside:
        one.start()
    for k, one in enumerate(beside):
        one.wait()
        row = row + near_slots[k + 1]
    result_ref[...] = row

    there.wait_send(0, 0, 4, 0)
    there.wait_send(1, 0, 4, 1)
    home.wait_send(0, 0, 4, 0)
    home.wait_send(1, 0, 3, 1)
    home.wait_send(1, 3, 1, 2)
    for one in (chosen_up, chosen_down, sum_down, sum_up_main, sum_up_tail):
        one.wait_send()


def last_kernel(total_ref, row_ref, potential_ref, result_ref, pad_ref):
    pad_ref[...] = jnp.zeros_like(pad_ref)
    pad_ref[:NZ, :] = unpack_field(total_ref[...])
    potential_ref[:, 0, :] = jnp.transpose(pad_ref[...])[:ROWS, :NZ]
    row = row_ref[...]
    lane = lanes((1, BLK))
    result = jnp.zeros((1, BLK), F32)
    for b in range(BLK):
        mine = lanes((1, 128)) // 32 == b
        result = jnp.where(lane == b, jnp.sum(jnp.where(mine, row, 0.0), axis=1, keepdims=True), result)
    result_ref[...] = result


def vm():
    return pl.BlockSpec(memory_space=pltpu.VMEM)


def sm():
    return pl.BlockSpec(memory_space=pltpu.SMEM)


def params(**extra):
    return pltpu.CompilerParams(vmem_limit_bytes=VMEM_LIMIT, **extra)


def shape(*dims):
    return jax.ShapeDtypeStruct(dims, F32)


def body(orbitals, picked, shells):
    forward, inverse = z_stacks()
    along_x, along_y = x_table(), y_tables()
    exchange = pltpu.VMEM((2, FFT, 4, 8, 128), F32)
    field = pltpu.VMEM((288, 128), F32)
    bands = pltpu.VMEM((BLK, 288, 128), F32)
    line = pltpu.VMEM((1, 128), F32)
    dma = pltpu.SemaphoreType.DMA
    total, row = pl.pallas_call(
        whole_kernel,
        out_shape=(shape(288, 128), shape(1, 128)),
        in_specs=[sm(), sm()] + [pl.BlockSpec(memory_space=pl.ANY)] * 6,
        out_specs=(vm(), vm()),
        scratch_shapes=[
            pltpu.VMEM((ROWS, BLK, NZ), F32),
            pltpu.VMEM(forward.shape, BF16),
            pltpu.VMEM(inverse.shape, BF16),
            pltpu.VMEM((NX, 128), F32),
            pltpu.VMEM(along_x.shape, BF16),
            pltpu.VMEM(along_y.shape, BF16),
            dma((6,)),
            bands,
            bands,
        ]
        + [field] * 7
        + [exchange] * 4
        + [
            pltpu.VMEM((1536, 128), F32),
            pltpu.VMEM((24 * NX, 128), F32),
            pltpu.VMEM((PLANES * NX, 256), F32),
            pltpu.VMEM((2 * PLANES * NX, 128), F32),
            pltpu.VMEM((256, 256), F32),
            line,
            pltpu.VMEM((8, 1, 128), F32),
            line,
            pltpu.VMEM((4, 1, 128), F32),
        ]
        + [dma((2,))] * 2
        + [dma((3,))] * 2
        + [dma((5,))] * 2
        + [dma((8,))] * 2
        + [dma((4,))] * 2,
        compiler_params=params(collective_id=0, has_side_effects=True),
    )(
        picked, shells, jnp.transpose(orbitals, (1, 0, 2)), jnp.asarray(forward), jnp.asarray(inverse),
        jnp.asarray(xy_square()), jnp.asarray(along_x), jnp.asarray(along_y),
    )
    potentials, result = pl.pallas_call(
        last_kernel,
        out_shape=(shape(ROWS, 1, NZ), shape(1, BLK)),
        in_specs=[vm()] * 2,
        out_specs=(vm(), vm()),
        scratch_shapes=[pltpu.VMEM((256, 256), F32)],
        compiler_params=params(),
    )(total, row)
    return jnp.transpose(potentials, (1, 0, 2)), jnp.transpose(result)


def solution(mesh):
    return jax.shard_map(
        body,
        mesh=mesh,
        in_specs=(P("band", "fft", None), P("band"), P()),
        out_specs=(P("band", "fft", None), P("band", None)),
        check_vma=False,
    )
```

```python
import math

import jax
import jax.numpy as jnp
import numpy as np
from jax import lax
from jax.experimental import pallas as pl
from jax.experimental.pallas import tpu as pltpu
from jax.sharding import PartitionSpec as P

NX = 72
NY = 72
NZ = 216
BLK = 4
NSHELL = 64
FIELDS = 7
FFT = 32
ROWS = 162
MAIN = 128
TAIL = ROWS - MAIN
SLABS = 9
PLANES = 13

SPACING = 0.2
SCREENING = 0.106
FRACTION = 0.25
SPAN = math.lcm(NX, NY, NZ)
QTOP = (SPAN // NX) ** 2 * (NX // 2) ** 2 + (SPAN // NY) ** 2 * (NY // 2) ** 2 + (SPAN // NZ) ** 2 * (NZ // 2) ** 2
MESH = pl.DeviceIdType.MESH
F32 = jnp.float32
BF16 = jnp.bfloat16
VMEM_LIMIT = 53 * 1024 * 1024


def halves(table):
    table = np.asarray(table, np.float32)
    high = table.astype(jnp.bfloat16)
    low = (table - high.astype(np.float32)).astype(jnp.bfloat16)
    return high, low


def z_tables():
    freq, is_sin = np.zeros(NZ, np.int64), np.zeros(NZ, bool)
    for t in range(NZ // 8):
        for i in range(4):
            freq[8 * t + i] = 4 * t + i
            freq[8 * t + 4 + i] = 4 * t + i
            is_sin[8 * t + 4 + i] = True
    freq[4], is_sin[4] = NZ // 2, False
    angle = 2 * np.pi * (freq[:, None] * np.arange(NZ)[None, :] % NZ) / NZ
    forward = np.where(is_sin[:, None], -np.sin(angle), np.cos(angle))
    weight = np.where((freq == 0) | (freq == NZ // 2), 1.0, 2.0) / (NX * NY * NZ)
    inverse = (-FRACTION * weight[:, None] * forward).T
    return forward, inverse


def z_stacks():
    forward, inverse = z_tables()
    pad = np.zeros((8, NZ), jnp.bfloat16)

    def stack(table):
        high, low = halves(table)
        return np.concatenate([high, pad, low, pad], axis=0)

    return stack(forward), stack(inverse)


def xy_angle():
    index = np.arange(NX)
    return 2 * np.pi * (index[:, None] * index[None, :] % NX) / NX


def x_table():
    table = np.concatenate([np.cos(xy_angle()), np.sin(xy_angle())], axis=0)
    high, low = halves(table)
    pad = np.zeros((2 * NX, 8), high.dtype)
    return np.concatenate([high, pad, low, pad, high, pad], axis=1)


def y_tables():
    cosine, sine = np.cos(xy_angle()), np.sin(xy_angle())
    forward = np.zeros((256, 256))
    forward[:NY, :NY] = cosine
    forward[128:128 + NY, 128:128 + NY] = cosine
    forward[:NY, 128:128 + NY] = -sine
    forward[128:128 + NY, :NY] = sine
    fh, fl = halves(forward)
    return np.stack([fh, fl, fh.T, fl.T])


def xy_square():
    index = np.arange(NX)
    signed = np.where(index > NX // 2, index - NX, index)
    square = np.zeros((NX, 128), np.float32)
    square[:, :NY] = 9 * (signed[:, None] ** 2 + signed[None, :] ** 2)
    return square


def split(value):
    high = value.astype(BF16)
    return high, (value - high.astype(F32)).astype(BF16)


def mm(left, right):
    return lax.dot_general(left, right, (((1,), (0,)), ((), ())), preferred_element_type=F32)


def lanes(shape):
    return lax.broadcasted_iota(jnp.int32, shape, len(shape) - 1)


def turn(value, shift):
    shift = shift % 128
    return value if shift == 0 else pltpu.roll(value, shift, 1)


def pack_tail(parts):
    lane = lanes(parts[0].shape)
    upper = jnp.where(lane < 2 * TAIL, turn(parts[1], TAIL), turn(parts[2], 2 * TAIL))
    return jnp.where(lane < TAIL, parts[0], upper)


def pack_thirds(tail):
    third = NZ // 3
    return pack_tail([tail[third * g:third * (g + 1)] for g in range(3)])


def pack_field(wide):
    return jnp.concatenate([wide[:, :MAIN], pack_thirds(wide[:, MAIN:])], axis=0)


def unpack_field(packed):
    tail = packed[NZ:]
    tails = jnp.concatenate([turn(tail, -TAIL * g) for g in range(3)], axis=0)
    return jnp.concatenate([packed[:NZ], tails], axis=1)


def z_transform(table_ref, wide):
    high, low = split(wide)
    both = mm(table_ref[...], high)
    return both[:NZ] + both[NZ + 8:2 * NZ + 8] + mm(table_ref[:NZ + 8], low)[:NZ]


def turned_band(band, pad_ref):
    pad_ref[:ROWS, :NZ] = band
    return pack_field(jnp.transpose(pad_ref[...])[:NZ])


def order_bands(picked, orbitals_ref, own_ref, order_ref, pad_ref):
    for b in range(BLK):
        own_ref[b] = turned_band(orbitals_ref[:, b, :], pad_ref)
    for j in range(1, BLK):
        order_ref[j] = jnp.where(picked >= j, own_ref[j - 1], own_ref[j])


def visitor_of(f):
    return (True, f + 1) if f < 3 else (False, f - 3)


def cuts_of(f):
    result = []
    for chunk in range(2):
        low, high = max(NZ * f, 768 * chunk), min(NZ * (f + 1), 768 * (chunk + 1))
        if low < high:
            result.append((low, high - low, low + 256 * chunk))
    return result


def runs(row, rows):
    tile, count = row // 8, rows // 8
    done = 0
    while done < count:
        place, peer = divmod(tile + done, FFT)
        take = min(count - done, FFT - peer)
        yield place // 4, place % 4, peer, take, done
        done += take


def put_rows(buffer, row, value):
    tiles = value.reshape(value.shape[0] // 8, 8, 128)
    for chunk, part, peer, take, done in runs(row, value.shape[0]):
        buffer[chunk, peer:peer + take, part] = tiles[done:done + take]


def get_rows(buffer, row, rows):
    parts = [buffer[chunk, peer:peer + take, part].reshape(8 * take, 128) for chunk, part, peer, take, _ in runs(row, rows)]
    return parts[0] if len(parts) == 1 else jnp.concatenate(parts, axis=0)


def spectrum_of(f, order_ref, upper_ref, lower_ref, table_ref, buffer, tail_ref):
    low_side, j = visitor_of(f)
    density = (lower_ref if low_side else upper_ref)[...] * order_ref[j]
    spectrum = z_transform(table_ref, unpack_field(density))
    for low, count, place in cuts_of(f):
        first = low - NZ * f
        put_rows(buffer, place, spectrum[first:first + count, :MAIN])
        tail_ref[pl.ds(low, count), :] = spectrum[first:first + count, MAIN:]


def close_tails(chunk, buffer, tail_ref):
    parts = [tail_ref[pl.ds(768 * chunk + 256 * p, 256), :] for p in range(3)]
    put_rows(buffer, 1024 * chunk + 768, pack_tail(parts))


def open_tails(chunk, buffer, tail_ref):
    tails = get_rows(buffer, 1024 * chunk + 768, 256)
    for p in range(3):
        tail_ref[pl.ds(768 * chunk + 256 * p, 256), :] = turn(tails, -TAIL * p)


def main_of(f, buffer):
    mains = [get_rows(buffer, place, count) for _, count, place in cuts_of(f)]
    return mains[0] if len(mains) == 1 else jnp.concatenate(mains, axis=0)


def tail_of(f, tail_ref):
    return tail_ref[pl.ds(NZ * f, NZ), :]


def pieces():
    result = []
    row = 0
    while row < 4 * ROWS:
        source, j = divmod(row, ROWS)
        slab, y = divmod(row, NY)
        stop = min((source + 1) * ROWS, (slab + 1) * NY)
        if j < MAIN:
            stop = min(stop, source * ROWS + MAIN)
        result.append((source, j >= MAIN, j if j < MAIN else j - MAIN, slab, y, stop - row))
        row = stop
    return result


def tile_of(owner, chunk, p):
    return lax.rem(96 * chunk + 32 * p + owner, NZ // 8)


def gain_of(owner, plane, shells_ref, xy_ref, gain):
    chunk, place = plane // PLANES, lax.rem(plane, PLANES)
    depth = jnp.where(place == PLANES - 1, NZ // 2, 4 * tile_of(owner, chunk, place // 4) + lax.rem(place, 4))
    square = xy_ref[...] + (depth * depth).astype(F32)
    total = jnp.full(square.shape, shells_ref[0].astype(F32), F32)
    for s in range(1, NSHELL):
        step = (shells_ref[s] - shells_ref[s - 1]).astype(F32)
        total = total + jnp.where(square >= float(-(-s * (QTOP + 1) // NSHELL)), step, 0.0)
    g_squared = (2.0 * math.pi / (SPACING * SPAN)) ** 2 * square
    safe = jnp.where(square == 0, 1.0, g_squared)
    value = 4.0 * math.pi / safe * (1.0 - jnp.exp(-safe / (4.0 * SCREENING**2)))
    gain[pl.ds(pl.multiple_of(plane * NX, 8), NX), :] = total * jnp.where(square == 0, math.pi / SCREENING**2, value)


def open_rows(got_ref, chunk, box):
    cuts = pieces()
    lane = lanes((8, 128))

    def one(chip, carry):
        for slab in range(SLABS):
            mine = [c for c in cuts if c[3] == slab]
            for p in range(3):
                value = None
                for source, tail, first, _, y, _ in mine:
                    part = got_ref[chunk, 4 * chip + source, 3 if tail else p]
                    part = turn(part, y - first - (TAIL * p if tail else 0))
                    value = part if value is None else jnp.where(lane >= y, part, value)
                box[pl.ds(8 * p * NX + SLABS * chip + slab, 8, stride=NX), :] = value
        return carry

    lax.fori_loop(0, 8, one, 0)


def close_rows(box, chunk, send_ref):
    cuts = pieces()
    lane = lanes((8, 128))

    def one(chip, carry):
        fields = [[box[pl.ds(8 * p * NX + SLABS * chip + slab, 8, stride=NX), :] for slab in range(SLABS)] for p in range(3)]
        for source in range(4):
            tail_value = None
            for p in range(3):
                value = None
                for s, tail, first, slab, y, _ in cuts:
                    if s != source:
                        continue
                    if tail:
                        place = first + TAIL * p
                        part = turn(fields[p][slab], place - y)
                        tail_value = part if tail_value is None else jnp.where(lane >= place, part, tail_value)
                    else:
                        part = turn(fields[p][slab], first - y)
                        value = part if value is None else jnp.where(lane >= first, part, value)
                send_ref[chunk, 4 * chip + source, p] = value
            send_ref[chunk, 4 * chip + source, 3] = tail_value
        return carry

    lax.fori_loop(0, 8, one, 0)


def screen_planes(owner, chunk, x_ref, y_ref, box, work, gain):
    flags = [jnp.where(tile_of(owner, chunk, p) == 0, 1.0, 0.0).astype(F32) for p in range(3)]

    def along_x(real, imag):
        wide = jnp.concatenate([real, imag], axis=1)
        wide = jnp.concatenate([wide, jnp.zeros((8, 256), F32)], axis=0)
        high, low = split(wide)
        both = mm(x_ref[...], jnp.concatenate([high, high, low], axis=0))
        return both[:NX, :128], both[:NX, 128:], both[NX:, :128], both[NX:, 128:]

    def along_y(value, k):
        high, low = split(value)
        return mm(high, y_ref[k]) + mm(low, y_ref[k]) + mm(high, y_ref[k + 1])

    for plane in range(PLANES):
        if plane == 12:
            real = sum(flags[p] * box[pl.ds((8 * p + 4) * NX, NX), :] for p in range(3))
            imag = jnp.zeros_like(real)
        else:
            p, i = divmod(plane, 4)
            real = box[pl.ds((8 * p + i) * NX, NX), :]
            imag = box[pl.ds((8 * p + 4 + i) * NX, NX), :]
            if i == 0:
                imag = imag * (1.0 - flags[p])
        cr, ci, sr, si = along_x(real, imag)
        work[pl.ds(plane * NX, NX), :] = jnp.concatenate([cr + si, ci - sr], axis=1)
    weight = gain[pl.ds(chunk * PLANES * NX, PLANES * NX), :]
    value = along_y(work[...], 0) * jnp.concatenate([weight, weight], axis=1)
    work[...] = along_y(value, 2)
    extra = None
    for plane in reversed(range(PLANES)):
        rows = work[pl.ds(plane * NX, NX), :]
        cr, ci, sr, si = along_x(rows[:, :128], rows[:, 128:])
        real, imag = cr - si, ci + sr
        if plane == 12:
            extra = real
        else:
            p, i = divmod(plane, 4)
            if i == 0:
                imag = imag * (1.0 - flags[p]) + extra * flags[p]
            box[pl.ds((8 * p + i) * NX, NX), :] = real
            box[pl.ds((8 * p + 4 + i) * NX, NX), :] = imag


def intersect(total, bands_ref, partial_ref):
    lines = []
    for b in range(BLK):
        product = (bands_ref[b] * total).reshape(36, 8, 128)
        line = jnp.sum(jnp.sum(product, axis=0), axis=0, keepdims=True)
        line = line + turn(line, 64)
        lines.append(line + turn(line, 32))
    quarter = lanes((1, 128)) // 32
    row = lines[0]
    for b in range(1, BLK):
        row = jnp.where(quarter == b, lines[b], row)
    partial_ref[...] = row * SPACING**3


STEPS = [((1, -2, 3, -1, 2, -3, 4)[k % 7], (0, 2, 1, 3)[k % 4]) for k in range(28)] + [(0, turned) for turned in (2, 1, 3)]


class Ring:
    def __init__(self, me, source, target, send_sem, recv_sem):
        self.source, self.target = source, target
        self.send_sem, self.recv_sem = send_sem, recv_sem
        self.me = me
        self.places = [lax.rem(me // 4 + k, 8) for k in range(8)]
        self.parts = [lax.rem(lax.rem(me, 4) + k, 4) for k in range(4)]

    def device(self, far, turned):
        return 4 * self.places[far % 8] + self.parts[turned % 4]

    def copy(self, source, target, peer, k):
        return pltpu.make_async_remote_copy(
            src_ref=source, dst_ref=target, send_sem=self.send_sem.at[k], recv_sem=self.recv_sem.at[k],
            device_id={"fft": peer}, device_id_type=MESH,
        )

    def start(self, chunk, first, count, k):
        rows = pl.ds(first, count)
        for far, turned in STEPS:
            peer = self.device(far, turned)
            self.copy(self.source.at[chunk, peer, rows], self.target.at[chunk, self.me, rows], peer, k).start()
        self.target[chunk, self.me, first:first + count] = self.source[chunk, self.me, first:first + count]

    def wait_recv(self, chunk, first, count, k):
        whole = self.target.at[chunk, pl.ds(0, FFT - 1), pl.ds(first, count)]
        self.copy(whole, whole, self.device(1, 0), k).wait_recv()

    def wait_send(self, chunk, first, count, k):
        whole = self.source.at[chunk, pl.ds(0, FFT - 1), pl.ds(first, count)]
        self.copy(whole, whole, self.device(1, 0), k).wait_send()


def whole_kernel(
    picked_ref, shells_ref, orbitals_far, forward_far, inverse_far, xy_far, x_far, y_far,
    total_ref, result_ref,
    orbitals_ref, forward_ref, inverse_ref, xy_ref, x_ref, y_ref, fetch_sem,
    own, order, upper, lower, up, down, above, below, mine, sent, got, back, returned, tails, box, work, gain, pad,
    partial, ring_slots, near, near_slots,
    there_send, there_recv, home_send, home_recv, band_send, band_recv, ring_send, ring_recv, near_send, near_recv,
):
    me = lax.axis_index("fft")
    group = lax.axis_index("band")
    count = lax.axis_size("band")
    above_me, below_me = lax.rem(group + 1, count), lax.rem(group + count - 1, count)

    barrier = pltpu.get_barrier_semaphore()
    for peer in (above_me, below_me):
        pl.semaphore_signal(barrier, inc=1, device_id={"band": peer}, device_id_type=MESH)
    there = Ring(me, sent, got, there_send, there_recv)
    home = Ring(me, back, returned, home_send, home_recv)
    for far, turned in STEPS:
        peer = there.device(far, turned)
        pl.semaphore_signal(barrier, inc=1, device_id={"fft": peer}, device_id_type=MESH)

    def to_band(source, target, peer, k):
        return pltpu.make_async_remote_copy(
            src_ref=source, dst_ref=target, send_sem=band_send.at[k], recv_sem=band_recv.at[k],
            device_id={"band": peer}, device_id_type=MESH,
        )

    chosen_up = to_band(order.at[0], lower, above_me, 0)
    chosen_down = to_band(order.at[0], upper, below_me, 1)
    sum_down = to_band(down, above, below_me, 2)
    main, tail = pl.ds(0, NZ), pl.ds(NZ, NZ // 3)
    sum_up_main = to_band(up.at[main], below.at[main], above_me, 3)
    sum_up_tail = to_band(up.at[tail], below.at[tail], above_me, 4)

    fetches = [
        pltpu.make_async_copy(far, ref, fetch_sem.at[k])
        for k, (far, ref) in enumerate(
            [
                (orbitals_far, orbitals_ref), (xy_far, xy_ref), (forward_far, forward_ref),
                (x_far, x_ref), (y_far, y_ref), (inverse_far, inverse_ref),
            ]
        )
    ]
    for one in fetches:
        one.start()
    picked = picked_ref[0]
    fetches[0].wait()
    pad[...] = jnp.zeros_like(pad)
    order[0] = turned_band(orbitals_ref[:, picked, :], pad)
    pl.semaphore_wait(barrier, FFT + 1)
    chosen_up.start()
    order_bands(picked, orbitals_ref, own, order, pad)

    def gain_step(plane, carry):
        gain_of(me, plane, shells_ref, xy_ref, gain)
        return carry

    for one in fetches[1:]:
        one.wait()
    lax.fori_loop(0, 3, gain_step, 0)
    chosen_down.start()
    lax.fori_loop(3, 10, gain_step, 0)
    tails[pl.ds(NZ * FIELDS, 24), :] = jnp.zeros((24, 128), F32)
    put_rows(sent, NZ * FIELDS + 256, jnp.zeros((24, 128), F32))

    chosen_up.wait_recv()
    for f in range(3):
        spectrum_of(f, order, upper, lower, forward_ref, sent, tails)
    there.start(0, 0, 2, 0)
    chosen_down.wait_recv()
    spectrum_of(3, order, upper, lower, forward_ref, sent, tails)
    close_tails(0, sent, tails)
    there.start(0, 2, 2, 0)
    for f in range(4, FIELDS):
        spectrum_of(f, order, upper, lower, forward_ref, sent, tails)
    close_tails(1, sent, tails)
    there.start(1, 0, 4, 1)
    lax.fori_loop(10, 2 * PLANES, gain_step, 0)

    for chunk in range(2):
        there.wait_recv(chunk, 0, 4, chunk)
        open_rows(got, chunk, box)
        screen_planes(me, chunk, x_ref, y_ref, box, work, gain)
        close_rows(box, chunk, back)
        if chunk == 0:
            home.start(0, 0, 4, 0)
        else:
            home.start(1, 0, 3, 1)
            home.start(1, 3, 1, 2)

    home.wait_recv(0, 0, 4, 0)
    open_tails(0, returned, tails)
    total = None
    for f in range(3):
        field = pack_field(z_transform(inverse_ref, jnp.concatenate([main_of(f, returned), tail_of(f, tails)], axis=1)))
        term = field * order[visitor_of(f)[1]]
        total = term if total is None else total + term
    down[...] = total
    sum_down.start()

    def up_part(rows, fields):
        total = None
        for f, field in fields:
            if f == 3:
                mine[rows, :] = field * upper[rows, :]
            term = field * order[visitor_of(f)[1], rows, :]
            total = term if total is None else total + term
        up[rows, :] = total

    home.wait_recv(1, 0, 3, 1)
    up_part(main, [(f, z_transform(inverse_ref, main_of(f, returned))) for f in range(3, FIELDS)])
    sum_up_main.start()
    home.wait_recv(1, 3, 1, 2)
    open_tails(1, returned, tails)
    up_part(tail, [(f, pack_thirds(z_transform(inverse_ref, tail_of(f, tails)))) for f in range(3, FIELDS)])
    sum_up_tail.start()
    sum_down.wait_recv()
    mine[...] += above[...]
    sum_up_main.wait_recv()
    sum_up_tail.wait_recv()
    total = mine[...] + below[...]
    total_ref[...] = total
    intersect(total, own, partial)

    place, part = me // 4, lax.rem(me, 4)

    def row_to(source, target, peer, send_sem, recv_sem):
        return pltpu.make_async_remote_copy(
            src_ref=source, dst_ref=target, send_sem=send_sem, recv_sem=recv_sem,
            device_id={"fft": peer}, device_id_type=MESH,
        )

    ring = [
        row_to(partial, ring_slots.at[k], 4 * lax.rem(place + k, 8) + part, ring_send.at[k], ring_recv.at[k])
        for k in range(1, 8)
    ]
    for one in ring:
        one.start()
    row = partial[...]
    for k, one in enumerate(ring):
        one.wait()
        row = row + ring_slots[k + 1]
    near[...] = row
    beside = [
        row_to(near, near_slots.at[k], 4 * place + lax.rem(part + k, 4), near_send.at[k], near_recv.at[k])
        for k in range(1, 4)
    ]
    for one in beside:
        one.start()
    for k, one in enumerate(beside):
        one.wait()
        row = row + near_slots[k + 1]
    result_ref[...] = row

    there.wait_send(0, 0, 4, 0)
    there.wait_send(1, 0, 4, 1)
    home.wait_send(0, 0, 4, 0)
    home.wait_send(1, 0, 3, 1)
    home.wait_send(1, 3, 1, 2)
    for one in (chosen_up, chosen_down, sum_down, sum_up_main, sum_up_tail):
        one.wait_send()


def last_kernel(total_ref, row_ref, potential_ref, result_ref, pad_ref):
    pad_ref[...] = jnp.zeros_like(pad_ref)
    pad_ref[:NZ, :] = unpack_field(total_ref[...])
    potential_ref[:, 0, :] = jnp.transpose(pad_ref[...])[:ROWS, :NZ]
    row = row_ref[...]
    lane = lanes((1, BLK))
    result = jnp.zeros((1, BLK), F32)
    for b in range(BLK):
        mine = lanes((1, 128)) // 32 == b
        result = jnp.where(lane == b, jnp.sum(jnp.where(mine, row, 0.0), axis=1, keepdims=True), result)
    result_ref[...] = result


def vm():
    return pl.BlockSpec(memory_space=pltpu.VMEM)


def sm():
    return pl.BlockSpec(memory_space=pltpu.SMEM)


def params(**extra):
    return pltpu.CompilerParams(vmem_limit_bytes=VMEM_LIMIT, **extra)


def shape(*dims):
    return jax.ShapeDtypeStruct(dims, F32)


def body(orbitals, picked, shells):
    forward, inverse = z_stacks()
    along_x, along_y = x_table(), y_tables()
    exchange = pltpu.VMEM((2, FFT, 4, 8, 128), F32)
    field = pltpu.VMEM((288, 128), F32)
    bands = pltpu.VMEM((BLK, 288, 128), F32)
    line = pltpu.VMEM((1, 128), F32)
    dma = pltpu.SemaphoreType.DMA
    total, row = pl.pallas_call(
        whole_kernel,
        out_shape=(shape(288, 128), shape(1, 128)),
        in_specs=[sm(), sm()] + [pl.BlockSpec(memory_space=pltpu.HBM)] * 6,
        out_specs=(vm(), vm()),
        scratch_shapes=[
            pltpu.VMEM((ROWS, BLK, NZ), F32),
            pltpu.VMEM(forward.shape, BF16),
            pltpu.VMEM(inverse.shape, BF16),
            pltpu.VMEM((NX, 128), F32),
            pltpu.VMEM(along_x.shape, BF16),
            pltpu.VMEM(along_y.shape, BF16),
            dma((6,)),
            bands,
            bands,
        ]
        + [field] * 7
        + [exchange] * 4
        + [
            pltpu.VMEM((1536, 128), F32),
            pltpu.VMEM((24 * NX, 128), F32),
            pltpu.VMEM((PLANES * NX, 256), F32),
            pltpu.VMEM((2 * PLANES * NX, 128), F32),
            pltpu.VMEM((256, 256), F32),
            line,
            pltpu.VMEM((8, 1, 128), F32),
            line,
            pltpu.VMEM((4, 1, 128), F32),
        ]
        + [dma((2,))] * 2
        + [dma((3,))] * 2
        + [dma((5,))] * 2
        + [dma((8,))] * 2
        + [dma((4,))] * 2,
        compiler_params=params(collective_id=0, has_side_effects=True),
    )(
        picked, shells, jnp.transpose(orbitals, (1, 0, 2)), jnp.asarray(forward), jnp.asarray(inverse),
        jnp.asarray(xy_square()), jnp.asarray(along_x), jnp.asarray(along_y),
    )
    potentials, result = pl.pallas_call(
        last_kernel,
        out_shape=(shape(ROWS, 1, NZ), shape(1, BLK)),
        in_specs=[vm()] * 2,
        out_specs=(vm(), vm()),
        scratch_shapes=[pltpu.VMEM((256, 256), F32)],
        compiler_params=params(),
    )(total, row)
    return jnp.transpose(potentials, (1, 0, 2)), jnp.transpose(result)


def solution(mesh):
    return jax.shard_map(
        body,
        mesh=mesh,
        in_specs=(P("band", "fft", None), P("band"), P()),
        out_specs=(P("band", "fft", None), P("band", None)),
        check_vma=False,
    )
```

```python
import math

import jax
import jax.numpy as jnp
import numpy as np
from jax import lax
from jax.experimental import pallas as pl
from jax.experimental.pallas import tpu as pltpu
from jax.sharding import PartitionSpec as P

NX = 72
NY = 72
NZ = 216
BLK = 4
NSHELL = 64
FIELDS = 7
FFT = 32
ROWS = 162
MAIN = 128
TAIL = ROWS - MAIN
SLABS = 9
PLANES = 13

SPACING = 0.2
SCREENING = 0.106
FRACTION = 0.25
SPAN = math.lcm(NX, NY, NZ)
QTOP = (SPAN // NX) ** 2 * (NX // 2) ** 2 + (SPAN // NY) ** 2 * (NY // 2) ** 2 + (SPAN // NZ) ** 2 * (NZ // 2) ** 2
MESH = pl.DeviceIdType.MESH
F32 = jnp.float32
BF16 = jnp.bfloat16
VMEM_LIMIT = 60 * 1024 * 1024


def halves(table):
    table = np.asarray(table, np.float32)
    high = table.astype(jnp.bfloat16)
    low = (table - high.astype(np.float32)).astype(jnp.bfloat16)
    return high, low


def z_tables():
    freq, is_sin = np.zeros(NZ, np.int64), np.zeros(NZ, bool)
    for t in range(NZ // 8):
        for i in range(4):
            freq[8 * t + i] = 4 * t + i
            freq[8 * t + 4 + i] = 4 * t + i
            is_sin[8 * t + 4 + i] = True
    freq[4], is_sin[4] = NZ // 2, False
    angle = 2 * np.pi * (freq[:, None] * np.arange(NZ)[None, :] % NZ) / NZ
    forward = np.where(is_sin[:, None], -np.sin(angle), np.cos(angle))
    weight = np.where((freq == 0) | (freq == NZ // 2), 1.0, 2.0) / (NX * NY * NZ)
    inverse = (-FRACTION * weight[:, None] * forward).T
    return forward, inverse


def z_stacks():
    forward, inverse = z_tables()
    pad = np.zeros((8, NZ), jnp.bfloat16)

    def stack(table):
        high, low = halves(table)
        return np.concatenate([high, pad, low, pad], axis=0)

    return stack(forward), stack(inverse)


def xy_angle():
    index = np.arange(NX)
    return 2 * np.pi * (index[:, None] * index[None, :] % NX) / NX


def x_table():
    table = np.concatenate([np.cos(xy_angle()), np.sin(xy_angle())], axis=0)
    high, low = halves(table)
    pad = np.zeros((2 * NX, 8), high.dtype)
    return np.concatenate([high, pad, low, pad, high, pad], axis=1)


def y_tables():
    cosine, sine = np.cos(xy_angle()), np.sin(xy_angle())
    forward = np.zeros((256, 256))
    forward[:NY, :NY] = cosine
    forward[128:128 + NY, 128:128 + NY] = cosine
    forward[:NY, 128:128 + NY] = -sine
    forward[128:128 + NY, :NY] = sine
    fh, fl = halves(forward)
    return np.stack([fh, fl, fh.T, fl.T])


def xy_square():
    index = np.arange(NX)
    signed = np.where(index > NX // 2, index - NX, index)
    square = np.zeros((NX, 128), np.float32)
    square[:, :NY] = 9 * (signed[:, None] ** 2 + signed[None, :] ** 2)
    return square


def split(value):
    high = value.astype(BF16)
    return high, (value - high.astype(F32)).astype(BF16)


def mm(left, right):
    return lax.dot_general(left, right, (((1,), (0,)), ((), ())), preferred_element_type=F32)


def lanes(shape):
    return lax.broadcasted_iota(jnp.int32, shape, len(shape) - 1)


def turn(value, shift):
    shift = shift % 128
    return value if shift == 0 else pltpu.roll(value, shift, 1)


def pack_tail(parts):
    lane = lanes(parts[0].shape)
    upper = jnp.where(lane < 2 * TAIL, turn(parts[1], TAIL), turn(parts[2], 2 * TAIL))
    return jnp.where(lane < TAIL, parts[0], upper)


def pack_thirds(tail):
    third = NZ // 3
    return pack_tail([tail[third * g:third * (g + 1)] for g in range(3)])


def pack_field(wide):
    return jnp.concatenate([wide[:, :MAIN], pack_thirds(wide[:, MAIN:])], axis=0)


def unpack_field(packed):
    tail = packed[NZ:]
    tails = jnp.concatenate([turn(tail, -TAIL * g) for g in range(3)], axis=0)
    return jnp.concatenate([packed[:NZ], tails], axis=1)


def z_transform(table_ref, wide):
    high, low = split(wide)
    both = mm(table_ref[...], high)
    return both[:NZ] + both[NZ + 8:2 * NZ + 8] + mm(table_ref[:NZ + 8], low)[:NZ]


def turned_band(band, pad_ref):
    pad_ref[:ROWS, :NZ] = band
    return pack_field(jnp.transpose(pad_ref[...])[:NZ])


def order_bands(picked, orbitals_ref, own_ref, order_ref, pad_ref):
    for b in range(BLK):
        own_ref[b] = turned_band(orbitals_ref[:, b, :], pad_ref)
    for j in range(1, BLK):
        order_ref[j] = jnp.where(picked >= j, own_ref[j - 1], own_ref[j])


def visitor_of(f):
    return (True, f + 1) if f < 3 else (False, f - 3)


def cuts_of(f):
    result = []
    for chunk in range(2):
        low, high = max(NZ * f, 768 * chunk), min(NZ * (f + 1), 768 * (chunk + 1))
        if low < high:
            result.append((low, high - low, low + 256 * chunk))
    return result


def runs(row, rows):
    tile, count = row // 8, rows // 8
    done = 0
    while done < count:
        place, peer = divmod(tile + done, FFT)
        take = min(count - done, FFT - peer)
        yield place // 4, place % 4, peer, take, done
        done += take


def put_rows(buffer, row, value):
    tiles = value.reshape(value.shape[0] // 8, 8, 128)
    for chunk, part, peer, take, done in runs(row, value.shape[0]):
        buffer[chunk, peer:peer + take, part] = tiles[done:done + take]


def get_rows(buffer, row, rows):
    parts = [buffer[chunk, peer:peer + take, part].reshape(8 * take, 128) for chunk, part, peer, take, _ in runs(row, rows)]
    return parts[0] if len(parts) == 1 else jnp.concatenate(parts, axis=0)


def spectrum_of(f, order_ref, upper_ref, lower_ref, table_ref, buffer, tail_ref):
    low_side, j = visitor_of(f)
    density = (lower_ref if low_side else upper_ref)[...] * order_ref[j]
    spectrum = z_transform(table_ref, unpack_field(density))
    for low, count, place in cuts_of(f):
        first = low - NZ * f
        put_rows(buffer, place, spectrum[first:first + count, :MAIN])
        tail_ref[pl.ds(low, count), :] = spectrum[first:first + count, MAIN:]


def close_tails(chunk, buffer, tail_ref):
    parts = [tail_ref[pl.ds(768 * chunk + 256 * p, 256), :] for p in range(3)]
    put_rows(buffer, 1024 * chunk + 768, pack_tail(parts))


def open_tails(chunk, buffer, tail_ref):
    tails = get_rows(buffer, 1024 * chunk + 768, 256)
    for p in range(3):
        tail_ref[pl.ds(768 * chunk + 256 * p, 256), :] = turn(tails, -TAIL * p)


def main_of(f, buffer):
    mains = [get_rows(buffer, place, count) for _, count, place in cuts_of(f)]
    return mains[0] if len(mains) == 1 else jnp.concatenate(mains, axis=0)


def tail_of(f, tail_ref):
    return tail_ref[pl.ds(NZ * f, NZ), :]


def pieces():
    result = []
    row = 0
    while row < 4 * ROWS:
        source, j = divmod(row, ROWS)
        slab, y = divmod(row, NY)
        stop = min((source + 1) * ROWS, (slab + 1) * NY)
        if j < MAIN:
            stop = min(stop, source * ROWS + MAIN)
        result.append((source, j >= MAIN, j if j < MAIN else j - MAIN, slab, y, stop - row))
        row = stop
    return result


def tile_of(owner, chunk, p):
    return lax.rem(96 * chunk + 32 * p + owner, NZ // 8)


def gain_of(owner, plane, shells_ref, xy_ref, gain):
    chunk, place = plane // PLANES, lax.rem(plane, PLANES)
    depth = jnp.where(place == PLANES - 1, NZ // 2, 4 * tile_of(owner, chunk, place // 4) + lax.rem(place, 4))
    square = xy_ref[...] + (depth * depth).astype(F32)
    total = jnp.full(square.shape, shells_ref[0].astype(F32), F32)
    for s in range(1, NSHELL):
        step = (shells_ref[s] - shells_ref[s - 1]).astype(F32)
        total = total + jnp.where(square >= float(-(-s * (QTOP + 1) // NSHELL)), step, 0.0)
    g_squared = (2.0 * math.pi / (SPACING * SPAN)) ** 2 * square
    safe = jnp.where(square == 0, 1.0, g_squared)
    value = 4.0 * math.pi / safe * (1.0 - jnp.exp(-safe / (4.0 * SCREENING**2)))
    gain[pl.ds(pl.multiple_of(plane * NX, 8), NX), :] = total * jnp.where(square == 0, math.pi / SCREENING**2, value)


def open_rows(got_ref, chunk, box):
    cuts = pieces()
    lane = lanes((8, 128))

    def one(chip, carry):
        for slab in range(SLABS):
            mine = [c for c in cuts if c[3] == slab]
            for p in range(3):
                value = None
                for source, tail, first, _, y, _ in mine:
                    part = got_ref[chunk, 4 * chip + source, 3 if tail else p]
                    part = turn(part, y - first - (TAIL * p if tail else 0))
                    value = part if value is None else jnp.where(lane >= y, part, value)
                box[pl.ds(8 * p * NX + SLABS * chip + slab, 8, stride=NX), :] = value
        return carry

    lax.fori_loop(0, 8, one, 0)


def close_rows(box, chunk, send_ref):
    cuts = pieces()
    lane = lanes((8, 128))

    def one(chip, carry):
        fields = [[box[pl.ds(8 * p * NX + SLABS * chip + slab, 8, stride=NX), :] for slab in range(SLABS)] for p in range(3)]
        for source in range(4):
            tail_value = None
            for p in range(3):
                value = None
                for s, tail, first, slab, y, _ in cuts:
                    if s != source:
                        continue
                    if tail:
                        place = first + TAIL * p
                        part = turn(fields[p][slab], place - y)
                        tail_value = part if tail_value is None else jnp.where(lane >= place, part, tail_value)
                    else:
                        part = turn(fields[p][slab], first - y)
                        value = part if value is None else jnp.where(lane >= first, part, value)
                send_ref[chunk, 4 * chip + source, p] = value
            send_ref[chunk, 4 * chip + source, 3] = tail_value
        return carry

    lax.fori_loop(0, 8, one, 0)


def screen_planes(owner, chunk, x_ref, y_ref, box, work, gain):
    flags = [jnp.where(tile_of(owner, chunk, p) == 0, 1.0, 0.0).astype(F32) for p in range(3)]

    def along_x(real, imag):
        wide = jnp.concatenate([real, imag], axis=1)
        wide = jnp.concatenate([wide, jnp.zeros((8, 256), F32)], axis=0)
        high, low = split(wide)
        both = mm(x_ref[...], jnp.concatenate([high, high, low], axis=0))
        return both[:NX, :128], both[:NX, 128:], both[NX:, :128], both[NX:, 128:]

    def along_y(value, k):
        high, low = split(value)
        return mm(high, y_ref[k]) + mm(low, y_ref[k]) + mm(high, y_ref[k + 1])

    for plane in range(PLANES):
        if plane == 12:
            real = sum(flags[p] * box[pl.ds((8 * p + 4) * NX, NX), :] for p in range(3))
            imag = jnp.zeros_like(real)
        else:
            p, i = divmod(plane, 4)
            real = box[pl.ds((8 * p + i) * NX, NX), :]
            imag = box[pl.ds((8 * p + 4 + i) * NX, NX), :]
            if i == 0:
                imag = imag * (1.0 - flags[p])
        cr, ci, sr, si = along_x(real, imag)
        work[pl.ds(plane * NX, NX), :] = jnp.concatenate([cr + si, ci - sr], axis=1)
    weight = gain[pl.ds(chunk * PLANES * NX, PLANES * NX), :]
    value = along_y(work[...], 0) * jnp.concatenate([weight, weight], axis=1)
    work[...] = along_y(value, 2)
    extra = None
    for plane in reversed(range(PLANES)):
        rows = work[pl.ds(plane * NX, NX), :]
        cr, ci, sr, si = along_x(rows[:, :128], rows[:, 128:])
        real, imag = cr - si, ci + sr
        if plane == 12:
            extra = real
        else:
            p, i = divmod(plane, 4)
            if i == 0:
                imag = imag * (1.0 - flags[p]) + extra * flags[p]
            box[pl.ds((8 * p + i) * NX, NX), :] = real
            box[pl.ds((8 * p + 4 + i) * NX, NX), :] = imag


def intersect(total, bands_ref, partial_ref):
    lines = []
    for b in range(BLK):
        product = (bands_ref[b] * total).reshape(36, 8, 128)
        line = jnp.sum(jnp.sum(product, axis=0), axis=0, keepdims=True)
        line = line + turn(line, 64)
        lines.append(line + turn(line, 32))
    quarter = lanes((1, 128)) // 32
    row = lines[0]
    for b in range(1, BLK):
        row = jnp.where(quarter == b, lines[b], row)
    partial_ref[...] = row * SPACING**3


STEPS = [((1, -2, 3, -1, 2, -3, 4)[k % 7], (0, 2, 1, 3)[k % 4]) for k in range(28)] + [(0, turned) for turned in (2, 1, 3)]


class Ring:
    def __init__(self, me, source, target, send_sem, recv_sem):
        self.source, self.target = source, target
        self.send_sem, self.recv_sem = send_sem, recv_sem
        self.me = me
        self.places = [lax.rem(me // 4 + k, 8) for k in range(8)]
        self.parts = [lax.rem(lax.rem(me, 4) + k, 4) for k in range(4)]

    def device(self, far, turned):
        return 4 * self.places[far % 8] + self.parts[turned % 4]

    def copy(self, source, target, peer, k):
        return pltpu.make_async_remote_copy(
            src_ref=source, dst_ref=target, send_sem=self.send_sem.at[k], recv_sem=self.recv_sem.at[k],
            device_id={"fft": peer}, device_id_type=MESH,
        )

    def start(self, chunk, first, count, k, low=0, high=FFT - 1):
        rows = pl.ds(first, count)
        for far, turned in STEPS[low:high]:
            peer = self.device(far, turned)
            self.copy(self.source.at[chunk, peer, rows], self.target.at[chunk, self.me, rows], peer, k).start()
        if high < FFT - 1:
            return
        self.target[chunk, self.me, first:first + count] = self.source[chunk, self.me, first:first + count]

    def wait_recv(self, chunk, first, count, k):
        whole = self.target.at[chunk, pl.ds(0, FFT - 1), pl.ds(first, count)]
        self.copy(whole, whole, self.device(1, 0), k).wait_recv()

    def wait_send(self, chunk, first, count, k):
        whole = self.source.at[chunk, pl.ds(0, FFT - 1), pl.ds(first, count)]
        self.copy(whole, whole, self.device(1, 0), k).wait_send()


def whole_kernel(
    picked_ref, shells_ref, orbitals_far, forward_far, inverse_far, xy_far, x_far, y_far,
    total_ref, result_ref,
    orbitals_ref, forward_ref, inverse_ref, xy_ref, x_ref, y_ref, fetch_sem,
    own, order, upper, lower, up, down, above, below, mine, sent, got, back, returned, tails, box, work, gain, pad,
    partial, ring_slots, near, near_slots,
    there_send, there_recv, home_send, home_recv, band_send, band_recv, ring_send, ring_recv, near_send, near_recv,
):
    me = lax.axis_index("fft")
    group = lax.axis_index("band")
    count = lax.axis_size("band")
    above_me, below_me = lax.rem(group + 1, count), lax.rem(group + count - 1, count)

    barrier = pltpu.get_barrier_semaphore()
    for peer in (above_me, below_me):
        pl.semaphore_signal(barrier, inc=1, device_id={"band": peer}, device_id_type=MESH)
    there = Ring(me, sent, got, there_send, there_recv)
    home = Ring(me, back, returned, home_send, home_recv)
    for far, turned in STEPS:
        peer = there.device(far, turned)
        pl.semaphore_signal(barrier, inc=1, device_id={"fft": peer}, device_id_type=MESH)

    def to_band(source, target, peer, k):
        return pltpu.make_async_remote_copy(
            src_ref=source, dst_ref=target, send_sem=band_send.at[k], recv_sem=band_recv.at[k],
            device_id={"band": peer}, device_id_type=MESH,
        )

    chosen_up = to_band(order.at[0], lower, above_me, 0)
    chosen_down = to_band(order.at[0], upper, below_me, 1)
    sum_down = to_band(down, above, below_me, 2)
    main, tail = pl.ds(0, NZ), pl.ds(NZ, NZ // 3)
    sum_up_main = to_band(up.at[main], below.at[main], above_me, 3)
    sum_up_tail = to_band(up.at[tail], below.at[tail], above_me, 4)

    fetches = [
        pltpu.make_async_copy(far, ref, fetch_sem.at[k])
        for k, (far, ref) in enumerate(
            [
                (orbitals_far, orbitals_ref), (xy_far, xy_ref), (forward_far, forward_ref),
                (x_far, x_ref), (y_far, y_ref), (inverse_far, inverse_ref),
            ]
        )
    ]
    for one in fetches:
        one.start()
    picked = picked_ref[0]
    fetches[0].wait()
    pad[...] = jnp.zeros_like(pad)
    order[0] = turned_band(orbitals_ref[:, picked, :], pad)
    pl.semaphore_wait(barrier, FFT + 1)
    chosen_up.start()
    order_bands(picked, orbitals_ref, own, order, pad)

    def gain_step(plane, carry):
        gain_of(me, plane, shells_ref, xy_ref, gain)
        return carry

    for one in fetches[1:]:
        one.wait()
    lax.fori_loop(0, 3, gain_step, 0)
    chosen_down.start()
    lax.fori_loop(3, 10, gain_step, 0)
    tails[pl.ds(NZ * FIELDS, 24), :] = jnp.zeros((24, 128), F32)
    put_rows(sent, NZ * FIELDS + 256, jnp.zeros((24, 128), F32))

    chosen_up.wait_recv()
    for f in range(3):
        spectrum_of(f, order, upper, lower, forward_ref, sent, tails)
    there.start(0, 0, 2, 0)
    chosen_down.wait_recv()
    spectrum_of(3, order, upper, lower, forward_ref, sent, tails)
    close_tails(0, sent, tails)
    there.start(0, 2, 2, 0)
    for f in range(4, FIELDS):
        spectrum_of(f, order, upper, lower, forward_ref, sent, tails)
    close_tails(1, sent, tails)
    there.start(1, 0, 4, 1)
    lax.fori_loop(10, 2 * PLANES, gain_step, 0)

    for chunk in range(2):
        there.wait_recv(chunk, 0, 4, chunk)
        open_rows(got, chunk, box)
        screen_planes(me, chunk, x_ref, y_ref, box, work, gain)
        close_rows(box, chunk, back)
        if chunk == 0:
            home.start(0, 0, 4, 0)
        else:
            home.start(1, 0, 3, 1, 0, 20)

    home.wait_recv(0, 0, 4, 0)
    open_tails(0, returned, tails)
    total = None
    for f in range(3):
        field = pack_field(z_transform(inverse_ref, jnp.concatenate([main_of(f, returned), tail_of(f, tails)], axis=1)))
        term = field * order[visitor_of(f)[1]]
        total = term if total is None else total + term
    down[...] = total
    sum_down.start()
    home.start(1, 0, 3, 1, 20)
    home.start(1, 3, 1, 2)

    def up_part(rows, fields):
        total = None
        for f, field in fields:
            if f == 3:
                mine[rows, :] = field * upper[rows, :]
            term = field * order[visitor_of(f)[1], rows, :]
            total = term if total is None else total + term
        up[rows, :] = total

    home.wait_recv(1, 0, 3, 1)
    up_part(main, [(f, z_transform(inverse_ref, main_of(f, returned))) for f in range(3, FIELDS)])
    sum_up_main.start()
    home.wait_recv(1, 3, 1, 2)
    open_tails(1, returned, tails)
    up_part(tail, [(f, pack_thirds(z_transform(inverse_ref, tail_of(f, tails)))) for f in range(3, FIELDS)])
    sum_up_tail.start()
    sum_down.wait_recv()
    mine[...] += above[...]
    sum_up_main.wait_recv()
    sum_up_tail.wait_recv()
    total = mine[...] + below[...]
    total_ref[...] = total
    intersect(total, own, partial)

    place, part = me // 4, lax.rem(me, 4)

    def row_to(source, target, peer, send_sem, recv_sem):
        return pltpu.make_async_remote_copy(
            src_ref=source, dst_ref=target, send_sem=send_sem, recv_sem=recv_sem,
            device_id={"fft": peer}, device_id_type=MESH,
        )

    ring = [
        row_to(partial, ring_slots.at[k], 4 * lax.rem(place + k, 8) + part, ring_send.at[k], ring_recv.at[k])
        for k in range(1, 8)
    ]
    for one in ring:
        one.start()
    row = partial[...]
    for k, one in enumerate(ring):
        one.wait()
        row = row + ring_slots[k + 1]
    near[...] = row
    beside = [
        row_to(near, near_slots.at[k], 4 * place + lax.rem(part + k, 4), near_send.at[k], near_recv.at[k])
        for k in range(1, 4)
    ]
    for one in beside:
        one.start()
    for k, one in enumerate(beside):
        one.wait()
        row = row + near_slots[k + 1]
    result_ref[...] = row

    there.wait_send(0, 0, 4, 0)
    there.wait_send(1, 0, 4, 1)
    home.wait_send(0, 0, 4, 0)
    home.wait_send(1, 0, 3, 1)
    home.wait_send(1, 3, 1, 2)
    for one in (chosen_up, chosen_down, sum_down, sum_up_main, sum_up_tail):
        one.wait_send()


def last_kernel(total_ref, row_ref, potential_ref, result_ref, pad_ref):
    pad_ref[...] = jnp.zeros_like(pad_ref)
    pad_ref[:NZ, :] = unpack_field(total_ref[...])
    potential_ref[:, 0, :] = jnp.transpose(pad_ref[...])[:ROWS, :NZ]
    row = row_ref[...]
    lane = lanes((1, BLK))
    result = jnp.zeros((1, BLK), F32)
    for b in range(BLK):
        mine = lanes((1, 128)) // 32 == b
        result = jnp.where(lane == b, jnp.sum(jnp.where(mine, row, 0.0), axis=1, keepdims=True), result)
    result_ref[...] = result


def vm():
    return pl.BlockSpec(memory_space=pltpu.VMEM)


def sm():
    return pl.BlockSpec(memory_space=pltpu.SMEM)


def params(**extra):
    return pltpu.CompilerParams(vmem_limit_bytes=VMEM_LIMIT, **extra)


def shape(*dims):
    return jax.ShapeDtypeStruct(dims, F32)


def body(orbitals, picked, shells):
    forward, inverse = z_stacks()
    along_x, along_y = x_table(), y_tables()
    exchange = pltpu.VMEM((2, FFT, 4, 8, 128), F32)
    field = pltpu.VMEM((288, 128), F32)
    bands = pltpu.VMEM((BLK, 288, 128), F32)
    line = pltpu.VMEM((1, 128), F32)
    dma = pltpu.SemaphoreType.DMA
    total, row = pl.pallas_call(
        whole_kernel,
        out_shape=(shape(288, 128), shape(1, 128)),
        in_specs=[sm(), sm()] + [pl.BlockSpec(memory_space=pltpu.HBM)] * 6,
        out_specs=(vm(), vm()),
        scratch_shapes=[
            pltpu.VMEM((ROWS, BLK, NZ), F32),
            pltpu.VMEM(forward.shape, BF16),
            pltpu.VMEM(inverse.shape, BF16),
            pltpu.VMEM((NX, 128), F32),
            pltpu.VMEM(along_x.shape, BF16),
            pltpu.VMEM(along_y.shape, BF16),
            dma((6,)),
            bands,
            bands,
        ]
        + [field] * 7
        + [exchange] * 4
        + [
            pltpu.VMEM((1536, 128), F32),
            pltpu.VMEM((24 * NX, 128), F32),
            pltpu.VMEM((PLANES * NX, 256), F32),
            pltpu.VMEM((2 * PLANES * NX, 128), F32),
            pltpu.VMEM((256, 256), F32),
            line,
            pltpu.VMEM((8, 1, 128), F32),
            line,
            pltpu.VMEM((4, 1, 128), F32),
        ]
        + [dma((2,))] * 2
        + [dma((3,))] * 2
        + [dma((5,))] * 2
        + [dma((8,))] * 2
        + [dma((4,))] * 2,
        compiler_params=params(collective_id=0, has_side_effects=True),
    )(
        picked, shells, jnp.transpose(orbitals, (1, 0, 2)), jnp.asarray(forward), jnp.asarray(inverse),
        jnp.asarray(xy_square()), jnp.asarray(along_x), jnp.asarray(along_y),
    )
    potentials, result = pl.pallas_call(
        last_kernel,
        out_shape=(shape(ROWS, 1, NZ), shape(1, BLK)),
        in_specs=[vm()] * 2,
        out_specs=(vm(), vm()),
        scratch_shapes=[pltpu.VMEM((256, 256), F32)],
        compiler_params=params(),
    )(total, row)
    return jnp.transpose(potentials, (1, 0, 2)), jnp.transpose(result)


def solution(mesh):
    return jax.shard_map(
        body,
        mesh=mesh,
        in_specs=(P("band", "fft", None), P("band"), P()),
        out_specs=(P("band", "fft", None), P("band", None)),
        check_vma=False,
    )
```

```python
import math

import jax
import jax.numpy as jnp
import numpy as np
from jax import lax
from jax.experimental import pallas as pl
from jax.experimental.pallas import tpu as pltpu
from jax.sharding import PartitionSpec as P

NX = 72
NY = 72
NZ = 216
BLK = 4
NSHELL = 64
FIELDS = 7
FFT = 32
ROWS = 162
MAIN = 128
TAIL = ROWS - MAIN
SLABS = 9
PLANES = 13

SPACING = 0.2
SCREENING = 0.106
FRACTION = 0.25
SPAN = math.lcm(NX, NY, NZ)
QTOP = (SPAN // NX) ** 2 * (NX // 2) ** 2 + (SPAN // NY) ** 2 * (NY // 2) ** 2 + (SPAN // NZ) ** 2 * (NZ // 2) ** 2
MESH = pl.DeviceIdType.MESH
F32 = jnp.float32
BF16 = jnp.bfloat16
VMEM_LIMIT = 60 * 1024 * 1024


def halves(table):
    table = np.asarray(table, np.float32)
    high = table.astype(jnp.bfloat16)
    low = (table - high.astype(np.float32)).astype(jnp.bfloat16)
    return high, low


def z_tables():
    freq, is_sin = np.zeros(NZ, np.int64), np.zeros(NZ, bool)
    for t in range(NZ // 8):
        for i in range(4):
            freq[8 * t + i] = 4 * t + i
            freq[8 * t + 4 + i] = 4 * t + i
            is_sin[8 * t + 4 + i] = True
    freq[4], is_sin[4] = NZ // 2, False
    angle = 2 * np.pi * (freq[:, None] * np.arange(NZ)[None, :] % NZ) / NZ
    forward = np.where(is_sin[:, None], -np.sin(angle), np.cos(angle))
    weight = np.where((freq == 0) | (freq == NZ // 2), 1.0, 2.0) / (NX * NY * NZ)
    inverse = (-FRACTION * weight[:, None] * forward).T
    return forward, inverse


def z_stacks():
    forward, inverse = z_tables()
    pad = np.zeros((8, NZ), jnp.bfloat16)

    def stack(table):
        high, low = halves(table)
        return np.concatenate([high, pad, low, pad], axis=0)

    return stack(forward), stack(inverse)


def xy_angle():
    index = np.arange(NX)
    return 2 * np.pi * (index[:, None] * index[None, :] % NX) / NX


def x_table():
    table = np.concatenate([np.cos(xy_angle()), np.sin(xy_angle())], axis=0)
    high, low = halves(table)
    pad = np.zeros((2 * NX, 8), high.dtype)
    return np.concatenate([high, pad, low, pad, high, pad], axis=1)


def y_tables():
    cosine, sine = np.cos(xy_angle()), np.sin(xy_angle())
    forward = np.zeros((256, 256))
    forward[:NY, :NY] = cosine
    forward[128:128 + NY, 128:128 + NY] = cosine
    forward[:NY, 128:128 + NY] = -sine
    forward[128:128 + NY, :NY] = sine
    fh, fl = halves(forward)
    return np.stack([fh, fl, fh.T, fl.T])


def xy_square():
    index = np.arange(NX)
    signed = np.where(index > NX // 2, index - NX, index)
    square = np.zeros((NX, 128), np.float32)
    square[:, :NY] = 9 * (signed[:, None] ** 2 + signed[None, :] ** 2)
    return square


def split(value):
    high = value.astype(BF16)
    return high, (value - high.astype(F32)).astype(BF16)


def mm(left, right):
    return lax.dot_general(left, right, (((1,), (0,)), ((), ())), preferred_element_type=F32)


def lanes(shape):
    return lax.broadcasted_iota(jnp.int32, shape, len(shape) - 1)


def turn(value, shift):
    shift = shift % 128
    return value if shift == 0 else pltpu.roll(value, shift, 1)


def pack_tail(parts):
    lane = lanes(parts[0].shape)
    upper = jnp.where(lane < 2 * TAIL, turn(parts[1], TAIL), turn(parts[2], 2 * TAIL))
    return jnp.where(lane < TAIL, parts[0], upper)


def pack_thirds(tail):
    third = NZ // 3
    return pack_tail([tail[third * g:third * (g + 1)] for g in range(3)])


def pack_field(wide):
    return jnp.concatenate([wide[:, :MAIN], pack_thirds(wide[:, MAIN:])], axis=0)


def unpack_field(packed):
    tail = packed[NZ:]
    tails = jnp.concatenate([turn(tail, -TAIL * g) for g in range(3)], axis=0)
    return jnp.concatenate([packed[:NZ], tails], axis=1)


def z_transform(table_ref, wide):
    high, low = split(wide)
    both = mm(table_ref[...], high)
    return both[:NZ] + both[NZ + 8:2 * NZ + 8] + mm(table_ref[:NZ + 8], low)[:NZ]


def turned_band(band, pad_ref):
    pad_ref[:ROWS, :NZ] = band
    return pack_field(jnp.transpose(pad_ref[...])[:NZ])


def order_bands(picked, orbitals_ref, own_ref, order_ref, pad_ref):
    for b in range(BLK):
        own_ref[b] = turned_band(orbitals_ref[:, b, :], pad_ref)
    for j in range(1, BLK):
        order_ref[j] = jnp.where(picked >= j, own_ref[j - 1], own_ref[j])


def visitor_of(f):
    return (True, f + 1) if f < 3 else (False, f - 3)


def cuts_of(f):
    result = []
    for chunk in range(2):
        low, high = max(NZ * f, 768 * chunk), min(NZ * (f + 1), 768 * (chunk + 1))
        if low < high:
            result.append((low, high - low, low + 256 * chunk))
    return result


def runs(row, rows):
    tile, count = row // 8, rows // 8
    done = 0
    while done < count:
        place, peer = divmod(tile + done, FFT)
        take = min(count - done, FFT - peer)
        yield place // 4, place % 4, peer, take, done
        done += take


def put_rows(buffer, row, value):
    tiles = value.reshape(value.shape[0] // 8, 8, 128)
    for chunk, part, peer, take, done in runs(row, value.shape[0]):
        buffer[chunk, peer:peer + take, part] = tiles[done:done + take]


def get_rows(buffer, row, rows):
    parts = [buffer[chunk, peer:peer + take, part].reshape(8 * take, 128) for chunk, part, peer, take, _ in runs(row, rows)]
    return parts[0] if len(parts) == 1 else jnp.concatenate(parts, axis=0)


def spectrum_of(f, order_ref, upper_ref, lower_ref, table_ref, buffer, tail_ref):
    low_side, j = visitor_of(f)
    density = (lower_ref if low_side else upper_ref)[...] * order_ref[j]
    spectrum = z_transform(table_ref, unpack_field(density))
    for low, count, place in cuts_of(f):
        first = low - NZ * f
        put_rows(buffer, place, spectrum[first:first + count, :MAIN])
        tail_ref[pl.ds(low, count), :] = spectrum[first:first + count, MAIN:]


def close_tails(chunk, buffer, tail_ref):
    parts = [tail_ref[pl.ds(768 * chunk + 256 * p, 256), :] for p in range(3)]
    put_rows(buffer, 1024 * chunk + 768, pack_tail(parts))


def open_tails(chunk, buffer, tail_ref):
    tails = get_rows(buffer, 1024 * chunk + 768, 256)
    for p in range(3):
        tail_ref[pl.ds(768 * chunk + 256 * p, 256), :] = turn(tails, -TAIL * p)


def main_of(f, buffer):
    mains = [get_rows(buffer, place, count) for _, count, place in cuts_of(f)]
    return mains[0] if len(mains) == 1 else jnp.concatenate(mains, axis=0)


def tail_of(f, tail_ref):
    return tail_ref[pl.ds(NZ * f, NZ), :]


def pieces():
    result = []
    row = 0
    while row < 4 * ROWS:
        source, j = divmod(row, ROWS)
        slab, y = divmod(row, NY)
        stop = min((source + 1) * ROWS, (slab + 1) * NY)
        if j < MAIN:
            stop = min(stop, source * ROWS + MAIN)
        result.append((source, j >= MAIN, j if j < MAIN else j - MAIN, slab, y, stop - row))
        row = stop
    return result


def tile_of(owner, chunk, p):
    return lax.rem(96 * chunk + 32 * p + owner, NZ // 8)


def gain_of(owner, plane, shells_ref, xy_ref, gain):
    chunk, place = plane // PLANES, lax.rem(plane, PLANES)
    depth = jnp.where(place == PLANES - 1, NZ // 2, 4 * tile_of(owner, chunk, place // 4) + lax.rem(place, 4))
    square = xy_ref[...] + (depth * depth).astype(F32)
    total = jnp.full(square.shape, shells_ref[0].astype(F32), F32)
    for s in range(1, NSHELL):
        step = (shells_ref[s] - shells_ref[s - 1]).astype(F32)
        total = total + jnp.where(square >= float(-(-s * (QTOP + 1) // NSHELL)), step, 0.0)
    g_squared = (2.0 * math.pi / (SPACING * SPAN)) ** 2 * square
    safe = jnp.where(square == 0, 1.0, g_squared)
    value = 4.0 * math.pi / safe * (1.0 - jnp.exp(-safe / (4.0 * SCREENING**2)))
    gain[pl.ds(pl.multiple_of(plane * NX, 8), NX), :] = total * jnp.where(square == 0, math.pi / SCREENING**2, value)


def open_rows(got_ref, chunk, box):
    cuts = pieces()
    lane = lanes((8, 128))

    def one(chip, carry):
        for slab in range(SLABS):
            mine = [c for c in cuts if c[3] == slab]
            for p in range(3):
                value = None
                for source, tail, first, _, y, _ in mine:
                    part = got_ref[chunk, 4 * chip + source, 3 if tail else p]
                    part = turn(part, y - first - (TAIL * p if tail else 0))
                    value = part if value is None else jnp.where(lane >= y, part, value)
                box[pl.ds(8 * p * NX + SLABS * chip + slab, 8, stride=NX), :] = value
        return carry

    lax.fori_loop(0, 8, one, 0)


def close_rows(box, chunk, send_ref):
    cuts = pieces()
    lane = lanes((8, 128))

    def one(chip, carry):
        fields = [[box[pl.ds(8 * p * NX + SLABS * chip + slab, 8, stride=NX), :] for slab in range(SLABS)] for p in range(3)]
        for source in range(4):
            tail_value = None
            for p in range(3):
                value = None
                for s, tail, first, slab, y, _ in cuts:
                    if s != source:
                        continue
                    if tail:
                        place = first + TAIL * p
                        part = turn(fields[p][slab], place - y)
                        tail_value = part if tail_value is None else jnp.where(lane >= place, part, tail_value)
                    else:
                        part = turn(fields[p][slab], first - y)
                        value = part if value is None else jnp.where(lane >= first, part, value)
                send_ref[chunk, 4 * chip + source, p] = value
            send_ref[chunk, 4 * chip + source, 3] = tail_value
        return carry

    lax.fori_loop(0, 8, one, 0)


def screen_planes(owner, chunk, x_ref, y_ref, box, work, gain):
    flags = [jnp.where(tile_of(owner, chunk, p) == 0, 1.0, 0.0).astype(F32) for p in range(3)]

    def along_x(real, imag):
        wide = jnp.concatenate([real, imag], axis=1)
        wide = jnp.concatenate([wide, jnp.zeros((8, 256), F32)], axis=0)
        high, low = split(wide)
        both = mm(x_ref[...], jnp.concatenate([high, high, low], axis=0))
        return both[:NX, :128], both[:NX, 128:], both[NX:, :128], both[NX:, 128:]

    def along_y(value, k):
        high, low = split(value)
        return mm(high, y_ref[k]) + mm(low, y_ref[k]) + mm(high, y_ref[k + 1])

    for plane in range(PLANES):
        if plane == 12:
            real = sum(flags[p] * box[pl.ds((8 * p + 4) * NX, NX), :] for p in range(3))
            imag = jnp.zeros_like(real)
        else:
            p, i = divmod(plane, 4)
            real = box[pl.ds((8 * p + i) * NX, NX), :]
            imag = box[pl.ds((8 * p + 4 + i) * NX, NX), :]
            if i == 0:
                imag = imag * (1.0 - flags[p])
        cr, ci, sr, si = along_x(real, imag)
        work[pl.ds(plane * NX, NX), :] = jnp.concatenate([cr + si, ci - sr], axis=1)
    weight = gain[pl.ds(chunk * PLANES * NX, PLANES * NX), :]
    value = along_y(work[...], 0) * jnp.concatenate([weight, weight], axis=1)
    work[...] = along_y(value, 2)
    extra = None
    for plane in reversed(range(PLANES)):
        rows = work[pl.ds(plane * NX, NX), :]
        cr, ci, sr, si = along_x(rows[:, :128], rows[:, 128:])
        real, imag = cr - si, ci + sr
        if plane == 12:
            extra = real
        else:
            p, i = divmod(plane, 4)
            if i == 0:
                imag = imag * (1.0 - flags[p]) + extra * flags[p]
            box[pl.ds((8 * p + i) * NX, NX), :] = real
            box[pl.ds((8 * p + 4 + i) * NX, NX), :] = imag


def intersect(total, bands_ref, partial_ref):
    lines = []
    for b in range(BLK):
        product = (bands_ref[b] * total).reshape(36, 8, 128)
        line = jnp.sum(jnp.sum(product, axis=0), axis=0, keepdims=True)
        line = line + turn(line, 64)
        lines.append(line + turn(line, 32))
    quarter = lanes((1, 128)) // 32
    row = lines[0]
    for b in range(1, BLK):
        row = jnp.where(quarter == b, lines[b], row)
    partial_ref[...] = row * SPACING**3


STEPS = [((1, -2, 3, -1, 2, -3, 4)[k % 7], (0, 2, 1, 3)[k % 4]) for k in range(28)] + [(0, turned) for turned in (2, 1, 3)]


class Ring:
    def __init__(self, me, source, target, send_sem, recv_sem):
        self.source, self.target = source, target
        self.send_sem, self.recv_sem = send_sem, recv_sem
        self.me = me
        self.places = [lax.rem(me // 4 + k, 8) for k in range(8)]
        self.parts = [lax.rem(lax.rem(me, 4) + k, 4) for k in range(4)]

    def device(self, far, turned):
        return 4 * self.places[far % 8] + self.parts[turned % 4]

    def copy(self, source, target, peer, k):
        return pltpu.make_async_remote_copy(
            src_ref=source, dst_ref=target, send_sem=self.send_sem.at[k], recv_sem=self.recv_sem.at[k],
            device_id={"fft": peer}, device_id_type=MESH,
        )

    def start(self, chunk, first, count, k, low=0, high=FFT - 1):
        rows = pl.ds(first, count)
        for far, turned in STEPS[low:high]:
            peer = self.device(far, turned)
            self.copy(self.source.at[chunk, peer, rows], self.target.at[chunk, self.me, rows], peer, k).start()
        if high < FFT - 1:
            return
        self.target[chunk, self.me, first:first + count] = self.source[chunk, self.me, first:first + count]

    def wait_recv(self, chunk, first, count, k):
        whole = self.target.at[chunk, pl.ds(0, FFT - 1), pl.ds(first, count)]
        self.copy(whole, whole, self.device(1, 0), k).wait_recv()

    def wait_send(self, chunk, first, count, k):
        whole = self.source.at[chunk, pl.ds(0, FFT - 1), pl.ds(first, count)]
        self.copy(whole, whole, self.device(1, 0), k).wait_send()


def whole_kernel(
    picked_ref, shells_ref, orbitals_far, forward_far, inverse_far, xy_far, x_far, y_far,
    total_ref, result_ref,
    orbitals_ref, forward_ref, inverse_ref, xy_ref, x_ref, y_ref, fetch_sem,
    own, order, upper, lower, up, down, above, below, mine, sent, got, back, returned, tails, box, work, gain, pad,
    partial, ring_slots, near, near_slots,
    there_send, there_recv, home_send, home_recv, band_send, band_recv, ring_send, ring_recv, near_send, near_recv,
):
    me = lax.axis_index("fft")
    group = lax.axis_index("band")
    count = lax.axis_size("band")
    above_me, below_me = lax.rem(group + 1, count), lax.rem(group + count - 1, count)

    barrier = pltpu.get_barrier_semaphore()
    for peer in (above_me, below_me):
        pl.semaphore_signal(barrier, inc=1, device_id={"band": peer}, device_id_type=MESH)
    there = Ring(me, sent, got, there_send, there_recv)
    home = Ring(me, back, returned, home_send, home_recv)
    for far, turned in STEPS:
        peer = there.device(far, turned)
        pl.semaphore_signal(barrier, inc=1, device_id={"fft": peer}, device_id_type=MESH)

    def to_band(source, target, peer, k):
        return pltpu.make_async_remote_copy(
            src_ref=source, dst_ref=target, send_sem=band_send.at[k], recv_sem=band_recv.at[k],
            device_id={"band": peer}, device_id_type=MESH,
        )

    chosen_up = to_band(order.at[0], lower, above_me, 0)
    chosen_down = to_band(order.at[0], upper, below_me, 1)
    sum_down = to_band(down, above, below_me, 2)
    main, tail = pl.ds(0, NZ), pl.ds(NZ, NZ // 3)
    sum_up_main = to_band(up.at[main], below.at[main], above_me, 3)
    sum_up_tail = to_band(up.at[tail], below.at[tail], above_me, 4)

    fetches = [
        pltpu.make_async_copy(far, ref, fetch_sem.at[k])
        for k, (far, ref) in enumerate(
            [
                (orbitals_far, orbitals_ref), (xy_far, xy_ref), (forward_far, forward_ref),
                (x_far, x_ref), (y_far, y_ref), (inverse_far, inverse_ref),
            ]
        )
    ]
    for one in fetches:
        one.start()
    picked = picked_ref[0]
    fetches[0].wait()
    pad[...] = jnp.zeros_like(pad)
    order[0] = turned_band(orbitals_ref[:, picked, :], pad)
    pl.semaphore_wait(barrier, FFT + 1)
    chosen_up.start()
    order_bands(picked, orbitals_ref, own, order, pad)

    def gain_step(plane, carry):
        gain_of(me, plane, shells_ref, xy_ref, gain)
        return carry

    chosen_down.start()
    for one in fetches[1:]:
        one.wait()
    tails[pl.ds(NZ * FIELDS, 24), :] = jnp.zeros((24, 128), F32)
    put_rows(sent, NZ * FIELDS + 256, jnp.zeros((24, 128), F32))

    chosen_up.wait_recv()
    for f in range(3):
        spectrum_of(f, order, upper, lower, forward_ref, sent, tails)
    there.start(0, 0, 2, 0)
    chosen_down.wait_recv()
    spectrum_of(3, order, upper, lower, forward_ref, sent, tails)
    close_tails(0, sent, tails)
    there.start(0, 2, 2, 0)
    for f in range(4, FIELDS):
        spectrum_of(f, order, upper, lower, forward_ref, sent, tails)
    close_tails(1, sent, tails)
    there.start(1, 0, 4, 1)
    lax.fori_loop(0, 2 * PLANES, gain_step, 0)

    for chunk in range(2):
        there.wait_recv(chunk, 0, 4, chunk)
        open_rows(got, chunk, box)
        screen_planes(me, chunk, x_ref, y_ref, box, work, gain)
        close_rows(box, chunk, back)
        if chunk == 0:
            home.start(0, 0, 4, 0)
        else:
            home.start(1, 0, 3, 1, 0, 20)

    home.wait_recv(0, 0, 4, 0)
    open_tails(0, returned, tails)
    total = None
    for f in range(3):
        field = pack_field(z_transform(inverse_ref, jnp.concatenate([main_of(f, returned), tail_of(f, tails)], axis=1)))
        term = field * order[visitor_of(f)[1]]
        total = term if total is None else total + term
    down[...] = total
    sum_down.start()
    home.start(1, 0, 3, 1, 20)
    home.start(1, 3, 1, 2)

    def up_part(rows, fields):
        total = None
        for f, field in fields:
            if f == 3:
                mine[rows, :] = field * upper[rows, :]
            term = field * order[visitor_of(f)[1], rows, :]
            total = term if total is None else total + term
        up[rows, :] = total

    home.wait_recv(1, 0, 3, 1)
    up_part(main, [(f, z_transform(inverse_ref, main_of(f, returned))) for f in range(3, FIELDS)])
    sum_up_main.start()
    home.wait_recv(1, 3, 1, 2)
    open_tails(1, returned, tails)
    up_part(tail, [(f, pack_thirds(z_transform(inverse_ref, tail_of(f, tails)))) for f in range(3, FIELDS)])
    sum_up_tail.start()
    sum_down.wait_recv()
    mine[...] += above[...]
    sum_up_main.wait_recv()
    sum_up_tail.wait_recv()
    total = mine[...] + below[...]
    total_ref[...] = total
    intersect(total, own, partial)

    place, part = me // 4, lax.rem(me, 4)

    def row_to(source, target, peer, send_sem, recv_sem):
        return pltpu.make_async_remote_copy(
            src_ref=source, dst_ref=target, send_sem=send_sem, recv_sem=recv_sem,
            device_id={"fft": peer}, device_id_type=MESH,
        )

    ring = [
        row_to(partial, ring_slots.at[k], 4 * lax.rem(place + k, 8) + part, ring_send.at[k], ring_recv.at[k])
        for k in range(1, 8)
    ]
    for one in ring:
        one.start()
    row = partial[...]
    for k, one in enumerate(ring):
        one.wait()
        row = row + ring_slots[k + 1]
    near[...] = row
    beside = [
        row_to(near, near_slots.at[k], 4 * place + lax.rem(part + k, 4), near_send.at[k], near_recv.at[k])
        for k in range(1, 4)
    ]
    for one in beside:
        one.start()
    for k, one in enumerate(beside):
        one.wait()
        row = row + near_slots[k + 1]
    result_ref[...] = row

    there.wait_send(0, 0, 4, 0)
    there.wait_send(1, 0, 4, 1)
    home.wait_send(0, 0, 4, 0)
    home.wait_send(1, 0, 3, 1)
    home.wait_send(1, 3, 1, 2)
    for one in (chosen_up, chosen_down, sum_down, sum_up_main, sum_up_tail):
        one.wait_send()


def last_kernel(total_ref, row_ref, potential_ref, result_ref, pad_ref):
    pad_ref[...] = jnp.zeros_like(pad_ref)
    pad_ref[:NZ, :] = unpack_field(total_ref[...])
    potential_ref[:, 0, :] = jnp.transpose(pad_ref[...])[:ROWS, :NZ]
    row = row_ref[...]
    lane = lanes((1, BLK))
    result = jnp.zeros((1, BLK), F32)
    for b in range(BLK):
        mine = lanes((1, 128)) // 32 == b
        result = jnp.where(lane == b, jnp.sum(jnp.where(mine, row, 0.0), axis=1, keepdims=True), result)
    result_ref[...] = result


def vm():
    return pl.BlockSpec(memory_space=pltpu.VMEM)


def sm():
    return pl.BlockSpec(memory_space=pltpu.SMEM)


def params(**extra):
    return pltpu.CompilerParams(vmem_limit_bytes=VMEM_LIMIT, **extra)


def shape(*dims):
    return jax.ShapeDtypeStruct(dims, F32)


def body(orbitals, picked, shells):
    forward, inverse = z_stacks()
    along_x, along_y = x_table(), y_tables()
    exchange = pltpu.VMEM((2, FFT, 4, 8, 128), F32)
    field = pltpu.VMEM((288, 128), F32)
    bands = pltpu.VMEM((BLK, 288, 128), F32)
    line = pltpu.VMEM((1, 128), F32)
    dma = pltpu.SemaphoreType.DMA
    total, row = pl.pallas_call(
        whole_kernel,
        out_shape=(shape(288, 128), shape(1, 128)),
        in_specs=[sm(), sm()] + [pl.BlockSpec(memory_space=pltpu.HBM)] * 6,
        out_specs=(vm(), vm()),
        scratch_shapes=[
            pltpu.VMEM((ROWS, BLK, NZ), F32),
            pltpu.VMEM(forward.shape, BF16),
            pltpu.VMEM(inverse.shape, BF16),
            pltpu.VMEM((NX, 128), F32),
            pltpu.VMEM(along_x.shape, BF16),
            pltpu.VMEM(along_y.shape, BF16),
            dma((6,)),
            bands,
            bands,
        ]
        + [field] * 7
        + [exchange] * 4
        + [
            pltpu.VMEM((1536, 128), F32),
            pltpu.VMEM((24 * NX, 128), F32),
            pltpu.VMEM((PLANES * NX, 256), F32),
            pltpu.VMEM((2 * PLANES * NX, 128), F32),
            pltpu.VMEM((256, 256), F32),
            line,
            pltpu.VMEM((8, 1, 128), F32),
            line,
            pltpu.VMEM((4, 1, 128), F32),
        ]
        + [dma((2,))] * 2
        + [dma((3,))] * 2
        + [dma((5,))] * 2
        + [dma((8,))] * 2
        + [dma((4,))] * 2,
        compiler_params=params(collective_id=0, has_side_effects=True),
    )(
        picked, shells, jnp.transpose(orbitals, (1, 0, 2)), jnp.asarray(forward), jnp.asarray(inverse),
        jnp.asarray(xy_square()), jnp.asarray(along_x), jnp.asarray(along_y),
    )
    potentials, result = pl.pallas_call(
        last_kernel,
        out_shape=(shape(ROWS, 1, NZ), shape(1, BLK)),
        in_specs=[vm()] * 2,
        out_specs=(vm(), vm()),
        scratch_shapes=[pltpu.VMEM((256, 256), F32)],
        compiler_params=params(),
    )(total, row)
    return jnp.transpose(potentials, (1, 0, 2)), jnp.transpose(result)


def solution(mesh):
    return jax.shard_map(
        body,
        mesh=mesh,
        in_specs=(P("band", "fft", None), P("band"), P()),
        out_specs=(P("band", "fft", None), P("band", None)),
        check_vma=False,
    )
```

```python
import math

import jax
import jax.numpy as jnp
import numpy as np
from jax import lax
from jax.experimental import pallas as pl
from jax.experimental.pallas import tpu as pltpu
from jax.sharding import PartitionSpec as P

NX = 72
NY = 72
NZ = 216
BLK = 4
NSHELL = 64
FIELDS = 7
FFT = 32
ROWS = 162
MAIN = 128
TAIL = ROWS - MAIN
SLABS = 9
PLANES = 13

SPACING = 0.2
SCREENING = 0.106
FRACTION = 0.25
SPAN = math.lcm(NX, NY, NZ)
QTOP = (SPAN // NX) ** 2 * (NX // 2) ** 2 + (SPAN // NY) ** 2 * (NY // 2) ** 2 + (SPAN // NZ) ** 2 * (NZ // 2) ** 2
MESH = pl.DeviceIdType.MESH
F32 = jnp.float32
BF16 = jnp.bfloat16
VMEM_LIMIT = 60 * 1024 * 1024


def halves(table):
    table = np.asarray(table, np.float32)
    high = table.astype(jnp.bfloat16)
    low = (table - high.astype(np.float32)).astype(jnp.bfloat16)
    return high, low


def z_tables():
    freq, is_sin = np.zeros(NZ, np.int64), np.zeros(NZ, bool)
    for t in range(NZ // 8):
        for i in range(4):
            freq[8 * t + i] = 4 * t + i
            freq[8 * t + 4 + i] = 4 * t + i
            is_sin[8 * t + 4 + i] = True
    freq[4], is_sin[4] = NZ // 2, False
    angle = 2 * np.pi * (freq[:, None] * np.arange(NZ)[None, :] % NZ) / NZ
    forward = np.where(is_sin[:, None], -np.sin(angle), np.cos(angle))
    weight = np.where((freq == 0) | (freq == NZ // 2), 1.0, 2.0) / (NX * NY * NZ)
    inverse = (-FRACTION * weight[:, None] * forward).T
    return forward, inverse


def z_stacks():
    forward, inverse = z_tables()
    pad = np.zeros((8, NZ), jnp.bfloat16)

    def stack(table):
        high, low = halves(table)
        return np.concatenate([high, pad, low, pad], axis=0)

    return stack(forward), stack(inverse)


def xy_angle():
    index = np.arange(NX)
    return 2 * np.pi * (index[:, None] * index[None, :] % NX) / NX


def x_table():
    table = np.concatenate([np.cos(xy_angle()), np.sin(xy_angle())], axis=0)
    high, low = halves(table)
    pad = np.zeros((2 * NX, 8), high.dtype)
    return np.concatenate([high, pad, low, pad, high, pad], axis=1)


def y_tables():
    cosine, sine = np.cos(xy_angle()), np.sin(xy_angle())
    forward = np.zeros((256, 256))
    forward[:NY, :NY] = cosine
    forward[128:128 + NY, 128:128 + NY] = cosine
    forward[:NY, 128:128 + NY] = -sine
    forward[128:128 + NY, :NY] = sine
    fh, fl = halves(forward)
    return np.stack([fh, fl, fh.T, fl.T])


def xy_square():
    index = np.arange(NX)
    signed = np.where(index > NX // 2, index - NX, index)
    square = np.zeros((NX, 128), np.float32)
    square[:, :NY] = 9 * (signed[:, None] ** 2 + signed[None, :] ** 2)
    return square


def split(value):
    high = value.astype(BF16)
    return high, (value - high.astype(F32)).astype(BF16)


def mm(left, right):
    return lax.dot_general(left, right, (((1,), (0,)), ((), ())), preferred_element_type=F32)


def lanes(shape):
    return lax.broadcasted_iota(jnp.int32, shape, len(shape) - 1)


def turn(value, shift):
    shift = shift % 128
    return value if shift == 0 else pltpu.roll(value, shift, 1)


def pack_tail(parts):
    lane = lanes(parts[0].shape)
    upper = jnp.where(lane < 2 * TAIL, turn(parts[1], TAIL), turn(parts[2], 2 * TAIL))
    return jnp.where(lane < TAIL, parts[0], upper)


def pack_thirds(tail):
    third = NZ // 3
    return pack_tail([tail[third * g:third * (g + 1)] for g in range(3)])


def pack_field(wide):
    return jnp.concatenate([wide[:, :MAIN], pack_thirds(wide[:, MAIN:])], axis=0)


def unpack_field(packed):
    tail = packed[NZ:]
    tails = jnp.concatenate([turn(tail, -TAIL * g) for g in range(3)], axis=0)
    return jnp.concatenate([packed[:NZ], tails], axis=1)


def z_transform(table_ref, wide):
    high, low = split(wide)
    both = mm(table_ref[...], high)
    return both[:NZ] + both[NZ + 8:2 * NZ + 8] + mm(table_ref[:NZ + 8], low)[:NZ]


def turned_band(band, pad_ref):
    pad_ref[:ROWS, :NZ] = band
    return pack_field(jnp.transpose(pad_ref[...])[:NZ])


def order_bands(picked, orbitals_ref, own_ref, order_ref, pad_ref):
    for b in range(BLK):
        own_ref[b] = turned_band(orbitals_ref[:, b, :], pad_ref)
    for j in range(1, BLK):
        order_ref[j] = jnp.where(picked >= j, own_ref[j - 1], own_ref[j])


def visitor_of(f):
    return (True, f + 1) if f < 3 else (False, f - 3)


def cuts_of(f):
    result = []
    for chunk in range(2):
        low, high = max(NZ * f, 768 * chunk), min(NZ * (f + 1), 768 * (chunk + 1))
        if low < high:
            result.append((low, high - low, low + 256 * chunk))
    return result


def runs(row, rows):
    tile, count = row // 8, rows // 8
    done = 0
    while done < count:
        place, peer = divmod(tile + done, FFT)
        take = min(count - done, FFT - peer)
        yield place // 4, place % 4, peer, take, done
        done += take


def put_rows(buffer, row, value):
    tiles = value.reshape(value.shape[0] // 8, 8, 128)
    for chunk, part, peer, take, done in runs(row, value.shape[0]):
        buffer[chunk, peer:peer + take, part] = tiles[done:done + take]


def get_rows(buffer, row, rows):
    parts = [buffer[chunk, peer:peer + take, part].reshape(8 * take, 128) for chunk, part, peer, take, _ in runs(row, rows)]
    return parts[0] if len(parts) == 1 else jnp.concatenate(parts, axis=0)


def spectrum_of(f, order_ref, upper_ref, lower_ref, table_ref, buffer, tail_ref):
    low_side, j = visitor_of(f)
    density = (lower_ref if low_side else upper_ref)[...] * order_ref[j]
    spectrum = z_transform(table_ref, unpack_field(density))
    for low, count, place in cuts_of(f):
        first = low - NZ * f
        put_rows(buffer, place, spectrum[first:first + count, :MAIN])
        tail_ref[pl.ds(low, count), :] = spectrum[first:first + count, MAIN:]


def close_tails(chunk, buffer, tail_ref):
    parts = [tail_ref[pl.ds(768 * chunk + 256 * p, 256), :] for p in range(3)]
    put_rows(buffer, 1024 * chunk + 768, pack_tail(parts))


def open_tails(chunk, buffer, tail_ref):
    tails = get_rows(buffer, 1024 * chunk + 768, 256)
    for p in range(3):
        tail_ref[pl.ds(768 * chunk + 256 * p, 256), :] = turn(tails, -TAIL * p)


def main_of(f, buffer):
    mains = [get_rows(buffer, place, count) for _, count, place in cuts_of(f)]
    return mains[0] if len(mains) == 1 else jnp.concatenate(mains, axis=0)


def tail_of(f, tail_ref):
    return tail_ref[pl.ds(NZ * f, NZ), :]


def pieces():
    result = []
    row = 0
    while row < 4 * ROWS:
        source, j = divmod(row, ROWS)
        slab, y = divmod(row, NY)
        stop = min((source + 1) * ROWS, (slab + 1) * NY)
        if j < MAIN:
            stop = min(stop, source * ROWS + MAIN)
        result.append((source, j >= MAIN, j if j < MAIN else j - MAIN, slab, y, stop - row))
        row = stop
    return result


def tile_of(owner, chunk, p):
    return lax.rem(96 * chunk + 32 * p + owner, NZ // 8)


def gain_of(owner, plane, shells_ref, xy_ref, gain):
    chunk, place = plane // PLANES, lax.rem(plane, PLANES)
    depth = jnp.where(place == PLANES - 1, NZ // 2, 4 * tile_of(owner, chunk, place // 4) + lax.rem(place, 4))
    square = xy_ref[...] + (depth * depth).astype(F32)
    total = jnp.full(square.shape, shells_ref[0].astype(F32), F32)
    for s in range(1, NSHELL):
        step = (shells_ref[s] - shells_ref[s - 1]).astype(F32)
        total = total + jnp.where(square >= float(-(-s * (QTOP + 1) // NSHELL)), step, 0.0)
    g_squared = (2.0 * math.pi / (SPACING * SPAN)) ** 2 * square
    safe = jnp.where(square == 0, 1.0, g_squared)
    value = 4.0 * math.pi / safe * (1.0 - jnp.exp(-safe / (4.0 * SCREENING**2)))
    gain[pl.ds(pl.multiple_of(plane * NX, 8), NX), :] = total * jnp.where(square == 0, math.pi / SCREENING**2, value)


def open_rows(got_ref, chunk, box):
    cuts = pieces()
    lane = lanes((8, 128))

    def one(chip, carry):
        for slab in range(SLABS):
            mine = [c for c in cuts if c[3] == slab]
            for p in range(3):
                value = None
                for source, tail, first, _, y, _ in mine:
                    part = got_ref[chunk, 4 * chip + source, 3 if tail else p]
                    part = turn(part, y - first - (TAIL * p if tail else 0))
                    value = part if value is None else jnp.where(lane >= y, part, value)
                box[pl.ds(8 * p * NX + SLABS * chip + slab, 8, stride=NX), :] = value
        return carry

    lax.fori_loop(0, 8, one, 0)


def close_rows(box, chunk, send_ref):
    cuts = pieces()
    lane = lanes((8, 128))

    def one(chip, carry):
        fields = [[box[pl.ds(8 * p * NX + SLABS * chip + slab, 8, stride=NX), :] for slab in range(SLABS)] for p in range(3)]
        for source in range(4):
            tail_value = None
            for p in range(3):
                value = None
                for s, tail, first, slab, y, _ in cuts:
                    if s != source:
                        continue
                    if tail:
                        place = first + TAIL * p
                        part = turn(fields[p][slab], place - y)
                        tail_value = part if tail_value is None else jnp.where(lane >= place, part, tail_value)
                    else:
                        part = turn(fields[p][slab], first - y)
                        value = part if value is None else jnp.where(lane >= first, part, value)
                send_ref[chunk, 4 * chip + source, p] = value
            send_ref[chunk, 4 * chip + source, 3] = tail_value
        return carry

    lax.fori_loop(0, 8, one, 0)


def screen_planes(owner, chunk, x_ref, y_ref, box, work, gain):
    flags = [jnp.where(tile_of(owner, chunk, p) == 0, 1.0, 0.0).astype(F32) for p in range(3)]

    def along_x(real, imag):
        wide = jnp.concatenate([real, imag], axis=1)
        wide = jnp.concatenate([wide, jnp.zeros((8, 256), F32)], axis=0)
        high, low = split(wide)
        both = mm(x_ref[...], jnp.concatenate([high, high, low], axis=0))
        return both[:NX, :128], both[:NX, 128:], both[NX:, :128], both[NX:, 128:]

    def along_y(value, k):
        high, low = split(value)
        return mm(high, y_ref[k]) + mm(low, y_ref[k]) + mm(high, y_ref[k + 1])

    for plane in range(PLANES):
        if plane == 12:
            real = sum(flags[p] * box[pl.ds((8 * p + 4) * NX, NX), :] for p in range(3))
            imag = jnp.zeros_like(real)
        else:
            p, i = divmod(plane, 4)
            real = box[pl.ds((8 * p + i) * NX, NX), :]
            imag = box[pl.ds((8 * p + 4 + i) * NX, NX), :]
            if i == 0:
                imag = imag * (1.0 - flags[p])
        cr, ci, sr, si = along_x(real, imag)
        work[pl.ds(plane * NX, NX), :] = jnp.concatenate([cr + si, ci - sr], axis=1)
    weight = gain[pl.ds(chunk * PLANES * NX, PLANES * NX), :]
    value = along_y(work[...], 0) * jnp.concatenate([weight, weight], axis=1)
    work[...] = along_y(value, 2)
    extra = None
    for plane in reversed(range(PLANES)):
        rows = work[pl.ds(plane * NX, NX), :]
        cr, ci, sr, si = along_x(rows[:, :128], rows[:, 128:])
        real, imag = cr - si, ci + sr
        if plane == 12:
            extra = real
        else:
            p, i = divmod(plane, 4)
            if i == 0:
                imag = imag * (1.0 - flags[p]) + extra * flags[p]
            box[pl.ds((8 * p + i) * NX, NX), :] = real
            box[pl.ds((8 * p + 4 + i) * NX, NX), :] = imag


def intersect(total, bands_ref, partial_ref):
    lines = []
    for b in range(BLK):
        product = (bands_ref[b] * total).reshape(36, 8, 128)
        line = jnp.sum(jnp.sum(product, axis=0), axis=0, keepdims=True)
        line = line + turn(line, 64)
        lines.append(line + turn(line, 32))
    quarter = lanes((1, 128)) // 32
    row = lines[0]
    for b in range(1, BLK):
        row = jnp.where(quarter == b, lines[b], row)
    partial_ref[...] = row * SPACING**3


AROUND = [((1, -2, 3, -1, 2, -3, 4)[k % 7], (0, 2, 1, 3)[k % 4]) for k in range(28)] + [(0, turned) for turned in (2, 1, 3)]
STEPS = (AROUND, AROUND + [(0, 0)])


class Ring:
    def __init__(self, me, group, source, target, send_sem, recv_sem):
        self.source, self.target = source, target
        self.send_sem, self.recv_sem = send_sem, recv_sem
        self.me = me
        self.groups = [group, group + 1 - 2 * lax.rem(group, 2)]
        self.places = [lax.rem(me // 4 + k, 8) for k in range(8)]
        self.parts = [lax.rem(lax.rem(me, 4) + k, 4) for k in range(4)]

    def device(self, chunk, far, turned):
        return {"band": self.groups[chunk], "fft": 4 * self.places[far % 8] + self.parts[turned % 4]}

    def copy(self, source, target, peer, k):
        return pltpu.make_async_remote_copy(
            src_ref=source, dst_ref=target, send_sem=self.send_sem.at[k], recv_sem=self.recv_sem.at[k],
            device_id=peer, device_id_type=MESH,
        )

    def start(self, chunk, first, count, k, low=0, high=FFT):
        rows = pl.ds(first, count)
        for far, turned in STEPS[chunk][low:high]:
            peer = self.device(chunk, far, turned)
            self.copy(self.source.at[chunk, peer["fft"], rows], self.target.at[chunk, self.me, rows], peer, k).start()
        if chunk == 0:
            self.target[chunk, self.me, first:first + count] = self.source[chunk, self.me, first:first + count]

    def wait_recv(self, chunk, first, count, k):
        whole = self.target.at[chunk, pl.ds(0, len(STEPS[chunk])), pl.ds(first, count)]
        self.copy(whole, whole, self.device(chunk, 1, 0), k).wait_recv()

    def wait_send(self, chunk, first, count, k):
        whole = self.source.at[chunk, pl.ds(0, len(STEPS[chunk])), pl.ds(first, count)]
        self.copy(whole, whole, self.device(chunk, 1, 0), k).wait_send()


def whole_kernel(
    picked_ref, shells_ref, orbitals_far, forward_far, inverse_far, xy_far, x_far, y_far,
    total_ref, result_ref,
    orbitals_ref, forward_ref, inverse_ref, xy_ref, x_ref, y_ref, fetch_sem,
    own, order, upper, lower, up, down, above, below, mine, sent, got, back, returned, tails, box, work, gain, pad,
    partial, ring_slots, near, near_slots,
    there_send, there_recv, home_send, home_recv, band_send, band_recv, ring_send, ring_recv, near_send, near_recv,
):
    me = lax.axis_index("fft")
    group = lax.axis_index("band")
    count = lax.axis_size("band")
    above_me, below_me = lax.rem(group + 1, count), lax.rem(group + count - 1, count)

    barrier = pltpu.get_barrier_semaphore()
    for peer in (above_me, below_me):
        pl.semaphore_signal(barrier, inc=1, device_id={"band": peer}, device_id_type=MESH)
    there = Ring(me, group, sent, got, there_send, there_recv)
    home = Ring(me, group, back, returned, home_send, home_recv)
    for chunk in range(2):
        for far, turned in AROUND:
            pl.semaphore_signal(barrier, inc=1, device_id=there.device(chunk, far, turned), device_id_type=MESH)

    def to_band(source, target, peer, k):
        return pltpu.make_async_remote_copy(
            src_ref=source, dst_ref=target, send_sem=band_send.at[k], recv_sem=band_recv.at[k],
            device_id={"band": peer}, device_id_type=MESH,
        )

    chosen_up = to_band(order.at[0], lower, above_me, 0)
    chosen_down = to_band(order.at[0], upper, below_me, 1)
    sum_down = to_band(down, above, below_me, 2)
    main, tail = pl.ds(0, NZ), pl.ds(NZ, NZ // 3)
    sum_up_main = to_band(up.at[main], below.at[main], above_me, 3)
    sum_up_tail = to_band(up.at[tail], below.at[tail], above_me, 4)

    fetches = [
        pltpu.make_async_copy(far, ref, fetch_sem.at[k])
        for k, (far, ref) in enumerate(
            [
                (orbitals_far, orbitals_ref), (xy_far, xy_ref), (forward_far, forward_ref),
                (x_far, x_ref), (y_far, y_ref), (inverse_far, inverse_ref),
            ]
        )
    ]
    for one in fetches:
        one.start()
    picked = picked_ref[0]
    fetches[0].wait()
    pad[...] = jnp.zeros_like(pad)
    order[0] = turned_band(orbitals_ref[:, picked, :], pad)
    pl.semaphore_wait(barrier, 2 * FFT)
    chosen_up.start()
    order_bands(picked, orbitals_ref, own, order, pad)

    def gain_step(plane, carry):
        gain_of(me, plane, shells_ref, xy_ref, gain)
        return carry

    chosen_down.start()
    for one in fetches[1:]:
        one.wait()
    tails[pl.ds(NZ * FIELDS, 24), :] = jnp.zeros((24, 128), F32)
    put_rows(sent, NZ * FIELDS + 256, jnp.zeros((24, 128), F32))

    chosen_up.wait_recv()
    for f in range(3):
        spectrum_of(f, order, upper, lower, forward_ref, sent, tails)
    there.start(0, 0, 2, 0)
    chosen_down.wait_recv()
    spectrum_of(3, order, upper, lower, forward_ref, sent, tails)
    close_tails(0, sent, tails)
    there.start(0, 2, 2, 0)
    for f in range(4, FIELDS):
        spectrum_of(f, order, upper, lower, forward_ref, sent, tails)
    close_tails(1, sent, tails)
    there.start(1, 0, 4, 1)
    lax.fori_loop(0, 2 * PLANES, gain_step, 0)

    for chunk in range(2):
        there.wait_recv(chunk, 0, 4, chunk)
        open_rows(got, chunk, box)
        screen_planes(me, chunk, x_ref, y_ref, box, work, gain)
        close_rows(box, chunk, back)
        if chunk == 0:
            home.start(0, 0, 4, 0)
        else:
            home.start(1, 0, 3, 1, 0, 20)

    home.wait_recv(0, 0, 4, 0)
    open_tails(0, returned, tails)
    total = None
    for f in range(3):
        field = pack_field(z_transform(inverse_ref, jnp.concatenate([main_of(f, returned), tail_of(f, tails)], axis=1)))
        term = field * order[visitor_of(f)[1]]
        total = term if total is None else total + term
    down[...] = total
    sum_down.start()
    home.start(1, 0, 3, 1, 20)
    home.start(1, 3, 1, 2)

    def up_part(rows, fields):
        total = None
        for f, field in fields:
            if f == 3:
                mine[rows, :] = field * upper[rows, :]
            term = field * order[visitor_of(f)[1], rows, :]
            total = term if total is None else total + term
        up[rows, :] = total

    home.wait_recv(1, 0, 3, 1)
    up_part(main, [(f, z_transform(inverse_ref, main_of(f, returned))) for f in range(3, FIELDS)])
    sum_up_main.start()
    home.wait_recv(1, 3, 1, 2)
    open_tails(1, returned, tails)
    up_part(tail, [(f, pack_thirds(z_transform(inverse_ref, tail_of(f, tails)))) for f in range(3, FIELDS)])
    sum_up_tail.start()
    sum_down.wait_recv()
    mine[...] += above[...]
    sum_up_main.wait_recv()
    sum_up_tail.wait_recv()
    total = mine[...] + below[...]
    total_ref[...] = total
    intersect(total, own, partial)

    place, part = me // 4, lax.rem(me, 4)

    def row_to(source, target, peer, send_sem, recv_sem):
        return pltpu.make_async_remote_copy(
            src_ref=source, dst_ref=target, send_sem=send_sem, recv_sem=recv_sem,
            device_id={"fft": peer}, device_id_type=MESH,
        )

    ring = [
        row_to(partial, ring_slots.at[k], 4 * lax.rem(place + k, 8) + part, ring_send.at[k], ring_recv.at[k])
        for k in range(1, 8)
    ]
    for one in ring:
        one.start()
    row = partial[...]
    for k, one in enumerate(ring):
        one.wait()
        row = row + ring_slots[k + 1]
    near[...] = row
    beside = [
        row_to(near, near_slots.at[k], 4 * place + lax.rem(part + k, 4), near_send.at[k], near_recv.at[k])
        for k in range(1, 4)
    ]
    for one in beside:
        one.start()
    for k, one in enumerate(beside):
        one.wait()
        row = row + near_slots[k + 1]
    result_ref[...] = row

    there.wait_send(0, 0, 4, 0)
    there.wait_send(1, 0, 4, 1)
    home.wait_send(0, 0, 4, 0)
    home.wait_send(1, 0, 3, 1)
    home.wait_send(1, 3, 1, 2)
    for one in (chosen_up, chosen_down, sum_down, sum_up_main, sum_up_tail):
        one.wait_send()


def last_kernel(total_ref, row_ref, potential_ref, result_ref, pad_ref):
    pad_ref[...] = jnp.zeros_like(pad_ref)
    pad_ref[:NZ, :] = unpack_field(total_ref[...])
    potential_ref[:, 0, :] = jnp.transpose(pad_ref[...])[:ROWS, :NZ]
    row = row_ref[...]
    lane = lanes((1, BLK))
    result = jnp.zeros((1, BLK), F32)
    for b in range(BLK):
        mine = lanes((1, 128)) // 32 == b
        result = jnp.where(lane == b, jnp.sum(jnp.where(mine, row, 0.0), axis=1, keepdims=True), result)
    result_ref[...] = result


def vm():
    return pl.BlockSpec(memory_space=pltpu.VMEM)


def sm():
    return pl.BlockSpec(memory_space=pltpu.SMEM)


def params(**extra):
    return pltpu.CompilerParams(vmem_limit_bytes=VMEM_LIMIT, **extra)


def shape(*dims):
    return jax.ShapeDtypeStruct(dims, F32)


def body(orbitals, picked, shells):
    forward, inverse = z_stacks()
    along_x, along_y = x_table(), y_tables()
    exchange = pltpu.VMEM((2, FFT, 4, 8, 128), F32)
    field = pltpu.VMEM((288, 128), F32)
    bands = pltpu.VMEM((BLK, 288, 128), F32)
    line = pltpu.VMEM((1, 128), F32)
    dma = pltpu.SemaphoreType.DMA
    total, row = pl.pallas_call(
        whole_kernel,
        out_shape=(shape(288, 128), shape(1, 128)),
        in_specs=[sm(), sm()] + [pl.BlockSpec(memory_space=pltpu.HBM)] * 6,
        out_specs=(vm(), vm()),
        scratch_shapes=[
            pltpu.VMEM((ROWS, BLK, NZ), F32),
            pltpu.VMEM(forward.shape, BF16),
            pltpu.VMEM(inverse.shape, BF16),
            pltpu.VMEM((NX, 128), F32),
            pltpu.VMEM(along_x.shape, BF16),
            pltpu.VMEM(along_y.shape, BF16),
            dma((6,)),
            bands,
            bands,
        ]
        + [field] * 7
        + [exchange] * 4
        + [
            pltpu.VMEM((1536, 128), F32),
            pltpu.VMEM((24 * NX, 128), F32),
            pltpu.VMEM((PLANES * NX, 256), F32),
            pltpu.VMEM((2 * PLANES * NX, 128), F32),
            pltpu.VMEM((256, 256), F32),
            line,
            pltpu.VMEM((8, 1, 128), F32),
            line,
            pltpu.VMEM((4, 1, 128), F32),
        ]
        + [dma((2,))] * 2
        + [dma((3,))] * 2
        + [dma((5,))] * 2
        + [dma((8,))] * 2
        + [dma((4,))] * 2,
        compiler_params=params(collective_id=0, has_side_effects=True),
    )(
        picked, shells, jnp.transpose(orbitals, (1, 0, 2)), jnp.asarray(forward), jnp.asarray(inverse),
        jnp.asarray(xy_square()), jnp.asarray(along_x), jnp.asarray(along_y),
    )
    potentials, result = pl.pallas_call(
        last_kernel,
        out_shape=(shape(ROWS, 1, NZ), shape(1, BLK)),
        in_specs=[vm()] * 2,
        out_specs=(vm(), vm()),
        scratch_shapes=[pltpu.VMEM((256, 256), F32)],
        compiler_params=params(),
    )(total, row)
    return jnp.transpose(potentials, (1, 0, 2)), jnp.transpose(result)


def solution(mesh):
    return jax.shard_map(
        body,
        mesh=mesh,
        in_specs=(P("band", "fft", None), P("band"), P()),
        out_specs=(P("band", "fft", None), P("band", None)),
        check_vma=False,
    )
```

```python
import math

import jax
import jax.numpy as jnp
import numpy as np
from jax import lax
from jax.experimental import pallas as pl
from jax.experimental.pallas import tpu as pltpu
from jax.sharding import PartitionSpec as P

NX = 72
NY = 72
NZ = 216
BLK = 4
NSHELL = 64
FIELDS = 7
FFT = 32
ROWS = 162
MAIN = 128
TAIL = ROWS - MAIN
SLABS = 9
PLANES = 13

SPACING = 0.2
SCREENING = 0.106
FRACTION = 0.25
SPAN = math.lcm(NX, NY, NZ)
QTOP = (SPAN // NX) ** 2 * (NX // 2) ** 2 + (SPAN // NY) ** 2 * (NY // 2) ** 2 + (SPAN // NZ) ** 2 * (NZ // 2) ** 2
MESH = pl.DeviceIdType.MESH
F32 = jnp.float32
BF16 = jnp.bfloat16
VMEM_LIMIT = 60 * 1024 * 1024


def halves(table):
    table = np.asarray(table, np.float32)
    high = table.astype(jnp.bfloat16)
    low = (table - high.astype(np.float32)).astype(jnp.bfloat16)
    return high, low


def z_tables():
    freq, is_sin = np.zeros(NZ, np.int64), np.zeros(NZ, bool)
    for t in range(NZ // 8):
        for i in range(4):
            freq[8 * t + i] = 4 * t + i
            freq[8 * t + 4 + i] = 4 * t + i
            is_sin[8 * t + 4 + i] = True
    freq[4], is_sin[4] = NZ // 2, False
    angle = 2 * np.pi * (freq[:, None] * np.arange(NZ)[None, :] % NZ) / NZ
    forward = np.where(is_sin[:, None], -np.sin(angle), np.cos(angle))
    weight = np.where((freq == 0) | (freq == NZ // 2), 1.0, 2.0) / (NX * NY * NZ)
    inverse = (-FRACTION * weight[:, None] * forward).T
    return forward, inverse


def z_stacks():
    forward, inverse = z_tables()
    pad = np.zeros((8, NZ), jnp.bfloat16)

    def stack(table):
        high, low = halves(table)
        return np.concatenate([high, pad, low, pad], axis=0)

    return stack(forward), stack(inverse)


def xy_angle():
    index = np.arange(NX)
    return 2 * np.pi * (index[:, None] * index[None, :] % NX) / NX


def x_table():
    table = np.concatenate([np.cos(xy_angle()), np.sin(xy_angle())], axis=0)
    high, low = halves(table)
    pad = np.zeros((2 * NX, 8), high.dtype)
    return np.concatenate([high, pad, low, pad, high, pad], axis=1)


def y_tables():
    cosine, sine = np.cos(xy_angle()), np.sin(xy_angle())
    forward = np.zeros((256, 256))
    forward[:NY, :NY] = cosine
    forward[128:128 + NY, 128:128 + NY] = cosine
    forward[:NY, 128:128 + NY] = -sine
    forward[128:128 + NY, :NY] = sine
    fh, fl = halves(forward)
    return np.stack([fh, fl, fh.T, fl.T])


def xy_square():
    index = np.arange(NX)
    signed = np.where(index > NX // 2, index - NX, index)
    square = np.zeros((NX, 128), np.float32)
    square[:, :NY] = 9 * (signed[:, None] ** 2 + signed[None, :] ** 2)
    return square


def split(value):
    high = value.astype(BF16)
    return high, (value - high.astype(F32)).astype(BF16)


def mm(left, right):
    return lax.dot_general(left, right, (((1,), (0,)), ((), ())), preferred_element_type=F32)


def lanes(shape):
    return lax.broadcasted_iota(jnp.int32, shape, len(shape) - 1)


def turn(value, shift):
    shift = shift % 128
    return value if shift == 0 else pltpu.roll(value, shift, 1)


def pack_tail(parts):
    lane = lanes(parts[0].shape)
    upper = jnp.where(lane < 2 * TAIL, turn(parts[1], TAIL), turn(parts[2], 2 * TAIL))
    return jnp.where(lane < TAIL, parts[0], upper)


def pack_thirds(tail):
    third = NZ // 3
    return pack_tail([tail[third * g:third * (g + 1)] for g in range(3)])


def pack_field(wide):
    return jnp.concatenate([wide[:, :MAIN], pack_thirds(wide[:, MAIN:])], axis=0)


def unpack_field(packed):
    tail = packed[NZ:]
    tails = jnp.concatenate([turn(tail, -TAIL * g) for g in range(3)], axis=0)
    return jnp.concatenate([packed[:NZ], tails], axis=1)


def z_transform(table_ref, wide):
    high, low = split(wide)
    both = mm(table_ref[...], high)
    return both[:NZ] + both[NZ + 8:2 * NZ + 8] + mm(table_ref[:NZ + 8], low)[:NZ]


def turned_band(band, pad_ref):
    pad_ref[:ROWS, :NZ] = band
    return pack_field(jnp.transpose(pad_ref[...])[:NZ])


def order_bands(picked, orbitals_ref, own_ref, order_ref, pad_ref):
    for b in range(BLK):
        own_ref[b] = turned_band(orbitals_ref[:, b, :], pad_ref)
    for j in range(1, BLK):
        order_ref[j] = jnp.where(picked >= j, own_ref[j - 1], own_ref[j])


def visitor_of(f):
    return (True, f + 1) if f < 3 else (False, f - 3)


def cuts_of(f):
    result = []
    for chunk in range(2):
        low, high = max(NZ * f, 768 * chunk), min(NZ * (f + 1), 768 * (chunk + 1))
        if low < high:
            result.append((low, high - low, low + 256 * chunk))
    return result


def runs(row, rows):
    tile, count = row // 8, rows // 8
    done = 0
    while done < count:
        place, peer = divmod(tile + done, FFT)
        take = min(count - done, FFT - peer)
        yield place // 4, place % 4, peer, take, done
        done += take


def put_rows(buffer, row, value):
    tiles = value.reshape(value.shape[0] // 8, 8, 128)
    for chunk, part, peer, take, done in runs(row, value.shape[0]):
        buffer[chunk, peer:peer + take, part] = tiles[done:done + take]


def get_rows(buffer, row, rows):
    parts = [buffer[chunk, peer:peer + take, part].reshape(8 * take, 128) for chunk, part, peer, take, _ in runs(row, rows)]
    return parts[0] if len(parts) == 1 else jnp.concatenate(parts, axis=0)


def spectrum_of(f, order_ref, upper_ref, lower_ref, table_ref, buffer, tail_ref):
    low_side, j = visitor_of(f)
    density = (lower_ref if low_side else upper_ref)[...] * order_ref[j]
    spectrum = z_transform(table_ref, unpack_field(density))
    for low, count, place in cuts_of(f):
        first = low - NZ * f
        put_rows(buffer, place, spectrum[first:first + count, :MAIN])
        tail_ref[pl.ds(low, count), :] = spectrum[first:first + count, MAIN:]


def close_tails(chunk, buffer, tail_ref):
    parts = [tail_ref[pl.ds(768 * chunk + 256 * p, 256), :] for p in range(3)]
    put_rows(buffer, 1024 * chunk + 768, pack_tail(parts))


def open_tails(chunk, buffer, tail_ref):
    tails = get_rows(buffer, 1024 * chunk + 768, 256)
    for p in range(3):
        tail_ref[pl.ds(768 * chunk + 256 * p, 256), :] = turn(tails, -TAIL * p)


def main_of(f, buffer):
    mains = [get_rows(buffer, place, count) for _, count, place in cuts_of(f)]
    return mains[0] if len(mains) == 1 else jnp.concatenate(mains, axis=0)


def tail_of(f, tail_ref):
    return tail_ref[pl.ds(NZ * f, NZ), :]


def pieces():
    result = []
    row = 0
    while row < 4 * ROWS:
        source, j = divmod(row, ROWS)
        slab, y = divmod(row, NY)
        stop = min((source + 1) * ROWS, (slab + 1) * NY)
        if j < MAIN:
            stop = min(stop, source * ROWS + MAIN)
        result.append((source, j >= MAIN, j if j < MAIN else j - MAIN, slab, y, stop - row))
        row = stop
    return result


def tile_of(owner, chunk, p):
    return lax.rem(96 * chunk + 32 * p + owner, NZ // 8)


def gain_of(owner, plane, shells_ref, xy_ref, gain):
    chunk, place = plane // PLANES, lax.rem(plane, PLANES)
    depth = jnp.where(place == PLANES - 1, NZ // 2, 4 * tile_of(owner, chunk, place // 4) + lax.rem(place, 4))
    square = xy_ref[...] + (depth * depth).astype(F32)
    total = jnp.full(square.shape, shells_ref[0].astype(F32), F32)
    for s in range(1, NSHELL):
        step = (shells_ref[s] - shells_ref[s - 1]).astype(F32)
        total = total + jnp.where(square >= float(-(-s * (QTOP + 1) // NSHELL)), step, 0.0)
    g_squared = (2.0 * math.pi / (SPACING * SPAN)) ** 2 * square
    safe = jnp.where(square == 0, 1.0, g_squared)
    value = 4.0 * math.pi / safe * (1.0 - jnp.exp(-safe / (4.0 * SCREENING**2)))
    gain[pl.ds(pl.multiple_of(plane * NX, 8), NX), :] = total * jnp.where(square == 0, math.pi / SCREENING**2, value)


def open_rows(got_ref, chunk, box):
    cuts = pieces()
    lane = lanes((8, 128))

    def one(chip, carry):
        for slab in range(SLABS):
            mine = [c for c in cuts if c[3] == slab]
            for p in range(3):
                value = None
                for source, tail, first, _, y, _ in mine:
                    part = got_ref[chunk, 4 * chip + source, 3 if tail else p]
                    part = turn(part, y - first - (TAIL * p if tail else 0))
                    value = part if value is None else jnp.where(lane >= y, part, value)
                box[pl.ds(8 * p * NX + SLABS * chip + slab, 8, stride=NX), :] = value
        return carry

    lax.fori_loop(0, 8, one, 0)


def close_rows(box, chunk, send_ref):
    cuts = pieces()
    lane = lanes((8, 128))

    def one(chip, carry):
        fields = [[box[pl.ds(8 * p * NX + SLABS * chip + slab, 8, stride=NX), :] for slab in range(SLABS)] for p in range(3)]
        for source in range(4):
            tail_value = None
            for p in range(3):
                value = None
                for s, tail, first, slab, y, _ in cuts:
                    if s != source:
                        continue
                    if tail:
                        place = first + TAIL * p
                        part = turn(fields[p][slab], place - y)
                        tail_value = part if tail_value is None else jnp.where(lane >= place, part, tail_value)
                    else:
                        part = turn(fields[p][slab], first - y)
                        value = part if value is None else jnp.where(lane >= first, part, value)
                send_ref[chunk, 4 * chip + source, p] = value
            send_ref[chunk, 4 * chip + source, 3] = tail_value
        return carry

    lax.fori_loop(0, 8, one, 0)


def screen_planes(owner, chunk, x_ref, y_ref, box, work, gain):
    flags = [jnp.where(tile_of(owner, chunk, p) == 0, 1.0, 0.0).astype(F32) for p in range(3)]

    def along_x(real, imag):
        wide = jnp.concatenate([real, imag], axis=1)
        wide = jnp.concatenate([wide, jnp.zeros((8, 256), F32)], axis=0)
        high, low = split(wide)
        both = mm(x_ref[...], jnp.concatenate([high, high, low], axis=0))
        return both[:NX, :128], both[:NX, 128:], both[NX:, :128], both[NX:, 128:]

    def along_y(value, k):
        high, low = split(value)
        return mm(high, y_ref[k]) + mm(low, y_ref[k]) + mm(high, y_ref[k + 1])

    for plane in range(PLANES):
        if plane == 12:
            real = sum(flags[p] * box[pl.ds((8 * p + 4) * NX, NX), :] for p in range(3))
            imag = jnp.zeros_like(real)
        else:
            p, i = divmod(plane, 4)
            real = box[pl.ds((8 * p + i) * NX, NX), :]
            imag = box[pl.ds((8 * p + 4 + i) * NX, NX), :]
            if i == 0:
                imag = imag * (1.0 - flags[p])
        cr, ci, sr, si = along_x(real, imag)
        work[pl.ds(plane * NX, NX), :] = jnp.concatenate([cr + si, ci - sr], axis=1)
    weight = gain[pl.ds(chunk * PLANES * NX, PLANES * NX), :]
    value = along_y(work[...], 0) * jnp.concatenate([weight, weight], axis=1)
    work[...] = along_y(value, 2)
    extra = None
    for plane in reversed(range(PLANES)):
        rows = work[pl.ds(plane * NX, NX), :]
        cr, ci, sr, si = along_x(rows[:, :128], rows[:, 128:])
        real, imag = cr - si, ci + sr
        if plane == 12:
            extra = real
        else:
            p, i = divmod(plane, 4)
            if i == 0:
                imag = imag * (1.0 - flags[p]) + extra * flags[p]
            box[pl.ds((8 * p + i) * NX, NX), :] = real
            box[pl.ds((8 * p + 4 + i) * NX, NX), :] = imag


def intersect(total, bands_ref, partial_ref):
    lines = []
    for b in range(BLK):
        product = (bands_ref[b] * total).reshape(36, 8, 128)
        line = jnp.sum(jnp.sum(product, axis=0), axis=0, keepdims=True)
        line = line + turn(line, 64)
        lines.append(line + turn(line, 32))
    quarter = lanes((1, 128)) // 32
    row = lines[0]
    for b in range(1, BLK):
        row = jnp.where(quarter == b, lines[b], row)
    partial_ref[...] = row * SPACING**3


AROUND = [((1, -2, 3, -1, 2, -3, 4)[k % 7], (0, 2, 1, 3)[k % 4]) for k in range(28)] + [(0, turned) for turned in (2, 1, 3)]
STEPS = (AROUND, AROUND + [(0, 0)])


class Ring:
    def __init__(self, me, group, source, target, send_sem, recv_sem):
        self.source, self.target = source, target
        self.send_sem, self.recv_sem = send_sem, recv_sem
        self.me = me
        self.groups = [group, group + 1 - 2 * lax.rem(group, 2)]
        self.places = [lax.rem(me // 4 + k, 8) for k in range(8)]
        self.parts = [lax.rem(lax.rem(me, 4) + k, 4) for k in range(4)]

    def device(self, chunk, far, turned):
        return {"band": self.groups[chunk], "fft": 4 * self.places[far % 8] + self.parts[turned % 4]}

    def copy(self, source, target, peer, k):
        return pltpu.make_async_remote_copy(
            src_ref=source, dst_ref=target, send_sem=self.send_sem.at[k], recv_sem=self.recv_sem.at[k],
            device_id=peer, device_id_type=MESH,
        )

    def start(self, chunk, first, count, k, low=0, high=FFT):
        rows = pl.ds(first, count)
        for far, turned in STEPS[chunk][low:high]:
            peer = self.device(chunk, far, turned)
            self.copy(self.source.at[chunk, peer["fft"], rows], self.target.at[chunk, self.me, rows], peer, k).start()
        if chunk == 0 and high == FFT:
            self.target[chunk, self.me, first:first + count] = self.source[chunk, self.me, first:first + count]

    def wait_recv(self, chunk, first, count, k):
        whole = self.target.at[chunk, pl.ds(0, len(STEPS[chunk])), pl.ds(first, count)]
        self.copy(whole, whole, self.device(chunk, 1, 0), k).wait_recv()

    def wait_send(self, chunk, first, count, k):
        whole = self.source.at[chunk, pl.ds(0, len(STEPS[chunk])), pl.ds(first, count)]
        self.copy(whole, whole, self.device(chunk, 1, 0), k).wait_send()


def whole_kernel(
    picked_ref, shells_ref, orbitals_far, forward_far, inverse_far, xy_far, x_far, y_far,
    total_ref, result_ref,
    orbitals_ref, forward_ref, inverse_ref, xy_ref, x_ref, y_ref, fetch_sem,
    own, order, upper, lower, up, down, above, below, mine, sent, got, back, returned, tails, box, work, gain, pad,
    partial, ring_slots, near, near_slots,
    there_send, there_recv, home_send, home_recv, band_send, band_recv, ring_send, ring_recv, near_send, near_recv,
):
    me = lax.axis_index("fft")
    group = lax.axis_index("band")
    count = lax.axis_size("band")
    above_me, below_me = lax.rem(group + 1, count), lax.rem(group + count - 1, count)

    barrier = pltpu.get_barrier_semaphore()
    for peer in (above_me, below_me):
        pl.semaphore_signal(barrier, inc=1, device_id={"band": peer}, device_id_type=MESH)
    there = Ring(me, group, sent, got, there_send, there_recv)
    home = Ring(me, group, back, returned, home_send, home_recv)
    for chunk in range(2):
        for far, turned in AROUND:
            pl.semaphore_signal(barrier, inc=1, device_id=there.device(chunk, far, turned), device_id_type=MESH)

    def to_band(source, target, peer, k):
        return pltpu.make_async_remote_copy(
            src_ref=source, dst_ref=target, send_sem=band_send.at[k], recv_sem=band_recv.at[k],
            device_id={"band": peer}, device_id_type=MESH,
        )

    chosen_up = to_band(order.at[0], lower, above_me, 0)
    chosen_down = to_band(order.at[0], upper, below_me, 1)
    sum_down = to_band(down, above, below_me, 2)
    main, tail = pl.ds(0, NZ), pl.ds(NZ, NZ // 3)
    sum_up_main = to_band(up.at[main], below.at[main], above_me, 3)
    sum_up_tail = to_band(up.at[tail], below.at[tail], above_me, 4)

    fetches = [
        pltpu.make_async_copy(far, ref, fetch_sem.at[k])
        for k, (far, ref) in enumerate(
            [
                (orbitals_far, orbitals_ref), (xy_far, xy_ref), (forward_far, forward_ref),
                (x_far, x_ref), (y_far, y_ref), (inverse_far, inverse_ref),
            ]
        )
    ]
    for one in fetches:
        one.start()
    picked = picked_ref[0]
    fetches[0].wait()
    pad[...] = jnp.zeros_like(pad)
    order[0] = turned_band(orbitals_ref[:, picked, :], pad)
    pl.semaphore_wait(barrier, 2 * FFT)
    chosen_up.start()
    order_bands(picked, orbitals_ref, own, order, pad)

    def gain_step(plane, carry):
        gain_of(me, plane, shells_ref, xy_ref, gain)
        return carry

    chosen_down.start()
    for one in fetches[1:]:
        one.wait()
    tails[pl.ds(NZ * FIELDS, 24), :] = jnp.zeros((24, 128), F32)
    put_rows(sent, NZ * FIELDS + 256, jnp.zeros((24, 128), F32))

    chosen_up.wait_recv()
    for f in range(3):
        spectrum_of(f, order, upper, lower, forward_ref, sent, tails)
    there.start(0, 0, 2, 0)
    chosen_down.wait_recv()
    spectrum_of(3, order, upper, lower, forward_ref, sent, tails)
    close_tails(0, sent, tails)
    there.start(0, 2, 2, 0)
    for f in range(4, FIELDS):
        spectrum_of(f, order, upper, lower, forward_ref, sent, tails)
    close_tails(1, sent, tails)
    there.start(1, 0, 4, 1)
    lax.fori_loop(0, 2 * PLANES, gain_step, 0)

    for chunk in range(2):
        there.wait_recv(chunk, 0, 4, chunk)
        if chunk == 1:
            home.start(0, 0, 4, 0, 8)
        open_rows(got, chunk, box)
        screen_planes(me, chunk, x_ref, y_ref, box, work, gain)
        close_rows(box, chunk, back)
        if chunk == 0:
            home.start(0, 0, 4, 0, 0, 8)
        else:
            home.start(1, 0, 3, 1, 0, 20)

    home.wait_recv(0, 0, 4, 0)
    open_tails(0, returned, tails)
    total = None
    for f in range(3):
        field = pack_field(z_transform(inverse_ref, jnp.concatenate([main_of(f, returned), tail_of(f, tails)], axis=1)))
        term = field * order[visitor_of(f)[1]]
        total = term if total is None else total + term
    down[...] = total
    sum_down.start()
    home.start(1, 0, 3, 1, 20)
    home.start(1, 3, 1, 2)

    def up_part(rows, fields):
        total = None
        for f, field in fields:
            if f == 3:
                mine[rows, :] = field * upper[rows, :]
            term = field * order[visitor_of(f)[1], rows, :]
            total = term if total is None else total + term
        up[rows, :] = total

    home.wait_recv(1, 0, 3, 1)
    up_part(main, [(f, z_transform(inverse_ref, main_of(f, returned))) for f in range(3, FIELDS)])
    sum_up_main.start()
    home.wait_recv(1, 3, 1, 2)
    open_tails(1, returned, tails)
    up_part(tail, [(f, pack_thirds(z_transform(inverse_ref, tail_of(f, tails)))) for f in range(3, FIELDS)])
    sum_up_tail.start()
    sum_down.wait_recv()
    mine[...] += above[...]
    sum_up_main.wait_recv()
    sum_up_tail.wait_recv()
    total = mine[...] + below[...]
    total_ref[...] = total
    intersect(total, own, partial)

    place, part = me // 4, lax.rem(me, 4)

    def row_to(source, target, peer, send_sem, recv_sem):
        return pltpu.make_async_remote_copy(
            src_ref=source, dst_ref=target, send_sem=send_sem, recv_sem=recv_sem,
            device_id={"fft": peer}, device_id_type=MESH,
        )

    ring = [
        row_to(partial, ring_slots.at[k], 4 * lax.rem(place + k, 8) + part, ring_send.at[k], ring_recv.at[k])
        for k in range(1, 8)
    ]
    for one in ring:
        one.start()
    row = partial[...]
    for k, one in enumerate(ring):
        one.wait()
        row = row + ring_slots[k + 1]
    near[...] = row
    beside = [
        row_to(near, near_slots.at[k], 4 * place + lax.rem(part + k, 4), near_send.at[k], near_recv.at[k])
        for k in range(1, 4)
    ]
    for one in beside:
        one.start()
    for k, one in enumerate(beside):
        one.wait()
        row = row + near_slots[k + 1]
    result_ref[...] = row

    there.wait_send(0, 0, 4, 0)
    there.wait_send(1, 0, 4, 1)
    home.wait_send(0, 0, 4, 0)
    home.wait_send(1, 0, 3, 1)
    home.wait_send(1, 3, 1, 2)
    for one in (chosen_up, chosen_down, sum_down, sum_up_main, sum_up_tail):
        one.wait_send()


def last_kernel(total_ref, row_ref, potential_ref, result_ref, pad_ref):
    pad_ref[...] = jnp.zeros_like(pad_ref)
    pad_ref[:NZ, :] = unpack_field(total_ref[...])
    potential_ref[:, 0, :] = jnp.transpose(pad_ref[...])[:ROWS, :NZ]
    row = row_ref[...]
    lane = lanes((1, BLK))
    result = jnp.zeros((1, BLK), F32)
    for b in range(BLK):
        mine = lanes((1, 128)) // 32 == b
        result = jnp.where(lane == b, jnp.sum(jnp.where(mine, row, 0.0), axis=1, keepdims=True), result)
    result_ref[...] = result


def vm():
    return pl.BlockSpec(memory_space=pltpu.VMEM)


def sm():
    return pl.BlockSpec(memory_space=pltpu.SMEM)


def params(**extra):
    return pltpu.CompilerParams(vmem_limit_bytes=VMEM_LIMIT, **extra)


def shape(*dims):
    return jax.ShapeDtypeStruct(dims, F32)


def body(orbitals, picked, shells):
    forward, inverse = z_stacks()
    along_x, along_y = x_table(), y_tables()
    exchange = pltpu.VMEM((2, FFT, 4, 8, 128), F32)
    field = pltpu.VMEM((288, 128), F32)
    bands = pltpu.VMEM((BLK, 288, 128), F32)
    line = pltpu.VMEM((1, 128), F32)
    dma = pltpu.SemaphoreType.DMA
    total, row = pl.pallas_call(
        whole_kernel,
        out_shape=(shape(288, 128), shape(1, 128)),
        in_specs=[sm(), sm()] + [pl.BlockSpec(memory_space=pltpu.HBM)] * 6,
        out_specs=(vm(), vm()),
        scratch_shapes=[
            pltpu.VMEM((ROWS, BLK, NZ), F32),
            pltpu.VMEM(forward.shape, BF16),
            pltpu.VMEM(inverse.shape, BF16),
            pltpu.VMEM((NX, 128), F32),
            pltpu.VMEM(along_x.shape, BF16),
            pltpu.VMEM(along_y.shape, BF16),
            dma((6,)),
            bands,
            bands,
        ]
        + [field] * 7
        + [exchange] * 4
        + [
            pltpu.VMEM((1536, 128), F32),
            pltpu.VMEM((24 * NX, 128), F32),
            pltpu.VMEM((PLANES * NX, 256), F32),
            pltpu.VMEM((2 * PLANES * NX, 128), F32),
            pltpu.VMEM((256, 256), F32),
            line,
            pltpu.VMEM((8, 1, 128), F32),
            line,
            pltpu.VMEM((4, 1, 128), F32),
        ]
        + [dma((2,))] * 2
        + [dma((3,))] * 2
        + [dma((5,))] * 2
        + [dma((8,))] * 2
        + [dma((4,))] * 2,
        compiler_params=params(collective_id=0, has_side_effects=True),
    )(
        picked, shells, jnp.transpose(orbitals, (1, 0, 2)), jnp.asarray(forward), jnp.asarray(inverse),
        jnp.asarray(xy_square()), jnp.asarray(along_x), jnp.asarray(along_y),
    )
    potentials, result = pl.pallas_call(
        last_kernel,
        out_shape=(shape(ROWS, 1, NZ), shape(1, BLK)),
        in_specs=[vm()] * 2,
        out_specs=(vm(), vm()),
        scratch_shapes=[pltpu.VMEM((256, 256), F32)],
        compiler_params=params(),
    )(total, row)
    return jnp.transpose(potentials, (1, 0, 2)), jnp.transpose(result)


def solution(mesh):
    return jax.shard_map(
        body,
        mesh=mesh,
        in_specs=(P("band", "fft", None), P("band"), P()),
        out_specs=(P("band", "fft", None), P("band", None)),
        check_vma=False,
    )
```

```python
import math

import jax
import jax.numpy as jnp
import numpy as np
from jax import lax
from jax.experimental import pallas as pl
from jax.experimental.pallas import tpu as pltpu
from jax.sharding import PartitionSpec as P

NX = 72
NY = 72
NZ = 216
BLK = 4
NSHELL = 64
FIELDS = 7
FFT = 32
ROWS = 162
MAIN = 128
TAIL = ROWS - MAIN
SLABS = 9
PLANES = 13

SPACING = 0.2
SCREENING = 0.106
FRACTION = 0.25
SPAN = math.lcm(NX, NY, NZ)
QTOP = (SPAN // NX) ** 2 * (NX // 2) ** 2 + (SPAN // NY) ** 2 * (NY // 2) ** 2 + (SPAN // NZ) ** 2 * (NZ // 2) ** 2
MESH = pl.DeviceIdType.MESH
F32 = jnp.float32
BF16 = jnp.bfloat16
VMEM_LIMIT = 60 * 1024 * 1024


def halves(table):
    table = np.asarray(table, np.float32)
    high = table.astype(jnp.bfloat16)
    low = (table - high.astype(np.float32)).astype(jnp.bfloat16)
    return high, low


def z_tables():
    freq, is_sin = np.zeros(NZ, np.int64), np.zeros(NZ, bool)
    for t in range(NZ // 8):
        for i in range(4):
            freq[8 * t + i] = 4 * t + i
            freq[8 * t + 4 + i] = 4 * t + i
            is_sin[8 * t + 4 + i] = True
    freq[4], is_sin[4] = NZ // 2, False
    angle = 2 * np.pi * (freq[:, None] * np.arange(NZ)[None, :] % NZ) / NZ
    forward = np.where(is_sin[:, None], -np.sin(angle), np.cos(angle))
    weight = np.where((freq == 0) | (freq == NZ // 2), 1.0, 2.0) / (NX * NY * NZ)
    inverse = (-FRACTION * weight[:, None] * forward).T
    return forward, inverse


def z_stacks():
    forward, inverse = z_tables()
    pad = np.zeros((8, NZ), jnp.bfloat16)

    def stack(table):
        high, low = halves(table)
        return np.concatenate([high, pad, low, pad], axis=0)

    return stack(forward), stack(inverse)


def xy_angle():
    index = np.arange(NX)
    return 2 * np.pi * (index[:, None] * index[None, :] % NX) / NX


def x_table():
    table = np.concatenate([np.cos(xy_angle()), np.sin(xy_angle())], axis=0)
    high, low = halves(table)
    pad = np.zeros((2 * NX, 8), high.dtype)
    return np.concatenate([high, pad, low, pad, high, pad], axis=1)


def y_tables():
    cosine, sine = np.cos(xy_angle()), np.sin(xy_angle())
    forward = np.zeros((256, 256))
    forward[:NY, :NY] = cosine
    forward[128:128 + NY, 128:128 + NY] = cosine
    forward[:NY, 128:128 + NY] = -sine
    forward[128:128 + NY, :NY] = sine
    fh, fl = halves(forward)
    return np.stack([fh, fl, fh.T, fl.T])


def xy_square():
    index = np.arange(NX)
    signed = np.where(index > NX // 2, index - NX, index)
    square = np.zeros((NX, 128), np.float32)
    square[:, :NY] = 9 * (signed[:, None] ** 2 + signed[None, :] ** 2)
    return square


def split(value):
    high = value.astype(BF16)
    return high, (value - high.astype(F32)).astype(BF16)


def mm(left, right):
    return lax.dot_general(left, right, (((1,), (0,)), ((), ())), preferred_element_type=F32)


def lanes(shape):
    return lax.broadcasted_iota(jnp.int32, shape, len(shape) - 1)


def turn(value, shift):
    shift = shift % 128
    return value if shift == 0 else pltpu.roll(value, shift, 1)


def pack_tail(parts):
    lane = lanes(parts[0].shape)
    upper = jnp.where(lane < 2 * TAIL, turn(parts[1], TAIL), turn(parts[2], 2 * TAIL))
    return jnp.where(lane < TAIL, parts[0], upper)


def pack_thirds(tail):
    third = NZ // 3
    return pack_tail([tail[third * g:third * (g + 1)] for g in range(3)])


def pack_field(wide):
    return jnp.concatenate([wide[:, :MAIN], pack_thirds(wide[:, MAIN:])], axis=0)


def unpack_field(packed):
    tail = packed[NZ:]
    tails = jnp.concatenate([turn(tail, -TAIL * g) for g in range(3)], axis=0)
    return jnp.concatenate([packed[:NZ], tails], axis=1)


def z_transform(table_ref, wide):
    high, low = split(wide)
    both = mm(table_ref[...], high)
    return both[:NZ] + both[NZ + 8:2 * NZ + 8] + mm(table_ref[:NZ + 8], low)[:NZ]


def turned_band(band, pad_ref):
    pad_ref[:ROWS, :NZ] = band
    return pack_field(jnp.transpose(pad_ref[...])[:NZ])


def order_bands(picked, orbitals_ref, own_ref, order_ref, pad_ref):
    for b in range(BLK):
        own_ref[b] = turned_band(orbitals_ref[:, b, :], pad_ref)
    for j in range(1, BLK):
        order_ref[j] = jnp.where(picked >= j, own_ref[j - 1], own_ref[j])


def visitor_of(f):
    return (True, f + 1) if f < 3 else (False, f - 3)


def cuts_of(f):
    result = []
    for chunk in range(2):
        low, high = max(NZ * f, 768 * chunk), min(NZ * (f + 1), 768 * (chunk + 1))
        if low < high:
            result.append((low, high - low, low + 256 * chunk))
    return result


def runs(row, rows):
    tile, count = row // 8, rows // 8
    done = 0
    while done < count:
        place, peer = divmod(tile + done, FFT)
        take = min(count - done, FFT - peer)
        yield place // 4, place % 4, peer, take, done
        done += take


def put_rows(buffer, row, value):
    tiles = value.reshape(value.shape[0] // 8, 8, 128)
    for chunk, part, peer, take, done in runs(row, value.shape[0]):
        buffer[chunk, peer:peer + take, part] = tiles[done:done + take]


def get_rows(buffer, row, rows):
    parts = [buffer[chunk, peer:peer + take, part].reshape(8 * take, 128) for chunk, part, peer, take, _ in runs(row, rows)]
    return parts[0] if len(parts) == 1 else jnp.concatenate(parts, axis=0)


def spectrum_of(f, order_ref, upper_ref, lower_ref, table_ref, buffer, tail_ref):
    low_side, j = visitor_of(f)
    density = (lower_ref if low_side else upper_ref)[...] * order_ref[j]
    spectrum = z_transform(table_ref, unpack_field(density))
    for low, count, place in cuts_of(f):
        first = low - NZ * f
        put_rows(buffer, place, spectrum[first:first + count, :MAIN])
        tail_ref[pl.ds(low, count), :] = spectrum[first:first + count, MAIN:]


def close_tails(chunk, buffer, tail_ref):
    parts = [tail_ref[pl.ds(768 * chunk + 256 * p, 256), :] for p in range(3)]
    put_rows(buffer, 1024 * chunk + 768, pack_tail(parts))


def open_tails(chunk, buffer, tail_ref):
    tails = get_rows(buffer, 1024 * chunk + 768, 256)
    for p in range(3):
        tail_ref[pl.ds(768 * chunk + 256 * p, 256), :] = turn(tails, -TAIL * p)


def main_of(f, buffer):
    mains = [get_rows(buffer, place, count) for _, count, place in cuts_of(f)]
    return mains[0] if len(mains) == 1 else jnp.concatenate(mains, axis=0)


def tail_of(f, tail_ref):
    return tail_ref[pl.ds(NZ * f, NZ), :]


def pieces():
    result = []
    row = 0
    while row < 4 * ROWS:
        source, j = divmod(row, ROWS)
        slab, y = divmod(row, NY)
        stop = min((source + 1) * ROWS, (slab + 1) * NY)
        if j < MAIN:
            stop = min(stop, source * ROWS + MAIN)
        result.append((source, j >= MAIN, j if j < MAIN else j - MAIN, slab, y, stop - row))
        row = stop
    return result


def tile_of(owner, chunk, p):
    return lax.rem(96 * chunk + 32 * p + owner, NZ // 8)


def gain_of(owner, plane, shells_ref, xy_ref, gain):
    chunk, place = plane // PLANES, lax.rem(plane, PLANES)
    depth = jnp.where(place == PLANES - 1, NZ // 2, 4 * tile_of(owner, chunk, place // 4) + lax.rem(place, 4))
    square = xy_ref[...] + (depth * depth).astype(F32)
    total = jnp.full(square.shape, shells_ref[0].astype(F32), F32)
    for s in range(1, NSHELL):
        step = (shells_ref[s] - shells_ref[s - 1]).astype(F32)
        total = total + jnp.where(square >= float(-(-s * (QTOP + 1) // NSHELL)), step, 0.0)
    g_squared = (2.0 * math.pi / (SPACING * SPAN)) ** 2 * square
    safe = jnp.where(square == 0, 1.0, g_squared)
    value = 4.0 * math.pi / safe * (1.0 - jnp.exp(-safe / (4.0 * SCREENING**2)))
    gain[pl.ds(pl.multiple_of(plane * NX, 8), NX), :] = total * jnp.where(square == 0, math.pi / SCREENING**2, value)


def open_rows(got_ref, chunk, box):
    cuts = pieces()
    lane = lanes((8, 128))

    def one(chip, carry):
        for slab in range(SLABS):
            mine = [c for c in cuts if c[3] == slab]
            for p in range(3):
                value = None
                for source, tail, first, _, y, _ in mine:
                    part = got_ref[chunk, 4 * chip + source, 3 if tail else p]
                    part = turn(part, y - first - (TAIL * p if tail else 0))
                    value = part if value is None else jnp.where(lane >= y, part, value)
                box[pl.ds(8 * p * NX + SLABS * chip + slab, 8, stride=NX), :] = value
        return carry

    lax.fori_loop(0, 8, one, 0)


def close_rows(box, chunk, send_ref):
    cuts = pieces()
    lane = lanes((8, 128))

    def one(chip, carry):
        fields = [[box[pl.ds(8 * p * NX + SLABS * chip + slab, 8, stride=NX), :] for slab in range(SLABS)] for p in range(3)]
        for source in range(4):
            tail_value = None
            for p in range(3):
                value = None
                for s, tail, first, slab, y, _ in cuts:
                    if s != source:
                        continue
                    if tail:
                        place = first + TAIL * p
                        part = turn(fields[p][slab], place - y)
                        tail_value = part if tail_value is None else jnp.where(lane >= place, part, tail_value)
                    else:
                        part = turn(fields[p][slab], first - y)
                        value = part if value is None else jnp.where(lane >= first, part, value)
                send_ref[chunk, 4 * chip + source, p] = value
            send_ref[chunk, 4 * chip + source, 3] = tail_value
        return carry

    lax.fori_loop(0, 8, one, 0)


def screen_planes(owner, chunk, x_ref, y_ref, box, work, gain):
    flags = [jnp.where(tile_of(owner, chunk, p) == 0, 1.0, 0.0).astype(F32) for p in range(3)]

    def along_x(real, imag):
        wide = jnp.concatenate([real, imag], axis=1)
        wide = jnp.concatenate([wide, jnp.zeros((8, 256), F32)], axis=0)
        high, low = split(wide)
        both = mm(x_ref[...], jnp.concatenate([high, high, low], axis=0))
        return both[:NX, :128], both[:NX, 128:], both[NX:, :128], both[NX:, 128:]

    def along_y(value, k):
        high, low = split(value)
        return mm(high, y_ref[k]) + mm(low, y_ref[k]) + mm(high, y_ref[k + 1])

    for plane in range(PLANES):
        if plane == 12:
            real = sum(flags[p] * box[pl.ds((8 * p + 4) * NX, NX), :] for p in range(3))
            imag = jnp.zeros_like(real)
        else:
            p, i = divmod(plane, 4)
            real = box[pl.ds((8 * p + i) * NX, NX), :]
            imag = box[pl.ds((8 * p + 4 + i) * NX, NX), :]
            if i == 0:
                imag = imag * (1.0 - flags[p])
        cr, ci, sr, si = along_x(real, imag)
        work[pl.ds(plane * NX, NX), :] = jnp.concatenate([cr + si, ci - sr], axis=1)
    weight = gain[pl.ds(chunk * PLANES * NX, PLANES * NX), :]
    value = along_y(work[...], 0) * jnp.concatenate([weight, weight], axis=1)
    work[...] = along_y(value, 2)
    extra = None
    for plane in reversed(range(PLANES)):
        rows = work[pl.ds(plane * NX, NX), :]
        cr, ci, sr, si = along_x(rows[:, :128], rows[:, 128:])
        real, imag = cr - si, ci + sr
        if plane == 12:
            extra = real
        else:
            p, i = divmod(plane, 4)
            if i == 0:
                imag = imag * (1.0 - flags[p]) + extra * flags[p]
            box[pl.ds((8 * p + i) * NX, NX), :] = real
            box[pl.ds((8 * p + 4 + i) * NX, NX), :] = imag


def intersect(total, bands_ref, partial_ref):
    lines = []
    for b in range(BLK):
        product = (bands_ref[b] * total).reshape(36, 8, 128)
        line = jnp.sum(jnp.sum(product, axis=0), axis=0, keepdims=True)
        line = line + turn(line, 64)
        lines.append(line + turn(line, 32))
    quarter = lanes((1, 128)) // 32
    row = lines[0]
    for b in range(1, BLK):
        row = jnp.where(quarter == b, lines[b], row)
    partial_ref[...] = row * SPACING**3


AROUND = [((1, -2, 3, -1, 2, -3, 4)[k % 7], (0, 2, 1, 3)[k % 4]) for k in range(28)] + [(0, turned) for turned in (2, 1, 3)]
STEPS = (AROUND, AROUND + [(0, 0)])


class Ring:
    def __init__(self, me, group, source, target, send_sem, recv_sem):
        self.source, self.target = source, target
        self.send_sem, self.recv_sem = send_sem, recv_sem
        self.me = me
        self.groups = [group, group + 1 - 2 * lax.rem(group, 2)]
        self.places = [lax.rem(me // 4 + k, 8) for k in range(8)]
        self.parts = [lax.rem(lax.rem(me, 4) + k, 4) for k in range(4)]

    def device(self, chunk, far, turned):
        return {"band": self.groups[chunk], "fft": 4 * self.places[far % 8] + self.parts[turned % 4]}

    def copy(self, source, target, peer, k):
        return pltpu.make_async_remote_copy(
            src_ref=source, dst_ref=target, send_sem=self.send_sem.at[k], recv_sem=self.recv_sem.at[k],
            device_id=peer, device_id_type=MESH,
        )

    def start(self, chunk, first, count, k, low=0, high=FFT):
        rows = pl.ds(first, count)
        for far, turned in STEPS[chunk][low:high]:
            peer = self.device(chunk, far, turned)
            self.copy(self.source.at[chunk, peer["fft"], rows], self.target.at[chunk, self.me, rows], peer, k).start()
        if chunk == 0:
            self.target[chunk, self.me, first:first + count] = self.source[chunk, self.me, first:first + count]

    def wait_recv(self, chunk, first, count, k):
        whole = self.target.at[chunk, pl.ds(0, len(STEPS[chunk])), pl.ds(first, count)]
        self.copy(whole, whole, self.device(chunk, 1, 0), k).wait_recv()

    def wait_send(self, chunk, first, count, k):
        whole = self.source.at[chunk, pl.ds(0, len(STEPS[chunk])), pl.ds(first, count)]
        self.copy(whole, whole, self.device(chunk, 1, 0), k).wait_send()


def whole_kernel(
    picked_ref, shells_ref, orbitals_far, forward_far, inverse_far, xy_far, x_far, y_far,
    result_ref,
    orbitals_ref, forward_ref, inverse_ref, xy_ref, x_ref, y_ref, fetch_sem,
    own, order, upper, lower, up, down, above, below, mine, sent, got, back, returned, tails, box, work, gain, pad,
    partial, ring_slots, near, near_slots,
    there_send, there_recv, home_send, home_recv, band_send, band_recv, ring_send, ring_recv, near_send, near_recv,
):
    me = lax.axis_index("fft")
    group = lax.axis_index("band")
    count = lax.axis_size("band")
    above_me, below_me = lax.rem(group + 1, count), lax.rem(group + count - 1, count)

    barrier = pltpu.get_barrier_semaphore()
    for peer in (above_me, below_me):
        pl.semaphore_signal(barrier, inc=1, device_id={"band": peer}, device_id_type=MESH)
    there = Ring(me, group, sent, got, there_send, there_recv)
    home = Ring(me, group, back, returned, home_send, home_recv)
    for chunk in range(2):
        for far, turned in AROUND:
            pl.semaphore_signal(barrier, inc=1, device_id=there.device(chunk, far, turned), device_id_type=MESH)

    def to_band(source, target, peer, k):
        return pltpu.make_async_remote_copy(
            src_ref=source, dst_ref=target, send_sem=band_send.at[k], recv_sem=band_recv.at[k],
            device_id={"band": peer}, device_id_type=MESH,
        )

    chosen_up = to_band(order.at[0], lower, above_me, 0)
    chosen_down = to_band(order.at[0], upper, below_me, 1)
    sum_down = to_band(down, above, below_me, 2)
    main, tail = pl.ds(0, NZ), pl.ds(NZ, NZ // 3)
    sum_up_main = to_band(up.at[main], below.at[main], above_me, 3)
    sum_up_tail = to_band(up.at[tail], below.at[tail], above_me, 4)

    fetches = [
        pltpu.make_async_copy(far, ref, fetch_sem.at[k])
        for k, (far, ref) in enumerate(
            [
                (orbitals_far, orbitals_ref), (xy_far, xy_ref), (forward_far, forward_ref),
                (x_far, x_ref), (y_far, y_ref), (inverse_far, inverse_ref),
            ]
        )
    ]
    for one in fetches:
        one.start()
    picked = picked_ref[0]
    fetches[0].wait()
    pad[...] = jnp.zeros_like(pad)
    order[0] = turned_band(orbitals_ref[:, picked, :], pad)
    pl.semaphore_wait(barrier, 2 * FFT)
    chosen_up.start()
    order_bands(picked, orbitals_ref, own, order, pad)

    def gain_step(plane, carry):
        gain_of(me, plane, shells_ref, xy_ref, gain)
        return carry

    chosen_down.start()
    for one in fetches[1:]:
        one.wait()
    tails[pl.ds(NZ * FIELDS, 24), :] = jnp.zeros((24, 128), F32)
    put_rows(sent, NZ * FIELDS + 256, jnp.zeros((24, 128), F32))

    chosen_up.wait_recv()
    for f in range(3):
        spectrum_of(f, order, upper, lower, forward_ref, sent, tails)
    there.start(0, 0, 2, 0)
    chosen_down.wait_recv()
    spectrum_of(3, order, upper, lower, forward_ref, sent, tails)
    close_tails(0, sent, tails)
    there.start(0, 2, 2, 0)
    for f in range(4, FIELDS):
        spectrum_of(f, order, upper, lower, forward_ref, sent, tails)
    close_tails(1, sent, tails)
    there.start(1, 0, 4, 1)
    lax.fori_loop(0, 2 * PLANES, gain_step, 0)

    for chunk in range(2):
        there.wait_recv(chunk, 0, 4, chunk)
        open_rows(got, chunk, box)
        screen_planes(me, chunk, x_ref, y_ref, box, work, gain)
        close_rows(box, chunk, back)
        if chunk == 0:
            home.start(0, 0, 4, 0)
        else:
            home.start(1, 0, 4, 1, 0, 20)

    home.wait_recv(0, 0, 4, 0)
    open_tails(0, returned, tails)
    total = None
    for f in range(3):
        field = pack_field(z_transform(inverse_ref, jnp.concatenate([main_of(f, returned), tail_of(f, tails)], axis=1)))
        term = field * order[visitor_of(f)[1]]
        total = term if total is None else total + term
    down[...] = total
    sum_down.start()
    home.start(1, 0, 4, 1, 20)

    def up_part(rows, fields):
        total = None
        for f, field in fields:
            if f == 3:
                mine[rows, :] = field * upper[rows, :]
            term = field * order[visitor_of(f)[1], rows, :]
            total = term if total is None else total + term
        up[rows, :] = total

    home.wait_recv(1, 0, 4, 1)
    up_part(main, [(f, z_transform(inverse_ref, main_of(f, returned))) for f in range(3, FIELDS)])
    sum_up_main.start()
    open_tails(1, returned, tails)
    up_part(tail, [(f, pack_thirds(z_transform(inverse_ref, tail_of(f, tails)))) for f in range(3, FIELDS)])
    sum_up_tail.start()
    sum_down.wait_recv()
    mine[...] += above[...]
    sum_up_main.wait_recv()
    sum_up_tail.wait_recv()
    total = mine[...] + below[...]
    result_ref[:288, :] = total
    intersect(total, own, partial)

    place, part = me // 4, lax.rem(me, 4)

    def row_to(source, target, peer, send_sem, recv_sem):
        return pltpu.make_async_remote_copy(
            src_ref=source, dst_ref=target, send_sem=send_sem, recv_sem=recv_sem,
            device_id={"fft": peer}, device_id_type=MESH,
        )

    ring = [
        row_to(partial, ring_slots.at[k], 4 * lax.rem(place + k, 8) + part, ring_send.at[k], ring_recv.at[k])
        for k in range(1, 8)
    ]
    for one in ring:
        one.start()
    row = partial[...]
    for k, one in enumerate(ring):
        one.wait()
        row = row + ring_slots[k + 1]
    near[...] = row
    beside = [
        row_to(near, near_slots.at[k], 4 * place + lax.rem(part + k, 4), near_send.at[k], near_recv.at[k])
        for k in range(1, 4)
    ]
    for one in beside:
        one.start()
    for k, one in enumerate(beside):
        one.wait()
        row = row + near_slots[k + 1]
    result_ref[288:, :] = jnp.broadcast_to(row, (8, 128))

    there.wait_send(0, 0, 4, 0)
    there.wait_send(1, 0, 4, 1)
    home.wait_send(0, 0, 4, 0)
    home.wait_send(1, 0, 4, 1)
    for one in (chosen_up, chosen_down, sum_down, sum_up_main, sum_up_tail):
        one.wait_send()


def last_kernel(given_ref, potential_ref, result_ref, pad_ref):
    pad_ref[...] = jnp.zeros_like(pad_ref)
    pad_ref[:NZ, :] = unpack_field(given_ref[:288, :])
    potential_ref[:, 0, :] = jnp.transpose(pad_ref[...])[:ROWS, :NZ]
    row = given_ref[288:289, :]
    lane = lanes((1, BLK))
    result = jnp.zeros((1, BLK), F32)
    for b in range(BLK):
        mine = lanes((1, 128)) // 32 == b
        result = jnp.where(lane == b, jnp.sum(jnp.where(mine, row, 0.0), axis=1, keepdims=True), result)
    result_ref[...] = result


def vm():
    return pl.BlockSpec(memory_space=pltpu.VMEM)


def sm():
    return pl.BlockSpec(memory_space=pltpu.SMEM)


def params(**extra):
    return pltpu.CompilerParams(vmem_limit_bytes=VMEM_LIMIT, **extra)


def shape(*dims):
    return jax.ShapeDtypeStruct(dims, F32)


def body(orbitals, picked, shells):
    forward, inverse = z_stacks()
    along_x, along_y = x_table(), y_tables()
    exchange = pltpu.VMEM((2, FFT, 4, 8, 128), F32)
    field = pltpu.VMEM((288, 128), F32)
    bands = pltpu.VMEM((BLK, 288, 128), F32)
    line = pltpu.VMEM((1, 128), F32)
    dma = pltpu.SemaphoreType.DMA
    given = pl.pallas_call(
        whole_kernel,
        out_shape=shape(296, 128),
        in_specs=[sm(), sm()] + [pl.BlockSpec(memory_space=pltpu.HBM)] * 6,
        out_specs=vm(),
        scratch_shapes=[
            pltpu.VMEM((ROWS, BLK, NZ), F32),
            pltpu.VMEM(forward.shape, BF16),
            pltpu.VMEM(inverse.shape, BF16),
            pltpu.VMEM((NX, 128), F32),
            pltpu.VMEM(along_x.shape, BF16),
            pltpu.VMEM(along_y.shape, BF16),
            dma((6,)),
            bands,
            bands,
        ]
        + [field] * 7
        + [exchange] * 4
        + [
            pltpu.VMEM((1536, 128), F32),
            pltpu.VMEM((24 * NX, 128), F32),
            pltpu.VMEM((PLANES * NX, 256), F32),
            pltpu.VMEM((2 * PLANES * NX, 128), F32),
            pltpu.VMEM((256, 256), F32),
            line,
            pltpu.VMEM((8, 1, 128), F32),
            line,
            pltpu.VMEM((4, 1, 128), F32),
        ]
        + [dma((2,))] * 2
        + [dma((2,))] * 2
        + [dma((5,))] * 2
        + [dma((8,))] * 2
        + [dma((4,))] * 2,
        compiler_params=params(collective_id=0, has_side_effects=True),
    )(
        picked, shells, jnp.transpose(orbitals, (1, 0, 2)), jnp.asarray(forward), jnp.asarray(inverse),
        jnp.asarray(xy_square()), jnp.asarray(along_x), jnp.asarray(along_y),
    )
    potentials, result = pl.pallas_call(
        last_kernel,
        out_shape=(shape(ROWS, 1, NZ), shape(1, BLK)),
        in_specs=[vm()],
        out_specs=(vm(), vm()),
        scratch_shapes=[pltpu.VMEM((256, 256), F32)],
        compiler_params=params(),
    )(given)
    return jnp.transpose(potentials, (1, 0, 2)), jnp.transpose(result)


def solution(mesh):
    return jax.shard_map(
        body,
        mesh=mesh,
        in_specs=(P("band", "fft", None), P("band"), P()),
        out_specs=(P("band", "fft", None), P("band", None)),
        check_vma=False,
    )
```

```python
import math

import jax
import jax.numpy as jnp
import numpy as np
from jax import lax
from jax.experimental import pallas as pl
from jax.experimental.pallas import tpu as pltpu
from jax.sharding import PartitionSpec as P

NX = 72
NY = 72
NZ = 216
BLK = 4
NSHELL = 64
FIELDS = 7
FFT = 32
ROWS = 162
MAIN = 128
TAIL = ROWS - MAIN
SLABS = 9
PLANES = 13

SPACING = 0.2
SCREENING = 0.106
FRACTION = 0.25
SPAN = math.lcm(NX, NY, NZ)
QTOP = (SPAN // NX) ** 2 * (NX // 2) ** 2 + (SPAN // NY) ** 2 * (NY // 2) ** 2 + (SPAN // NZ) ** 2 * (NZ // 2) ** 2
MESH = pl.DeviceIdType.MESH
F32 = jnp.float32
BF16 = jnp.bfloat16
VMEM_LIMIT = 60 * 1024 * 1024


def halves(table):
    table = np.asarray(table, np.float32)
    high = table.astype(jnp.bfloat16)
    low = (table - high.astype(np.float32)).astype(jnp.bfloat16)
    return high, low


def z_tables():
    freq, is_sin = np.zeros(NZ, np.int64), np.zeros(NZ, bool)
    for t in range(NZ // 8):
        for i in range(4):
            freq[8 * t + i] = 4 * t + i
            freq[8 * t + 4 + i] = 4 * t + i
            is_sin[8 * t + 4 + i] = True
    freq[4], is_sin[4] = NZ // 2, False
    angle = 2 * np.pi * (freq[:, None] * np.arange(NZ)[None, :] % NZ) / NZ
    forward = np.where(is_sin[:, None], -np.sin(angle), np.cos(angle))
    weight = np.where((freq == 0) | (freq == NZ // 2), 1.0, 2.0) / (NX * NY * NZ)
    inverse = (-FRACTION * weight[:, None] * forward).T
    return forward, inverse


def z_stacks():
    forward, inverse = z_tables()
    pad = np.zeros((8, NZ), jnp.bfloat16)

    def stack(table):
        high, low = halves(table)
        return np.concatenate([high, pad, low, pad], axis=0)

    return stack(forward), stack(inverse)


def xy_angle():
    index = np.arange(NX)
    return 2 * np.pi * (index[:, None] * index[None, :] % NX) / NX


def x_table():
    table = np.concatenate([np.cos(xy_angle()), np.sin(xy_angle())], axis=0)
    high, low = halves(table)
    pad = np.zeros((2 * NX, 8), high.dtype)
    return np.concatenate([high, pad, low, pad, high, pad], axis=1)


def y_tables():
    cosine, sine = np.cos(xy_angle()), np.sin(xy_angle())
    forward = np.zeros((256, 256))
    forward[:NY, :NY] = cosine
    forward[128:128 + NY, 128:128 + NY] = cosine
    forward[:NY, 128:128 + NY] = -sine
    forward[128:128 + NY, :NY] = sine
    fh, fl = halves(forward)
    return np.stack([fh, fl, fh.T, fl.T])


def xy_square():
    index = np.arange(NX)
    signed = np.where(index > NX // 2, index - NX, index)
    square = np.zeros((NX, 128), np.float32)
    square[:, :NY] = 9 * (signed[:, None] ** 2 + signed[None, :] ** 2)
    return square


def split(value):
    high = value.astype(BF16)
    return high, (value - high.astype(F32)).astype(BF16)


def mm(left, right):
    return lax.dot_general(left, right, (((1,), (0,)), ((), ())), preferred_element_type=F32)


def lanes(shape):
    return lax.broadcasted_iota(jnp.int32, shape, len(shape) - 1)


def turn(value, shift):
    shift = shift % 128
    return value if shift == 0 else pltpu.roll(value, shift, 1)


def pack_tail(parts):
    lane = lanes(parts[0].shape)
    upper = jnp.where(lane < 2 * TAIL, turn(parts[1], TAIL), turn(parts[2], 2 * TAIL))
    return jnp.where(lane < TAIL, parts[0], upper)


def pack_thirds(tail):
    third = NZ // 3
    return pack_tail([tail[third * g:third * (g + 1)] for g in range(3)])


def pack_field(wide):
    return jnp.concatenate([wide[:, :MAIN], pack_thirds(wide[:, MAIN:])], axis=0)


def unpack_field(packed):
    tail = packed[NZ:]
    tails = jnp.concatenate([turn(tail, -TAIL * g) for g in range(3)], axis=0)
    return jnp.concatenate([packed[:NZ], tails], axis=1)


def z_transform(table_ref, wide):
    high, low = split(wide)
    both = mm(table_ref[...], high)
    return both[:NZ] + both[NZ + 8:2 * NZ + 8] + mm(table_ref[:NZ + 8], low)[:NZ]


def turned_band(band, pad_ref):
    pad_ref[:ROWS, :NZ] = band
    return pack_field(jnp.transpose(pad_ref[...])[:NZ])


def order_bands(picked, orbitals_ref, own_ref, order_ref, pad_ref):
    for b in range(BLK):
        own_ref[b] = turned_band(orbitals_ref[:, b, :], pad_ref)
    for j in range(1, BLK):
        order_ref[j] = jnp.where(picked >= j, own_ref[j - 1], own_ref[j])


def visitor_of(f):
    return (True, f + 1) if f < 3 else (False, f - 3)


def cuts_of(f):
    result = []
    for chunk in range(2):
        low, high = max(NZ * f, 768 * chunk), min(NZ * (f + 1), 768 * (chunk + 1))
        if low < high:
            result.append((low, high - low, low + 256 * chunk))
    return result


def runs(row, rows):
    tile, count = row // 8, rows // 8
    done = 0
    while done < count:
        place, peer = divmod(tile + done, FFT)
        take = min(count - done, FFT - peer)
        yield place // 4, place % 4, peer, take, done
        done += take


def put_rows(buffer, row, value):
    tiles = value.reshape(value.shape[0] // 8, 8, 128)
    for chunk, part, peer, take, done in runs(row, value.shape[0]):
        buffer[chunk, peer:peer + take, part] = tiles[done:done + take]


def get_rows(buffer, row, rows):
    parts = [buffer[chunk, peer:peer + take, part].reshape(8 * take, 128) for chunk, part, peer, take, _ in runs(row, rows)]
    return parts[0] if len(parts) == 1 else jnp.concatenate(parts, axis=0)


def spectrum_of(f, order_ref, upper_ref, lower_ref, table_ref, buffer, tail_ref):
    low_side, j = visitor_of(f)
    density = (lower_ref if low_side else upper_ref)[...] * order_ref[j]
    spectrum = z_transform(table_ref, unpack_field(density))
    for low, count, place in cuts_of(f):
        first = low - NZ * f
        put_rows(buffer, place, spectrum[first:first + count, :MAIN])
        tail_ref[pl.ds(low, count), :] = spectrum[first:first + count, MAIN:]


def close_tails(chunk, buffer, tail_ref):
    parts = [tail_ref[pl.ds(768 * chunk + 256 * p, 256), :] for p in range(3)]
    put_rows(buffer, 1024 * chunk + 768, pack_tail(parts))


def open_tails(chunk, buffer, tail_ref):
    tails = get_rows(buffer, 1024 * chunk + 768, 256)
    for p in range(3):
        tail_ref[pl.ds(768 * chunk + 256 * p, 256), :] = turn(tails, -TAIL * p)


def main_of(f, buffer):
    mains = [get_rows(buffer, place, count) for _, count, place in cuts_of(f)]
    return mains[0] if len(mains) == 1 else jnp.concatenate(mains, axis=0)


def tail_of(f, tail_ref):
    return tail_ref[pl.ds(NZ * f, NZ), :]


def pieces():
    result = []
    row = 0
    while row < 4 * ROWS:
        source, j = divmod(row, ROWS)
        slab, y = divmod(row, NY)
        stop = min((source + 1) * ROWS, (slab + 1) * NY)
        if j < MAIN:
            stop = min(stop, source * ROWS + MAIN)
        result.append((source, j >= MAIN, j if j < MAIN else j - MAIN, slab, y, stop - row))
        row = stop
    return result


def tile_of(owner, chunk, p):
    return lax.rem(96 * chunk + 32 * p + owner, NZ // 8)


def gain_of(owner, plane, shells_ref, xy_ref, gain):
    chunk, place = plane // PLANES, lax.rem(plane, PLANES)
    depth = jnp.where(place == PLANES - 1, NZ // 2, 4 * tile_of(owner, chunk, place // 4) + lax.rem(place, 4))
    square = xy_ref[...] + (depth * depth).astype(F32)
    total = jnp.full(square.shape, shells_ref[0].astype(F32), F32)
    for s in range(1, NSHELL):
        step = (shells_ref[s] - shells_ref[s - 1]).astype(F32)
        total = total + jnp.where(square >= float(-(-s * (QTOP + 1) // NSHELL)), step, 0.0)
    g_squared = (2.0 * math.pi / (SPACING * SPAN)) ** 2 * square
    safe = jnp.where(square == 0, 1.0, g_squared)
    value = 4.0 * math.pi / safe * (1.0 - jnp.exp(-safe / (4.0 * SCREENING**2)))
    gain[pl.ds(pl.multiple_of(plane * NX, 8), NX), :] = total * jnp.where(square == 0, math.pi / SCREENING**2, value)


def open_rows(got_ref, chunk, box):
    cuts = pieces()
    lane = lanes((8, 128))

    def one(chip, carry):
        for slab in range(SLABS):
            mine = [c for c in cuts if c[3] == slab]
            for p in range(3):
                value = None
                for source, tail, first, _, y, _ in mine:
                    part = got_ref[chunk, 4 * chip + source, 3 if tail else p]
                    part = turn(part, y - first - (TAIL * p if tail else 0))
                    value = part if value is None else jnp.where(lane >= y, part, value)
                box[pl.ds(8 * p * NX + SLABS * chip + slab, 8, stride=NX), :] = value
        return carry

    lax.fori_loop(0, 8, one, 0)


def close_rows(box, chunk, send_ref):
    cuts = pieces()
    lane = lanes((8, 128))

    def one(chip, carry):
        fields = [[box[pl.ds(8 * p * NX + SLABS * chip + slab, 8, stride=NX), :] for slab in range(SLABS)] for p in range(3)]
        for source in range(4):
            tail_value = None
            for p in range(3):
                value = None
                for s, tail, first, slab, y, _ in cuts:
                    if s != source:
                        continue
                    if tail:
                        place = first + TAIL * p
                        part = turn(fields[p][slab], place - y)
                        tail_value = part if tail_value is None else jnp.where(lane >= place, part, tail_value)
                    else:
                        part = turn(fields[p][slab], first - y)
                        value = part if value is None else jnp.where(lane >= first, part, value)
                send_ref[chunk, 4 * chip + source, p] = value
            send_ref[chunk, 4 * chip + source, 3] = tail_value
        return carry

    lax.fori_loop(0, 8, one, 0)


def screen_planes(owner, chunk, x_ref, y_ref, box, work, gain):
    flags = [jnp.where(tile_of(owner, chunk, p) == 0, 1.0, 0.0).astype(F32) for p in range(3)]

    def along_x(real, imag):
        wide = jnp.concatenate([real, imag], axis=1)
        wide = jnp.concatenate([wide, jnp.zeros((8, 256), F32)], axis=0)
        high, low = split(wide)
        both = mm(x_ref[...], jnp.concatenate([high, high, low], axis=0))
        return both[:NX, :128], both[:NX, 128:], both[NX:, :128], both[NX:, 128:]

    def along_y(value, k):
        high, low = split(value)
        return mm(high, y_ref[k]) + mm(low, y_ref[k]) + mm(high, y_ref[k + 1])

    for plane in range(PLANES):
        if plane == 12:
            real = sum(flags[p] * box[pl.ds((8 * p + 4) * NX, NX), :] for p in range(3))
            imag = jnp.zeros_like(real)
        else:
            p, i = divmod(plane, 4)
            real = box[pl.ds((8 * p + i) * NX, NX), :]
            imag = box[pl.ds((8 * p + 4 + i) * NX, NX), :]
            if i == 0:
                imag = imag * (1.0 - flags[p])
        cr, ci, sr, si = along_x(real, imag)
        work[pl.ds(plane * NX, NX), :] = jnp.concatenate([cr + si, ci - sr], axis=1)
    weight = gain[pl.ds(chunk * PLANES * NX, PLANES * NX), :]
    value = along_y(work[...], 0) * jnp.concatenate([weight, weight], axis=1)
    work[...] = along_y(value, 2)
    extra = None
    for plane in reversed(range(PLANES)):
        rows = work[pl.ds(plane * NX, NX), :]
        cr, ci, sr, si = along_x(rows[:, :128], rows[:, 128:])
        real, imag = cr - si, ci + sr
        if plane == 12:
            extra = real
        else:
            p, i = divmod(plane, 4)
            if i == 0:
                imag = imag * (1.0 - flags[p]) + extra * flags[p]
            box[pl.ds((8 * p + i) * NX, NX), :] = real
            box[pl.ds((8 * p + 4 + i) * NX, NX), :] = imag


def intersect(total, bands_ref, partial_ref):
    lines = []
    for b in range(BLK):
        product = (bands_ref[b] * total).reshape(36, 8, 128)
        line = jnp.sum(jnp.sum(product, axis=0), axis=0, keepdims=True)
        line = line + turn(line, 64)
        lines.append(line + turn(line, 32))
    quarter = lanes((1, 128)) // 32
    row = lines[0]
    for b in range(1, BLK):
        row = jnp.where(quarter == b, lines[b], row)
    partial_ref[...] = row * SPACING**3


AROUND = [((1, -2, 3, -1, 2, -3, 4)[k % 7], (0, 2, 1, 3)[k % 4]) for k in range(28)] + [(0, turned) for turned in (2, 1, 3)]
STEPS = (AROUND, AROUND + [(0, 0)])


class Ring:
    def __init__(self, me, group, source, target, send_sem, recv_sem):
        self.source, self.target = source, target
        self.send_sem, self.recv_sem = send_sem, recv_sem
        self.me = me
        self.groups = [group, group + 1 - 2 * lax.rem(group, 2)]
        self.places = [lax.rem(me // 4 + k, 8) for k in range(8)]
        self.parts = [lax.rem(lax.rem(me, 4) + k, 4) for k in range(4)]

    def device(self, chunk, far, turned):
        return {"band": self.groups[chunk], "fft": 4 * self.places[far % 8] + self.parts[turned % 4]}

    def copy(self, source, target, peer, k):
        return pltpu.make_async_remote_copy(
            src_ref=source, dst_ref=target, send_sem=self.send_sem.at[k], recv_sem=self.recv_sem.at[k],
            device_id=peer, device_id_type=MESH,
        )

    def start(self, chunk, first, count, k, low=0, high=FFT):
        rows = pl.ds(first, count)
        for far, turned in STEPS[chunk][low:high]:
            peer = self.device(chunk, far, turned)
            self.copy(self.source.at[chunk, peer["fft"], rows], self.target.at[chunk, self.me, rows], peer, k).start()
        if chunk == 0:
            self.target[chunk, self.me, first:first + count] = self.source[chunk, self.me, first:first + count]

    def wait_recv(self, chunk, first, count, k):
        whole = self.target.at[chunk, pl.ds(0, len(STEPS[chunk])), pl.ds(first, count)]
        self.copy(whole, whole, self.device(chunk, 1, 0), k).wait_recv()

    def wait_send(self, chunk, first, count, k):
        whole = self.source.at[chunk, pl.ds(0, len(STEPS[chunk])), pl.ds(first, count)]
        self.copy(whole, whole, self.device(chunk, 1, 0), k).wait_send()


def whole_kernel(
    picked_ref, shells_ref, orbitals_far, forward_far, inverse_far, xy_far, x_far, y_far,
    result_ref,
    orbitals_ref, forward_ref, inverse_ref, xy_ref, x_ref, y_ref, fetch_sem,
    own, order, upper, lower, up, down, above, below, mine, sent, got, back, returned, tails, box, work, gain, pad,
    partial, ring_slots, near, near_slots,
    there_send, there_recv, home_send, home_recv, band_send, band_recv, ring_send, ring_recv, near_send, near_recv,
):
    me = lax.axis_index("fft")
    group = lax.axis_index("band")
    count = lax.axis_size("band")
    above_me, below_me = lax.rem(group + 1, count), lax.rem(group + count - 1, count)

    barrier = pltpu.get_barrier_semaphore()
    for peer in (above_me, below_me):
        pl.semaphore_signal(barrier, inc=1, device_id={"band": peer}, device_id_type=MESH)
    there = Ring(me, group, sent, got, there_send, there_recv)
    home = Ring(me, group, back, returned, home_send, home_recv)
    for chunk in range(2):
        for far, turned in AROUND:
            pl.semaphore_signal(barrier, inc=1, device_id=there.device(chunk, far, turned), device_id_type=MESH)

    def to_band(source, target, peer, k):
        return pltpu.make_async_remote_copy(
            src_ref=source, dst_ref=target, send_sem=band_send.at[k], recv_sem=band_recv.at[k],
            device_id={"band": peer}, device_id_type=MESH,
        )

    chosen_up = to_band(order.at[0], lower, above_me, 0)
    chosen_down = to_band(order.at[0], upper, below_me, 1)
    sum_down = to_band(down, above, below_me, 2)
    main, tail = pl.ds(0, NZ), pl.ds(NZ, NZ // 3)
    sum_up_main = to_band(up.at[main], below.at[main], above_me, 3)
    sum_up_tail = to_band(up.at[tail], below.at[tail], above_me, 4)

    fetches = [
        pltpu.make_async_copy(far, ref, fetch_sem.at[k])
        for k, (far, ref) in enumerate(
            [
                (orbitals_far, orbitals_ref), (xy_far, xy_ref), (forward_far, forward_ref),
                (x_far, x_ref), (y_far, y_ref), (inverse_far, inverse_ref),
            ]
        )
    ]
    for one in fetches:
        one.start()
    picked = picked_ref[0]
    fetches[0].wait()
    pad[...] = jnp.zeros_like(pad)
    order[0] = turned_band(orbitals_ref[:, picked, :], pad)
    pl.semaphore_wait(barrier, 2 * FFT)
    chosen_up.start()
    order_bands(picked, orbitals_ref, own, order, pad)

    def gain_step(plane, carry):
        gain_of(me, plane, shells_ref, xy_ref, gain)
        return carry

    chosen_down.start()
    for one in fetches[1:]:
        one.wait()
    tails[pl.ds(NZ * FIELDS, 24), :] = jnp.zeros((24, 128), F32)
    put_rows(sent, NZ * FIELDS + 256, jnp.zeros((24, 128), F32))

    chosen_up.wait_recv()
    for f in range(3):
        spectrum_of(f, order, upper, lower, forward_ref, sent, tails)
    chosen_down.wait_recv()
    spectrum_of(3, order, upper, lower, forward_ref, sent, tails)
    close_tails(0, sent, tails)
    there.start(0, 0, 4, 0)
    for f in range(4, FIELDS):
        spectrum_of(f, order, upper, lower, forward_ref, sent, tails)
    close_tails(1, sent, tails)
    there.start(1, 0, 4, 1)
    lax.fori_loop(0, 2 * PLANES, gain_step, 0)

    for chunk in range(2):
        there.wait_recv(chunk, 0, 4, chunk)
        open_rows(got, chunk, box)
        screen_planes(me, chunk, x_ref, y_ref, box, work, gain)
        close_rows(box, chunk, back)
        if chunk == 0:
            home.start(0, 0, 4, 0)
        else:
            home.start(1, 0, 4, 1, 0, 20)

    home.wait_recv(0, 0, 4, 0)
    open_tails(0, returned, tails)
    total = None
    for f in range(3):
        field = pack_field(z_transform(inverse_ref, jnp.concatenate([main_of(f, returned), tail_of(f, tails)], axis=1)))
        term = field * order[visitor_of(f)[1]]
        total = term if total is None else total + term
    down[...] = total
    sum_down.start()
    home.start(1, 0, 4, 1, 20)

    def up_part(rows, fields):
        total = None
        for f, field in fields:
            if f == 3:
                mine[rows, :] = field * upper[rows, :]
            term = field * order[visitor_of(f)[1], rows, :]
            total = term if total is None else total + term
        up[rows, :] = total

    home.wait_recv(1, 0, 4, 1)
    up_part(main, [(f, z_transform(inverse_ref, main_of(f, returned))) for f in range(3, FIELDS)])
    sum_up_main.start()
    open_tails(1, returned, tails)
    up_part(tail, [(f, pack_thirds(z_transform(inverse_ref, tail_of(f, tails)))) for f in range(3, FIELDS)])
    sum_up_tail.start()
    sum_down.wait_recv()
    mine[...] += above[...]
    sum_up_main.wait_recv()
    sum_up_tail.wait_recv()
    total = mine[...] + below[...]
    result_ref[:288, :] = total
    intersect(total, own, partial)

    place, part = me // 4, lax.rem(me, 4)

    def row_to(source, target, peer, send_sem, recv_sem):
        return pltpu.make_async_remote_copy(
            src_ref=source, dst_ref=target, send_sem=send_sem, recv_sem=recv_sem,
            device_id={"fft": peer}, device_id_type=MESH,
        )

    ring = [
        row_to(partial, ring_slots.at[k], 4 * lax.rem(place + k, 8) + part, ring_send.at[k], ring_recv.at[k])
        for k in range(1, 8)
    ]
    for one in ring:
        one.start()
    row = partial[...]
    for k, one in enumerate(ring):
        one.wait()
        row = row + ring_slots[k + 1]
    near[...] = row
    beside = [
        row_to(near, near_slots.at[k], 4 * place + lax.rem(part + k, 4), near_send.at[k], near_recv.at[k])
        for k in range(1, 4)
    ]
    for one in beside:
        one.start()
    for k, one in enumerate(beside):
        one.wait()
        row = row + near_slots[k + 1]
    result_ref[288:, :] = jnp.broadcast_to(row, (8, 128))

    there.wait_send(0, 0, 4, 0)
    there.wait_send(1, 0, 4, 1)
    home.wait_send(0, 0, 4, 0)
    home.wait_send(1, 0, 4, 1)
    for one in (chosen_up, chosen_down, sum_down, sum_up_main, sum_up_tail):
        one.wait_send()


def last_kernel(given_ref, potential_ref, result_ref, pad_ref):
    pad_ref[...] = jnp.zeros_like(pad_ref)
    pad_ref[:NZ, :] = unpack_field(given_ref[:288, :])
    potential_ref[:, 0, :] = jnp.transpose(pad_ref[...])[:ROWS, :NZ]
    row = given_ref[288:289, :]
    lane = lanes((1, BLK))
    result = jnp.zeros((1, BLK), F32)
    for b in range(BLK):
        mine = lanes((1, 128)) // 32 == b
        result = jnp.where(lane == b, jnp.sum(jnp.where(mine, row, 0.0), axis=1, keepdims=True), result)
    result_ref[...] = result


def vm():
    return pl.BlockSpec(memory_space=pltpu.VMEM)


def sm():
    return pl.BlockSpec(memory_space=pltpu.SMEM)


def params(**extra):
    return pltpu.CompilerParams(vmem_limit_bytes=VMEM_LIMIT, **extra)


def shape(*dims):
    return jax.ShapeDtypeStruct(dims, F32)


def body(orbitals, picked, shells):
    forward, inverse = z_stacks()
    along_x, along_y = x_table(), y_tables()
    exchange = pltpu.VMEM((2, FFT, 4, 8, 128), F32)
    field = pltpu.VMEM((288, 128), F32)
    bands = pltpu.VMEM((BLK, 288, 128), F32)
    line = pltpu.VMEM((1, 128), F32)
    dma = pltpu.SemaphoreType.DMA
    given = pl.pallas_call(
        whole_kernel,
        out_shape=shape(296, 128),
        in_specs=[sm(), sm()] + [pl.BlockSpec(memory_space=pltpu.HBM)] * 6,
        out_specs=vm(),
        scratch_shapes=[
            pltpu.VMEM((ROWS, BLK, NZ), F32),
            pltpu.VMEM(forward.shape, BF16),
            pltpu.VMEM(inverse.shape, BF16),
            pltpu.VMEM((NX, 128), F32),
            pltpu.VMEM(along_x.shape, BF16),
            pltpu.VMEM(along_y.shape, BF16),
            dma((6,)),
            bands,
            bands,
        ]
        + [field] * 7
        + [exchange] * 4
        + [
            pltpu.VMEM((1536, 128), F32),
            pltpu.VMEM((24 * NX, 128), F32),
            pltpu.VMEM((PLANES * NX, 256), F32),
            pltpu.VMEM((2 * PLANES * NX, 128), F32),
            pltpu.VMEM((256, 256), F32),
            line,
            pltpu.VMEM((8, 1, 128), F32),
            line,
            pltpu.VMEM((4, 1, 128), F32),
        ]
        + [dma((2,))] * 2
        + [dma((2,))] * 2
        + [dma((5,))] * 2
        + [dma((8,))] * 2
        + [dma((4,))] * 2,
        compiler_params=params(collective_id=0, has_side_effects=True),
    )(
        picked, shells, jnp.transpose(orbitals, (1, 0, 2)), jnp.asarray(forward), jnp.asarray(inverse),
        jnp.asarray(xy_square()), jnp.asarray(along_x), jnp.asarray(along_y),
    )
    potentials, result = pl.pallas_call(
        last_kernel,
        out_shape=(shape(ROWS, 1, NZ), shape(1, BLK)),
        in_specs=[vm()],
        out_specs=(vm(), vm()),
        scratch_shapes=[pltpu.VMEM((256, 256), F32)],
        compiler_params=params(),
    )(given)
    return jnp.transpose(potentials, (1, 0, 2)), jnp.transpose(result)


def solution(mesh):
    return jax.shard_map(
        body,
        mesh=mesh,
        in_specs=(P("band", "fft", None), P("band"), P()),
        out_specs=(P("band", "fft", None), P("band", None)),
        check_vma=False,
    )
```

```python
import math

import jax
import jax.numpy as jnp
import numpy as np
from jax import lax
from jax.experimental import pallas as pl
from jax.experimental.pallas import tpu as pltpu
from jax.sharding import PartitionSpec as P

NX = 72
NY = 72
NZ = 216
BLK = 4
NSHELL = 64
FIELDS = 7
FFT = 32
ROWS = 162
MAIN = 128
TAIL = ROWS - MAIN
SLABS = 9
PLANES = 13

SPACING = 0.2
SCREENING = 0.106
FRACTION = 0.25
SPAN = math.lcm(NX, NY, NZ)
QTOP = (SPAN // NX) ** 2 * (NX // 2) ** 2 + (SPAN // NY) ** 2 * (NY // 2) ** 2 + (SPAN // NZ) ** 2 * (NZ // 2) ** 2
MESH = pl.DeviceIdType.MESH
F32 = jnp.float32
BF16 = jnp.bfloat16
VMEM_LIMIT = 60 * 1024 * 1024


def halves(table):
    table = np.asarray(table, np.float32)
    high = table.astype(jnp.bfloat16)
    low = (table - high.astype(np.float32)).astype(jnp.bfloat16)
    return high, low


def z_tables():
    freq, is_sin = np.zeros(NZ, np.int64), np.zeros(NZ, bool)
    for t in range(NZ // 8):
        for i in range(4):
            freq[8 * t + i] = 4 * t + i
            freq[8 * t + 4 + i] = 4 * t + i
            is_sin[8 * t + 4 + i] = True
    freq[4], is_sin[4] = NZ // 2, False
    angle = 2 * np.pi * (freq[:, None] * np.arange(NZ)[None, :] % NZ) / NZ
    forward = np.where(is_sin[:, None], -np.sin(angle), np.cos(angle))
    weight = np.where((freq == 0) | (freq == NZ // 2), 1.0, 2.0) / (NX * NY * NZ)
    inverse = (-FRACTION * weight[:, None] * forward).T
    return forward, inverse


def z_stacks():
    forward, inverse = z_tables()
    pad = np.zeros((8, NZ), jnp.bfloat16)

    def stack(table):
        high, low = halves(table)
        return np.concatenate([high, pad, low, pad], axis=0)

    return stack(forward), stack(inverse)


def xy_angle():
    index = np.arange(NX)
    return 2 * np.pi * (index[:, None] * index[None, :] % NX) / NX


def x_table():
    table = np.concatenate([np.cos(xy_angle()), np.sin(xy_angle())], axis=0)
    high, low = halves(table)
    pad = np.zeros((2 * NX, 8), high.dtype)
    return np.concatenate([high, pad, low, pad, high, pad], axis=1)


def y_tables():
    cosine, sine = np.cos(xy_angle()), np.sin(xy_angle())
    forward = np.zeros((256, 256))
    forward[:NY, :NY] = cosine
    forward[128:128 + NY, 128:128 + NY] = cosine
    forward[:NY, 128:128 + NY] = -sine
    forward[128:128 + NY, :NY] = sine
    fh, fl = halves(forward)
    return np.stack([fh, fl, fh.T, fl.T])


def xy_square():
    index = np.arange(NX)
    signed = np.where(index > NX // 2, index - NX, index)
    square = np.zeros((NX, 128), np.float32)
    square[:, :NY] = 9 * (signed[:, None] ** 2 + signed[None, :] ** 2)
    return square


def split(value):
    high = value.astype(BF16)
    return high, (value - high.astype(F32)).astype(BF16)


def mm(left, right):
    return lax.dot_general(left, right, (((1,), (0,)), ((), ())), preferred_element_type=F32)


def lanes(shape):
    return lax.broadcasted_iota(jnp.int32, shape, len(shape) - 1)


def turn(value, shift):
    shift = shift % 128
    return value if shift == 0 else pltpu.roll(value, shift, 1)


def pack_tail(parts):
    lane = lanes(parts[0].shape)
    upper = jnp.where(lane < 2 * TAIL, turn(parts[1], TAIL), turn(parts[2], 2 * TAIL))
    return jnp.where(lane < TAIL, parts[0], upper)


def pack_thirds(tail):
    third = NZ // 3
    return pack_tail([tail[third * g:third * (g + 1)] for g in range(3)])


def pack_field(wide):
    return jnp.concatenate([wide[:, :MAIN], pack_thirds(wide[:, MAIN:])], axis=0)


def unpack_field(packed):
    tail = packed[NZ:]
    tails = jnp.concatenate([turn(tail, -TAIL * g) for g in range(3)], axis=0)
    return jnp.concatenate([packed[:NZ], tails], axis=1)


def z_transform(table_ref, wide):
    high, low = split(wide)
    both = mm(table_ref[...], high)
    return both[:NZ] + both[NZ + 8:2 * NZ + 8] + mm(table_ref[:NZ + 8], low)[:NZ]


def turned_band(band, pad_ref):
    pad_ref[:ROWS, :NZ] = band
    return pack_field(jnp.transpose(pad_ref[...])[:NZ])


def order_bands(picked, orbitals_ref, own_ref, order_ref, pad_ref):
    for b in range(BLK):
        own_ref[b] = turned_band(orbitals_ref[:, b, :], pad_ref)
    for j in range(1, BLK):
        order_ref[j] = jnp.where(picked >= j, own_ref[j - 1], own_ref[j])


def visitor_of(f):
    return (True, f + 1) if f < 3 else (False, f - 3)


def cuts_of(f):
    result = []
    for chunk in range(2):
        low, high = max(NZ * f, 768 * chunk), min(NZ * (f + 1), 768 * (chunk + 1))
        if low < high:
            result.append((low, high - low, low + 256 * chunk))
    return result


def runs(row, rows):
    tile, count = row // 8, rows // 8
    done = 0
    while done < count:
        place, peer = divmod(tile + done, FFT)
        take = min(count - done, FFT - peer)
        yield place // 4, place % 4, peer, take, done
        done += take


def put_rows(buffer, row, value):
    tiles = value.reshape(value.shape[0] // 8, 8, 128)
    for chunk, part, peer, take, done in runs(row, value.shape[0]):
        buffer[chunk, peer:peer + take, part] = tiles[done:done + take]


def get_rows(buffer, row, rows):
    parts = [buffer[chunk, peer:peer + take, part].reshape(8 * take, 128) for chunk, part, peer, take, _ in runs(row, rows)]
    return parts[0] if len(parts) == 1 else jnp.concatenate(parts, axis=0)


def spectrum_of(f, order_ref, upper_ref, lower_ref, table_ref, buffer, tail_ref):
    low_side, j = visitor_of(f)
    density = (lower_ref if low_side else upper_ref)[...] * order_ref[j]
    spectrum = z_transform(table_ref, unpack_field(density))
    for low, count, place in cuts_of(f):
        first = low - NZ * f
        put_rows(buffer, place, spectrum[first:first + count, :MAIN])
        tail_ref[pl.ds(low, count), :] = spectrum[first:first + count, MAIN:]


def close_tails(chunk, buffer, tail_ref):
    parts = [tail_ref[pl.ds(768 * chunk + 256 * p, 256), :] for p in range(3)]
    put_rows(buffer, 1024 * chunk + 768, pack_tail(parts))


def open_tails(chunk, buffer, tail_ref):
    tails = get_rows(buffer, 1024 * chunk + 768, 256)
    for p in range(3):
        tail_ref[pl.ds(768 * chunk + 256 * p, 256), :] = turn(tails, -TAIL * p)


def main_of(f, buffer):
    mains = [get_rows(buffer, place, count) for _, count, place in cuts_of(f)]
    return mains[0] if len(mains) == 1 else jnp.concatenate(mains, axis=0)


def tail_of(f, tail_ref):
    return tail_ref[pl.ds(NZ * f, NZ), :]


def pieces():
    result = []
    row = 0
    while row < 4 * ROWS:
        source, j = divmod(row, ROWS)
        slab, y = divmod(row, NY)
        stop = min((source + 1) * ROWS, (slab + 1) * NY)
        if j < MAIN:
            stop = min(stop, source * ROWS + MAIN)
        result.append((source, j >= MAIN, j if j < MAIN else j - MAIN, slab, y, stop - row))
        row = stop
    return result


def tile_of(owner, chunk, p):
    return lax.rem(96 * chunk + 32 * p + owner, NZ // 8)


def gain_of(owner, plane, shells_ref, xy_ref, gain):
    chunk, place = plane // PLANES, lax.rem(plane, PLANES)
    depth = jnp.where(place == PLANES - 1, NZ // 2, 4 * tile_of(owner, chunk, place // 4) + lax.rem(place, 4))
    square = xy_ref[...] + (depth * depth).astype(F32)
    total = jnp.full(square.shape, shells_ref[0].astype(F32), F32)
    for s in range(1, NSHELL):
        step = (shells_ref[s] - shells_ref[s - 1]).astype(F32)
        total = total + jnp.where(square >= float(-(-s * (QTOP + 1) // NSHELL)), step, 0.0)
    g_squared = (2.0 * math.pi / (SPACING * SPAN)) ** 2 * square
    safe = jnp.where(square == 0, 1.0, g_squared)
    value = 4.0 * math.pi / safe * (1.0 - jnp.exp(-safe / (4.0 * SCREENING**2)))
    gain[pl.ds(pl.multiple_of(plane * NX, 8), NX), :] = total * jnp.where(square == 0, math.pi / SCREENING**2, value)


def open_rows(got_ref, chunk, box):
    cuts = pieces()
    lane = lanes((8, 128))

    def one(chip, carry):
        for slab in range(SLABS):
            mine = [c for c in cuts if c[3] == slab]
            for p in range(3):
                value = None
                for source, tail, first, _, y, _ in mine:
                    part = got_ref[chunk, 4 * chip + source, 3 if tail else p]
                    part = turn(part, y - first - (TAIL * p if tail else 0))
                    value = part if value is None else jnp.where(lane >= y, part, value)
                box[pl.ds(8 * p * NX + SLABS * chip + slab, 8, stride=NX), :] = value
        return carry

    lax.fori_loop(0, 8, one, 0)


def close_rows(box, chunk, send_ref):
    cuts = pieces()
    lane = lanes((8, 128))

    def one(chip, carry):
        fields = [[box[pl.ds(8 * p * NX + SLABS * chip + slab, 8, stride=NX), :] for slab in range(SLABS)] for p in range(3)]
        for source in range(4):
            tail_value = None
            for p in range(3):
                value = None
                for s, tail, first, slab, y, _ in cuts:
                    if s != source:
                        continue
                    if tail:
                        place = first + TAIL * p
                        part = turn(fields[p][slab], place - y)
                        tail_value = part if tail_value is None else jnp.where(lane >= place, part, tail_value)
                    else:
                        part = turn(fields[p][slab], first - y)
                        value = part if value is None else jnp.where(lane >= first, part, value)
                send_ref[chunk, 4 * chip + source, p] = value
            send_ref[chunk, 4 * chip + source, 3] = tail_value
        return carry

    lax.fori_loop(0, 8, one, 0)


def screen_planes(owner, chunk, x_ref, y_ref, box, work, gain):
    flags = [jnp.where(tile_of(owner, chunk, p) == 0, 1.0, 0.0).astype(F32) for p in range(3)]

    def along_x(real, imag):
        wide = jnp.concatenate([real, imag], axis=1)
        wide = jnp.concatenate([wide, jnp.zeros((8, 256), F32)], axis=0)
        high, low = split(wide)
        both = mm(x_ref[...], jnp.concatenate([high, high, low], axis=0))
        return both[:NX, :128], both[:NX, 128:], both[NX:, :128], both[NX:, 128:]

    def along_y(value, k):
        high, low = split(value)
        return mm(high, y_ref[k]) + mm(low, y_ref[k]) + mm(high, y_ref[k + 1])

    for plane in range(PLANES):
        if plane == 12:
            real = sum(flags[p] * box[pl.ds((8 * p + 4) * NX, NX), :] for p in range(3))
            imag = jnp.zeros_like(real)
        else:
            p, i = divmod(plane, 4)
            real = box[pl.ds((8 * p + i) * NX, NX), :]
            imag = box[pl.ds((8 * p + 4 + i) * NX, NX), :]
            if i == 0:
                imag = imag * (1.0 - flags[p])
        cr, ci, sr, si = along_x(real, imag)
        work[pl.ds(plane * NX, NX), :] = jnp.concatenate([cr + si, ci - sr], axis=1)
    weight = gain[pl.ds(chunk * PLANES * NX, PLANES * NX), :]
    value = along_y(work[...], 0) * jnp.concatenate([weight, weight], axis=1)
    work[...] = along_y(value, 2)
    extra = None
    for plane in reversed(range(PLANES)):
        rows = work[pl.ds(plane * NX, NX), :]
        cr, ci, sr, si = along_x(rows[:, :128], rows[:, 128:])
        real, imag = cr - si, ci + sr
        if plane == 12:
            extra = real
        else:
            p, i = divmod(plane, 4)
            if i == 0:
                imag = imag * (1.0 - flags[p]) + extra * flags[p]
            box[pl.ds((8 * p + i) * NX, NX), :] = real
            box[pl.ds((8 * p + 4 + i) * NX, NX), :] = imag


def intersect(total, bands_ref, partial_ref):
    lines = []
    for b in range(BLK):
        product = (bands_ref[b] * total).reshape(36, 8, 128)
        line = jnp.sum(jnp.sum(product, axis=0), axis=0, keepdims=True)
        line = line + turn(line, 64)
        lines.append(line + turn(line, 32))
    quarter = lanes((1, 128)) // 32
    row = lines[0]
    for b in range(1, BLK):
        row = jnp.where(quarter == b, lines[b], row)
    partial_ref[...] = row * SPACING**3


AROUND = [((1, -2, 3, -1, 2, -3, 4)[k % 7], (0, 2, 1, 3)[k % 4]) for k in range(28)] + [(0, turned) for turned in (2, 1, 3)]
STEPS = (AROUND, AROUND + [(0, 0)])


class Ring:
    def __init__(self, me, group, source, target, send_sem, recv_sem):
        self.source, self.target = source, target
        self.send_sem, self.recv_sem = send_sem, recv_sem
        self.me = me
        self.groups = [group, group + 1 - 2 * lax.rem(group, 2)]
        self.places = [lax.rem(me // 4 + k, 8) for k in range(8)]
        self.parts = [lax.rem(lax.rem(me, 4) + k, 4) for k in range(4)]

    def device(self, chunk, far, turned):
        return {"band": self.groups[chunk], "fft": 4 * self.places[far % 8] + self.parts[turned % 4]}

    def copy(self, source, target, peer, k):
        return pltpu.make_async_remote_copy(
            src_ref=source, dst_ref=target, send_sem=self.send_sem.at[k], recv_sem=self.recv_sem.at[k],
            device_id=peer, device_id_type=MESH,
        )

    def start(self, chunk, first, count, k, low=0, high=FFT):
        rows = pl.ds(first, count)
        for far, turned in STEPS[chunk][low:high]:
            peer = self.device(chunk, far, turned)
            self.copy(self.source.at[chunk, peer["fft"], rows], self.target.at[chunk, self.me, rows], peer, k).start()
        if chunk == 0:
            self.target[chunk, self.me, first:first + count] = self.source[chunk, self.me, first:first + count]

    def wait_recv(self, chunk, first, count, k):
        whole = self.target.at[chunk, pl.ds(0, len(STEPS[chunk])), pl.ds(first, count)]
        self.copy(whole, whole, self.device(chunk, 1, 0), k).wait_recv()

    def wait_send(self, chunk, first, count, k):
        whole = self.source.at[chunk, pl.ds(0, len(STEPS[chunk])), pl.ds(first, count)]
        self.copy(whole, whole, self.device(chunk, 1, 0), k).wait_send()


def whole_kernel(
    picked_ref, shells_ref, orbitals_far, forward_far, inverse_far, xy_far, x_far, y_far,
    result_ref,
    orbitals_ref, forward_ref, inverse_ref, xy_ref, x_ref, y_ref, fetch_sem,
    own, order, upper, lower, up, down, above, below, mine, sent, got, back, returned, tails, box, work, gain, pad,
    partial, ring_slots, near, near_slots,
    there_send, there_recv, home_send, home_recv, band_send, band_recv, ring_send, ring_recv, near_send, near_recv,
):
    me = lax.axis_index("fft")
    group = lax.axis_index("band")
    count = lax.axis_size("band")
    above_me, below_me = lax.rem(group + 1, count), lax.rem(group + count - 1, count)

    barrier = pltpu.get_barrier_semaphore()
    for peer in (above_me, below_me):
        pl.semaphore_signal(barrier, inc=1, device_id={"band": peer}, device_id_type=MESH)
    there = Ring(me, group, sent, got, there_send, there_recv)
    home = Ring(me, group, back, returned, home_send, home_recv)
    for chunk in range(2):
        for far, turned in AROUND:
            pl.semaphore_signal(barrier, inc=1, device_id=there.device(chunk, far, turned), device_id_type=MESH)

    def to_band(source, target, peer, k):
        return pltpu.make_async_remote_copy(
            src_ref=source, dst_ref=target, send_sem=band_send.at[k], recv_sem=band_recv.at[k],
            device_id={"band": peer}, device_id_type=MESH,
        )

    chosen_up = to_band(order.at[0], lower, above_me, 0)
    chosen_down = to_band(order.at[0], upper, below_me, 1)
    sum_down = to_band(down, above, below_me, 2)
    main, tail = pl.ds(0, NZ), pl.ds(NZ, NZ // 3)
    sum_up_main = to_band(up.at[main], below.at[main], above_me, 3)
    sum_up_tail = to_band(up.at[tail], below.at[tail], above_me, 4)

    fetches = [
        pltpu.make_async_copy(far, ref, fetch_sem.at[k])
        for k, (far, ref) in enumerate(
            [
                (orbitals_far, orbitals_ref), (xy_far, xy_ref), (forward_far, forward_ref),
                (x_far, x_ref), (y_far, y_ref), (inverse_far, inverse_ref),
            ]
        )
    ]
    for one in fetches:
        one.start()
    picked = picked_ref[0]
    fetches[0].wait()
    pad[...] = jnp.zeros_like(pad)
    order[0] = turned_band(orbitals_ref[:, picked, :], pad)
    pl.semaphore_wait(barrier, 2 * FFT)
    chosen_up.start()
    order_bands(picked, orbitals_ref, own, order, pad)

    def gain_step(plane, carry):
        gain_of(me, plane, shells_ref, xy_ref, gain)
        return carry

    for one in fetches[1:]:
        one.wait()
    lax.fori_loop(0, 3, gain_step, 0)
    chosen_down.start()
    tails[pl.ds(NZ * FIELDS, 24), :] = jnp.zeros((24, 128), F32)
    put_rows(sent, NZ * FIELDS + 256, jnp.zeros((24, 128), F32))

    chosen_up.wait_recv()
    for f in range(3):
        spectrum_of(f, order, upper, lower, forward_ref, sent, tails)
    there.start(0, 0, 2, 0)
    chosen_down.wait_recv()
    spectrum_of(3, order, upper, lower, forward_ref, sent, tails)
    close_tails(0, sent, tails)
    there.start(0, 2, 2, 0)
    for f in range(4, FIELDS):
        spectrum_of(f, order, upper, lower, forward_ref, sent, tails)
    close_tails(1, sent, tails)
    there.start(1, 0, 4, 1)
    lax.fori_loop(3, 2 * PLANES, gain_step, 0)

    for chunk in range(2):
        there.wait_recv(chunk, 0, 4, chunk)
        open_rows(got, chunk, box)
        screen_planes(me, chunk, x_ref, y_ref, box, work, gain)
        close_rows(box, chunk, back)
        if chunk == 0:
            home.start(0, 0, 4, 0)
        else:
            home.start(1, 0, 4, 1, 0, 20)

    home.wait_recv(0, 0, 4, 0)
    open_tails(0, returned, tails)
    total = None
    for f in range(3):
        field = pack_field(z_transform(inverse_ref, jnp.concatenate([main_of(f, returned), tail_of(f, tails)], axis=1)))
        term = field * order[visitor_of(f)[1]]
        total = term if total is None else total + term
    down[...] = total
    sum_down.start()
    home.start(1, 0, 4, 1, 20)

    def up_part(rows, fields):
        total = None
        for f, field in fields:
            if f == 3:
                mine[rows, :] = field * upper[rows, :]
            term = field * order[visitor_of(f)[1], rows, :]
            total = term if total is None else total + term
        up[rows, :] = total

    home.wait_recv(1, 0, 4, 1)
    up_part(main, [(f, z_transform(inverse_ref, main_of(f, returned))) for f in range(3, FIELDS)])
    sum_up_main.start()
    open_tails(1, returned, tails)
    up_part(tail, [(f, pack_thirds(z_transform(inverse_ref, tail_of(f, tails)))) for f in range(3, FIELDS)])
    sum_up_tail.start()
    sum_down.wait_recv()
    mine[...] += above[...]
    sum_up_main.wait_recv()
    sum_up_tail.wait_recv()
    total = mine[...] + below[...]
    result_ref[:288, :] = total
    intersect(total, own, partial)

    place, part = me // 4, lax.rem(me, 4)

    def row_to(source, target, peer, send_sem, recv_sem):
        return pltpu.make_async_remote_copy(
            src_ref=source, dst_ref=target, send_sem=send_sem, recv_sem=recv_sem,
            device_id={"fft": peer}, device_id_type=MESH,
        )

    ring = [
        row_to(partial, ring_slots.at[k], 4 * lax.rem(place + k, 8) + part, ring_send.at[k], ring_recv.at[k])
        for k in range(1, 8)
    ]
    for one in ring:
        one.start()
    row = partial[...]
    for k, one in enumerate(ring):
        one.wait()
        row = row + ring_slots[k + 1]
    near[...] = row
    beside = [
        row_to(near, near_slots.at[k], 4 * place + lax.rem(part + k, 4), near_send.at[k], near_recv.at[k])
        for k in range(1, 4)
    ]
    for one in beside:
        one.start()
    for k, one in enumerate(beside):
        one.wait()
        row = row + near_slots[k + 1]
    result_ref[288:, :] = jnp.broadcast_to(row, (8, 128))

    there.wait_send(0, 0, 4, 0)
    there.wait_send(1, 0, 4, 1)
    home.wait_send(0, 0, 4, 0)
    home.wait_send(1, 0, 4, 1)
    for one in (chosen_up, chosen_down, sum_down, sum_up_main, sum_up_tail):
        one.wait_send()


def last_kernel(given_ref, potential_ref, result_ref, pad_ref):
    pad_ref[...] = jnp.zeros_like(pad_ref)
    pad_ref[:NZ, :] = unpack_field(given_ref[:288, :])
    potential_ref[:, 0, :] = jnp.transpose(pad_ref[...])[:ROWS, :NZ]
    row = given_ref[288:289, :]
    lane = lanes((1, BLK))
    result = jnp.zeros((1, BLK), F32)
    for b in range(BLK):
        mine = lanes((1, 128)) // 32 == b
        result = jnp.where(lane == b, jnp.sum(jnp.where(mine, row, 0.0), axis=1, keepdims=True), result)
    result_ref[...] = result


def vm():
    return pl.BlockSpec(memory_space=pltpu.VMEM)


def sm():
    return pl.BlockSpec(memory_space=pltpu.SMEM)


def params(**extra):
    return pltpu.CompilerParams(vmem_limit_bytes=VMEM_LIMIT, **extra)


def shape(*dims):
    return jax.ShapeDtypeStruct(dims, F32)


def body(orbitals, picked, shells):
    forward, inverse = z_stacks()
    along_x, along_y = x_table(), y_tables()
    exchange = pltpu.VMEM((2, FFT, 4, 8, 128), F32)
    field = pltpu.VMEM((288, 128), F32)
    bands = pltpu.VMEM((BLK, 288, 128), F32)
    line = pltpu.VMEM((1, 128), F32)
    dma = pltpu.SemaphoreType.DMA
    given = pl.pallas_call(
        whole_kernel,
        out_shape=shape(296, 128),
        in_specs=[sm(), sm()] + [pl.BlockSpec(memory_space=pltpu.HBM)] * 6,
        out_specs=vm(),
        scratch_shapes=[
            pltpu.VMEM((ROWS, BLK, NZ), F32),
            pltpu.VMEM(forward.shape, BF16),
            pltpu.VMEM(inverse.shape, BF16),
            pltpu.VMEM((NX, 128), F32),
            pltpu.VMEM(along_x.shape, BF16),
            pltpu.VMEM(along_y.shape, BF16),
            dma((6,)),
            bands,
            bands,
        ]
        + [field] * 7
        + [exchange] * 4
        + [
            pltpu.VMEM((1536, 128), F32),
            pltpu.VMEM((24 * NX, 128), F32),
            pltpu.VMEM((PLANES * NX, 256), F32),
            pltpu.VMEM((2 * PLANES * NX, 128), F32),
            pltpu.VMEM((256, 256), F32),
            line,
            pltpu.VMEM((8, 1, 128), F32),
            line,
            pltpu.VMEM((4, 1, 128), F32),
        ]
        + [dma((2,))] * 2
        + [dma((2,))] * 2
        + [dma((5,))] * 2
        + [dma((8,))] * 2
        + [dma((4,))] * 2,
        compiler_params=params(collective_id=0, has_side_effects=True),
    )(
        picked, shells, jnp.transpose(orbitals, (1, 0, 2)), jnp.asarray(forward), jnp.asarray(inverse),
        jnp.asarray(xy_square()), jnp.asarray(along_x), jnp.asarray(along_y),
    )
    potentials, result = pl.pallas_call(
        last_kernel,
        out_shape=(shape(ROWS, 1, NZ), shape(1, BLK)),
        in_specs=[vm()],
        out_specs=(vm(), vm()),
        scratch_shapes=[pltpu.VMEM((256, 256), F32)],
        compiler_params=params(),
    )(given)
    return jnp.transpose(potentials, (1, 0, 2)), jnp.transpose(result)


def solution(mesh):
    return jax.shard_map(
        body,
        mesh=mesh,
        in_specs=(P("band", "fft", None), P("band"), P()),
        out_specs=(P("band", "fft", None), P("band", None)),
        check_vma=False,
    )
```
